256 devices in a mesh: dp: 256 (over z, x, y, core).
Axes of the slice: x: 4, y: 4, z: 8, core: 2. Of those that a mesh axis runs over, the one named last changes fastest.
Arguments:
- img_feats: bfloat16 [131072, 1152], P('dp'), may hold values from -6 to 6
- txt_feats: bfloat16 [131072, 1152], P('dp'), may hold values from -6 to 6
- img_head: bfloat16 [1152, 1152], replicated, may hold values from -0.1875 to 0.1875
- txt_head: bfloat16 [1152, 1152], replicated, may hold values from -0.1875 to 0.1875
- log_temp: float32 [], replicated, may hold values from 1.5 to 2.5
- logit_bias: float32 [], replicated, may hold values from -6 to -2
- caption_row: int32 [131072], P('dp'), may hold values from 0 to 511, as said below
Outputs:
- head_grads: float32 [2304, 1152], P('dp')
The draws below stay inside these ranges and needn't reach their ends.
Inputs may be any that keep to these rules, and one draw needn't show every extreme that they name: `caption_row`: each device's block of 512 entries is a permutation of 0 .. 511.
All inputs are finite; a program needn't handle non-finite values.
Results may differ from the reference program's by a relative error of at most 0.0023.
Values may be sent and summed in bfloat16 or wider, within the bound.
No kernel may reach another device: no remote copies, remote signals or barrier semaphores. Data moves between devices by JAX's collectives and lax.ppermute only.
A program may use at most 128 MiB of HBM per device.

```python
import jax
import jax.numpy as jnp
from jax import lax

D = 1152
ROWS_DEV = 512
ROUNDS = 2
TOTAL_ROWS = 131072


def draw_caption_row(key, part):
    key = jax.random.fold_in(key, 11)
    blocks = TOTAL_ROWS // ROWS_DEV
    block_keys = jax.random.split(key, blocks)

    def one_block(block_key):
        return jax.random.permutation(block_key, ROWS_DEV)
    orders = jax.vmap(one_block)(block_keys)
    return orders.reshape(-1).astype(jnp.int32)


def block_scale(rng, dims, pieces, low, top_value):
    gain = 1.0
    for axis_at, parts in pieces:
        heights = jax.random.uniform(jax.random.fold_in(jax.random.fold_in(rng, 6), axis_at), (parts,), jnp.float32, low / len(pieces), top_value / len(pieces))
        gain = gain * jnp.repeat(jnp.exp(heights), dims[axis_at] // parts).reshape((-1,) + (1,) * (len(dims) - 1 - axis_at))
    return gain


def scatter_about(own_key, extent, scale, bound, cuts=(), kind=jnp.bfloat16):
    level = block_scale(own_key, extent, cuts, -0.22, 0.18) if cuts else 1.0
    array = jax.random.normal(own_key, extent, jnp.float32) * scale * level
    return jnp.minimum(jnp.maximum(array, -bound), bound).astype(kind)


def setup_inputs(seed: int = 0) -> dict:
    streams_of = jax.random.split(jax.random.key(seed), 8)
    return {
        "img_feats": scatter_about(streams_of[0], (TOTAL_ROWS, D), 1.0, 6.0, ((0, 256),)),
        "txt_feats": scatter_about(streams_of[1], (TOTAL_ROWS, D), 1.0, 6.0, ((0, 256),)),
        "img_head": scatter_about(streams_of[2], (D, D), D ** -0.5, 0.1875),
        "txt_head": scatter_about(streams_of[3], (D, D), D ** -0.5, 0.1875),
        "log_temp": jnp.clip(jax.random.uniform(streams_of[4], (), jnp.float32, 1.5, 2.5), 1.5, 2.5),
        "logit_bias": jnp.clip(jax.random.uniform(streams_of[5], (), jnp.float32, -6.0, -2.0), -6.0, -2.0),
        "caption_row": draw_caption_row(jax.random.fold_in(streams_of[7], 71), 0),
    }


def embed(features, head):
    projected = jnp.dot(features, head, preferred_element_type=jnp.float32)
    scale = jnp.sqrt(lax.optimization_barrier(jnp.sum(projected * projected, axis=-1, keepdims=True)) + 1e-06)
    return (projected / scale, scale)

def tile_slope(left, right, label_sign, temper, offset):
    scores = temper * jnp.dot(left, right.T, preferred_element_type=jnp.float32) + offset
    margin = label_sign * scores
    return (-label_sign * jax.nn.sigmoid(-margin) * temper).astype(jnp.bfloat16)

def reference(img_feats, txt_feats, img_head, txt_head, log_temp, logit_bias, caption_row):
    img_unit, img_scale = embed(img_feats, img_head)
    txt_unit, txt_scale = embed(txt_feats, txt_head)
    blocks = TOTAL_ROWS // ROWS_DEV
    img_low = img_unit.astype(jnp.bfloat16).reshape(blocks, ROWS_DEV, D)
    txt_low = txt_unit.astype(jnp.bfloat16).reshape(blocks, ROWS_DEV, D)
    caption_blocks = caption_row.reshape(blocks, ROWS_DEV)
    temper = jnp.exp(log_temp)
    columns = jnp.arange(ROWS_DEV, dtype=jnp.int32)

    def per_block(index):
        own_img = img_low[index]
        own_txt = txt_low[index]
        label_sign = jnp.where(columns[None, :] == caption_blocks[index][:, None], 1.0, -1.0).astype(jnp.float32)
        slope = tile_slope(own_img, own_txt, label_sign, temper, logit_bias)
        img_grad = jnp.dot(slope, own_txt, preferred_element_type=jnp.float32)
        txt_grad = jnp.dot(slope.T, own_img, preferred_element_type=jnp.float32)
        for turn_index in range(ROUNDS):
            partner = jnp.bitwise_xor(index, jnp.int32(blocks // 2 >> turn_index))
            far_img = img_low[partner]
            far_txt = txt_low[partner]
            slope = tile_slope(own_img, far_txt, jnp.float32(-1.0), temper, logit_bias)
            img_grad = img_grad + jnp.dot(slope, far_txt, preferred_element_type=jnp.float32)
            back_slope = tile_slope(far_img, own_txt, jnp.float32(-1.0), temper, logit_bias)
            txt_grad = txt_grad + jnp.dot(back_slope.T, far_img, preferred_element_type=jnp.float32)
        return (img_grad, txt_grad)
    img_grad, txt_grad = lax.map(per_block, jnp.arange(blocks, dtype=jnp.int32))
    img_grad = img_grad.reshape(TOTAL_ROWS, D)
    txt_grad = txt_grad.reshape(TOTAL_ROWS, D)
    img_dz = ((img_grad - img_unit * lax.optimization_barrier(jnp.sum(img_unit * img_grad, axis=-1, keepdims=True))) / img_scale).astype(jnp.bfloat16)
    txt_dz = ((txt_grad - txt_unit * lax.optimization_barrier(jnp.sum(txt_unit * txt_grad, axis=-1, keepdims=True))) / txt_scale).astype(jnp.bfloat16)
    stacked = jnp.concatenate([jnp.dot(img_feats.T, img_dz, preferred_element_type=jnp.float32), jnp.dot(txt_feats.T, txt_dz, preferred_element_type=jnp.float32)], axis=0)
    spread = jnp.sqrt(jnp.mean(stacked * stacked) + 1e-06)
    return stacked / spread
```

```python
import jax
import jax.numpy as jnp
from jax import lax
from jax.sharding import PartitionSpec as P

SPLIT = 640


def permute(value, target):
    pairs = [(source, target(source)) for source in range(lax.axis_size("dp"))]
    return lax.ppermute(value, "dp", pairs)


def sibling(value):
    return permute(value, lambda d: d ^ 1)


def groups(bit, count):
    mask = (2**count - 1) << bit
    bases = [d for d in range(lax.axis_size("dp")) if not d & mask]
    return [[base + (k << bit) for k in range(2**count)] for base in bases]


def embed(features, head):
    projected = jnp.dot(features, head, preferred_element_type=jnp.float32)
    scale = jnp.sqrt(jnp.sum(projected * projected, axis=-1, keepdims=True) + 1e-06)
    return (projected / scale, scale)


def tile_slope(left, right, label_sign, temper, offset):
    scores = temper * jnp.dot(left, right.T, preferred_element_type=jnp.float32) + offset
    margin = label_sign * scores
    return (-label_sign * jax.nn.sigmoid(-margin) * temper).astype(jnp.bfloat16)


def to_dz(grad, unit, scale):
    inner = jnp.sum(unit * grad, axis=-1, keepdims=True)
    norm = jnp.sqrt(jnp.sum(grad * grad, axis=-1, keepdims=True))
    dz = ((grad - unit * inner) / scale).astype(jnp.bfloat16)
    return dz, jnp.sum(norm / scale)


def dot(a, b):
    return jnp.dot(a, b, preferred_element_type=jnp.float32)


def exchange_sum(block, bit, power):
    rows = block.shape[1]
    if power is not None:
        mark = jnp.full((4, 16, block.shape[2]), power, jnp.float16)
        block = jnp.concatenate([(block * jnp.exp2(14.0 - power)).astype(jnp.float16), mark], axis=1)
    got = lax.all_to_all(block, "dp", 0, 0, axis_index_groups=groups(bit, 2), tiled=True)
    if power is not None:
        back = jnp.exp2(got[:, rows, 0].astype(jnp.float32) - 14.0)
        got = got[:, :rows].astype(jnp.float32) * back[:, None, None]
    return jnp.sum(got, axis=0)


def per_device(img_feats, txt_feats, img_head, txt_head, log_temp, logit_bias, caption_row):
    core = lax.axis_index("dp") & 1
    first = core == 0
    width = img_feats.shape[1]
    block_rows = caption_row.shape[0]

    far_img = permute(img_feats, lambda d: d ^ (192 if d & 1 else 64))
    far_txt = permute(txt_feats, lambda d: d ^ (64 if d & 1 else 192))
    p = jnp.where(first, img_feats, txt_feats)
    q = jnp.where(first, txt_feats, img_feats)
    p_head = jnp.where(first, img_head, txt_head)
    q_head = jnp.where(first, txt_head, img_head)
    sib_q = sibling(q)

    temper = jnp.exp(log_temp)
    index = jnp.arange(block_rows, dtype=jnp.int32)
    match = jnp.where(first, caption_row, index)[:, None] == jnp.where(first, index, caption_row)[None, :]
    label_sign = jnp.where(match, 1.0, -1.0).astype(jnp.float32)
    negative = jnp.float32(-1.0)

    p_unit, p_scale = embed(p, p_head)
    q_unit, q_scale = embed(q, q_head)
    p_low = p_unit.astype(jnp.bfloat16)
    q_low = q_unit.astype(jnp.bfloat16)
    slope = tile_slope(p_low, q_low, label_sign, temper, logit_bias)
    p_dz, p_bound = to_dz(dot(slope, q_low), p_unit, p_scale)
    q_grad = dot(slope.T, p_low)

    pf = jnp.where(first, far_img, far_txt)
    qf = jnp.where(first, far_txt, far_img)
    sib_qf = sibling(qf)
    pf_unit, pf_scale = embed(pf, p_head)
    qf_unit, qf_scale = embed(qf, q_head)
    pf_low = pf_unit.astype(jnp.bfloat16)
    qf_low = qf_unit.astype(jnp.bfloat16)
    slope_a = tile_slope(pf_low, q_low, negative, temper, logit_bias)
    slope_b = tile_slope(pf_low, qf_low, negative, temper, logit_bias)
    q_dz, q_bound = to_dz(q_grad + dot(slope_a.T, pf_low), q_unit, q_scale)
    qf_dz, qf_bound = to_dz(dot(slope_b.T, pf_low), qf_unit, qf_scale)
    sib_q_dz = sibling(q_dz)
    sib_qf_dz = sibling(qf_dz)
    sib_bound = sibling(jnp.full((8, 128), q_bound + qf_bound, jnp.float32))
    pf_dz, pf_bound = to_dz(dot(slope_a, q_low) + dot(slope_b, qf_low), pf_unit, pf_scale)

    bound = 6.1 * (p_bound + pf_bound + sib_bound[0, 0])
    power = jnp.ceil(jnp.log2(jnp.maximum(bound, 1e-18)))
    feats = jnp.concatenate([p, sib_q, pf, sib_qf], axis=0)
    dz = jnp.concatenate([p_dz, sib_q_dz, pf_dz, sib_qf_dz], axis=0)

    left = dot(feats.T, dz[:, :SPLIT])
    right = dot(feats.T, dz[:, SPLIT:])
    left = exchange_sum(left.reshape(4, 288, SPLIT), 3, power)
    right = right.reshape(4, 4, 72, width - SPLIT).transpose(1, 0, 2, 3).reshape(4, 288, width - SPLIT)
    right = exchange_sum(right, 1, power)
    left = exchange_sum(left.reshape(4, 72, SPLIT), 1, None)
    right = exchange_sum(right.reshape(4, 72, width - SPLIT), 3, None)
    part = jnp.concatenate([left, right], axis=1).reshape(8, 9, width)
    got = lax.all_to_all(part, "dp", 0, 0, axis_index_groups=groups(5, 3), tiled=True)
    total = jnp.sum(got, axis=0)

    def owner(d):
        z, x, y, s = d >> 5, d >> 3 & 3, d >> 1 & 3, d & 1
        return (4 * s + x) << 5 | y << 3 | (z >> 1) << 1 | z & 1

    rows = permute(total, owner)
    squares = lax.all_gather(jnp.full((8, 128), jnp.sum(total * total), jnp.float32), "dp", tiled=True)
    entries = 2 * width * width
    spread = jnp.sqrt(jnp.sum(squares) / (1024.0 * entries) + 1e-06)
    return rows / spread


def solution(mesh):
    return jax.shard_map(
        per_device,
        mesh=mesh,
        in_specs=(P("dp", None), P("dp", None), P(), P(), P(), P(), P("dp")),
        out_specs=P("dp", None),
        check_vma=False,
    )
```

```python
import functools

import jax
import jax.numpy as jnp
from jax import lax
from jax.experimental import pallas as pl
from jax.experimental.pallas import tpu as pltpu
from jax.sharding import PartitionSpec as P

SPLIT = 640
F32, BF16 = jnp.float32, jnp.bfloat16
VMEM = pl.BlockSpec(memory_space=pltpu.VMEM)
SMEM = pl.BlockSpec(memory_space=pltpu.SMEM)


def permute(value, target):
    pairs = [(source, target(source)) for source in range(lax.axis_size("dp"))]
    return lax.ppermute(value, "dp", pairs)


def sibling(value):
    return permute(value, lambda d: d ^ 1)


def dot(a, b):
    return jnp.dot(a, b, preferred_element_type=F32)


def call(kernel, ins, outs, flops, scratch=(), aliases=None, limit=48):
    moved = sum(v.size * v.dtype.itemsize for v in [*ins, *outs])
    return pl.pallas_call(
        kernel,
        out_shape=outs,
        in_specs=[SMEM if v.size <= 8 else VMEM for v in ins],
        out_specs=[VMEM] * len(outs),
        scratch_shapes=scratch,
        input_output_aliases=aliases or {},
        cost_estimate=pl.CostEstimate(flops=flops, bytes_accessed=moved, transcendentals=0),
        compiler_params=pltpu.CompilerParams(vmem_limit_bytes=limit * 2**20),
    )(*ins)


def shape(rows, columns, kind):
    return jax.ShapeDtypeStruct((rows, columns), kind)


def embed(features, head):
    projected = dot(features, head)
    scale = jnp.sqrt(jnp.sum(projected * projected, axis=-1, keepdims=True) + 1e-06)
    return (projected / scale, scale)


def tile_slope(left, right, label_sign, temper, offset):
    scores = temper * dot(left, right.T) + offset
    margin = label_sign * scores
    return (-label_sign * jax.nn.sigmoid(-margin) * temper).astype(BF16)


def project(grad, unit, scale):
    inner = jnp.sum(unit * grad, axis=-1, keepdims=True)
    return (grad - unit * inner) * (1.0 / scale)


def pair(value):
    high = value.astype(BF16)
    return high, (value - high.astype(F32)).astype(BF16)


def early_kernel(p, sib_q, p_grad, p_unit, p_scale, left, right, sib_q_t, p_t, high, low):
    rows, width = p.shape
    for at in range(0, rows, 256):
        part = pl.ds(at, 256)
        high[part, :], low[part, :] = pair(project(p_grad[part, :], p_unit[part, :], p_scale[part, :]))
    p_t[...] = p[...].T
    sib_q_t[...] = sib_q[...].T
    for at in range(0, width, 384):
        part = pl.ds(at, 384)
        left[part, :] = dot(p_t[part, :], high[:, :SPLIT]) + dot(p_t[part, :], low[:, :SPLIT])
        right[part, :] = dot(p_t[part, :], high[:, SPLIT:]) + dot(p_t[part, :], low[:, SPLIT:])


def far_kernel(
    scalars, pf, qf, p_head, q_head, q_low, q_unit, q_scale, q_grad,
    send, pf_low, qf_low, pf_unit, pf_scale, slope_a, slope_b, pf_t,
    qf_unit, qf_scale,
):
    rows = pf.shape[0]
    step = 256
    temper, offset = scalars[0], scalars[1]
    for at in range(0, rows, step):
        part = pl.ds(at, step)
        for feats, head, unit, scale, low in (
            (pf, p_head, pf_unit, pf_scale, pf_low),
            (qf, q_head, qf_unit, qf_scale, qf_low),
        ):
            projected = dot(feats[part, :], head[...])
            length = jnp.sqrt(jnp.sum(projected * projected, axis=-1, keepdims=True) + 1e-06)
            there = projected / length
            unit[part, :] = there
            scale[part, :] = length
            low[part, :] = there.astype(BF16)
    pf_t[...] = pf[...].T
    for at in range(0, rows, step):
        part = pl.ds(at, step)
        for low, slope in ((q_low, slope_a), (qf_low, slope_b)):
            raw = lax.dot_general(
                pf_low[part, :], low[...], (((1,), (1,)), ((), ())), preferred_element_type=F32
            )
            slope[part, :] = (jax.nn.sigmoid(temper * raw + offset) * temper).astype(BF16)
    for at in range(0, rows, step):
        part = pl.ds(at, step)
        grad = q_grad[part, :] + dot(slope_a[:, part].T, pf_low[...])
        high, low = pair(project(grad, q_unit[part, :], q_scale[part, :]))
        send[part, :] = high
        send[pl.ds(rows + at, step), :] = low
        grad = dot(slope_b[:, part].T, pf_low[...])
        send[pl.ds(2 * rows + at, step), :] = project(grad, qf_unit[part, :], qf_scale[part, :]).astype(BF16)


def near_kernel(
    slope_a, slope_b, q_low, qf_low, pf_unit, pf_scale, pf_t, sib_qf, left, right,
    left_out, right_out, sib_qf_t, dz,
):
    rows, width = pf_unit.shape
    for at in range(0, rows, 256):
        part = pl.ds(at, 256)
        grad = dot(slope_a[part, :], q_low[...]) + dot(slope_b[part, :], qf_low[...])
        dz[part, :] = project(grad, pf_unit[part, :], pf_scale[part, :]).astype(BF16)
    sib_qf_t[...] = sib_qf[...].T
    for at in range(0, width, 384):
        part = pl.ds(at, 384)
        left_out[part, :] = left[part, :] + dot(pf_t[part, :], dz[:, :SPLIT])
        right_out[part, :] = right[part, :] + dot(pf_t[part, :], dz[:, SPLIT:])


def pieces_kernel(first, along_x, place, near, got, sib_q_t, sib_qf_t, keep_1, send_1, keep_3, send_3, total):
    width, count = near.shape
    rows = sib_q_t.shape[1]
    columns = pl.ds(first, count)
    for at in range(0, width, 384):
        part = pl.ds(at, 384)
        total[part, :] = (
            near[part, :]
            + dot(sib_q_t[part, :], got[pl.ds(0, rows), columns])
            + dot(sib_q_t[part, :], got[pl.ds(rows, rows), columns])
            + dot(sib_qf_t[part, :], got[pl.ds(2 * rows, rows), columns])
        )

    def half(target, which):
        if along_x:
            return total[pl.ds(pl.multiple_of(288 * target + 144 * which, 8), 144), :]
        starts = [288 * (2 * which + block) + 72 * target for block in (0, 1)]
        return jnp.concatenate([total[pl.ds(pl.multiple_of(at, 8), 72), :] for at in starts], axis=0)

    me = place[0]
    keep_1[pl.ds(0, 144), :] = half(me, 0)
    keep_1[pl.ds(144, 144), :] = half(me ^ 3, 0)
    send_1[pl.ds(0, 144), :] = half(me ^ 1, 0).astype(BF16)
    send_1[pl.ds(144, 144), :] = half(me ^ 2, 0).astype(BF16)
    keep_3[pl.ds(0, 144), :] = half(me, 1)
    keep_3[pl.ds(144, 144), :] = half(me ^ 1, 1)
    send_3[pl.ds(0, 144), :] = half(me ^ 3, 1).astype(BF16)
    send_3[pl.ds(144, 144), :] = half(me ^ 2, 1).astype(BF16)


def second_kernel(keep_1, got_1, keep_3, got_3, own, send_3, send_1):
    top, low = pl.ds(0, 144), pl.ds(144, 144)
    first = keep_1[...] + got_1[...].astype(F32)
    own[top, :] = first[:144]
    send_3[...] = first[144:]
    other = keep_3[...] + got_3[...].astype(F32)
    own[low, :] = other[:144]
    send_1[...] = other[144:]


def third_kernel(place, own, got_3, got_1, *rest):
    outs, total = rest[:4], rest[4]
    total[pl.ds(0, 144), :] = own[pl.ds(0, 144), :] + got_3[...]
    total[pl.ds(144, 144), :] = own[pl.ds(144, 144), :] + got_1[...]
    for j in range(4):
        outs[j][...] = total[pl.ds(pl.multiple_of(72 * (place[0] ^ j), 8), 72), :]


def z_pieces_kernel(place, *rest):
    left, right, outs, total, padded = rest[:4], rest[4:8], rest[8:16], rest[16], rest[17]
    total[:, :SPLIT] = left[0][...] + left[1][...] + left[2][...] + left[3][...]
    total[:, SPLIT:] = right[0][...] + right[1][...] + right[2][...] + right[3][...]
    for at in range(8):
        padded[at, 0:9, :] = total[9 * at : 9 * at + 9, :]
    for j in range(8):
        outs[j][...] = padded[place[0] ^ j, 0:9, :]


def sum_kernel(*rest):
    ins, total, squares = rest[:8], rest[8], rest[9]
    value = ins[0][...]
    for j in range(1, 8):
        value = value + ins[j][...]
    total[...] = value
    line = jnp.sum(value * value, axis=0, keepdims=True)
    lanes = line[:, 0:128]
    for at in range(128, line.shape[1], 128):
        lanes = lanes + line[:, at : at + 128]
    squares[...] = lanes


def per_device(img_feats, txt_feats, img_head, txt_head, log_temp, logit_bias, caption_row):
    me = lax.axis_index("dp")
    core, y, x, z = me & 1, (me >> 1) & 3, (me >> 3) & 3, me >> 5
    first = core == 0
    rows, width = img_feats.shape

    far_img = permute(img_feats, lambda d: d ^ (192 if d & 1 else 64))
    far_txt = permute(txt_feats, lambda d: d ^ (64 if d & 1 else 192))
    p = jnp.where(first, img_feats, txt_feats)
    q = jnp.where(first, txt_feats, img_feats)
    p_head = jnp.where(first, img_head, txt_head)
    q_head = jnp.where(first, txt_head, img_head)
    sib_q = sibling(q)

    temper = jnp.exp(log_temp)
    index = jnp.arange(rows, dtype=jnp.int32)
    match = jnp.where(first, caption_row, index)[:, None] == jnp.where(first, index, caption_row)[None, :]
    label_sign = jnp.where(match, 1.0, -1.0).astype(F32)

    p_unit, p_scale = embed(p, p_head)
    q_unit, q_scale = embed(q, q_head)
    p_low = p_unit.astype(BF16)
    q_low = q_unit.astype(BF16)
    slope = tile_slope(p_low, q_low, label_sign, temper, logit_bias)
    p_grad = dot(slope, q_low)
    q_grad = dot(slope.T, p_low)
    scalars = jnp.stack([temper, logit_bias])
    left, right, sib_q_t = call(
        early_kernel,
        (p, sib_q, p_grad, p_unit, p_scale),
        (shape(width, SPLIT, F32), shape(width, width - SPLIT, F32), shape(width, rows, BF16)),
        4 * rows * width * width,
        [pltpu.VMEM((width, rows), BF16)] + [pltpu.VMEM((rows, width), BF16)] * 2,
        limit=32,
    )
    far_img, far_txt, left, right, sib_q_t, q_grad = lax.optimization_barrier(
        (far_img, far_txt, left, right, sib_q_t, q_grad)
    )

    pf = jnp.where(first, far_img, far_txt)
    qf = jnp.where(first, far_txt, far_img)
    sib_qf = sibling(qf)
    big = functools.partial(shape, rows, width)
    send, pf_low, qf_low, pf_unit, pf_scale, slope_a, slope_b, pf_t = call(
        far_kernel,
        (scalars, pf, qf, p_head, q_head, q_low, q_unit, q_scale, q_grad),
        (
            shape(3 * rows, width, BF16), big(BF16), big(BF16), big(F32), shape(rows, 1, F32),
            shape(rows, rows, BF16), shape(rows, rows, BF16), shape(width, rows, BF16),
        ),
        4 * rows * width * width + 8 * rows * rows * width,
        [pltpu.VMEM((rows, width), F32), pltpu.VMEM((rows, 1), F32)],
        limit=40,
    )
    got = sibling(send)
    left, right, sib_qf_t = call(
        near_kernel,
        (slope_a, slope_b, q_low, qf_low, pf_unit, pf_scale, pf_t, sib_qf, left, right),
        (shape(width, SPLIT, F32), shape(width, width - SPLIT, F32), shape(width, rows, BF16)),
        2 * rows * width * width + 4 * rows * rows * width,
        [pltpu.VMEM((rows, width), BF16)],
        {8: 0, 9: 1},
        limit=32,
    )

    def reduce(head_grad, start, along_x):
        count = head_grad.shape[1]
        bit, other_bit = (3, 1) if along_x else (1, 3)
        place, other = (x, y) if along_x else (y, x)
        keep_1, send_1, keep_3, send_3 = call(
            functools.partial(pieces_kernel, start, along_x),
            (jnp.stack([place, 0]), head_grad, got, sib_q_t, sib_qf_t),
            (shape(288, count, F32), shape(288, count, BF16)) * 2,
            6 * rows * width * count,
            [pltpu.VMEM((width, count), F32)],
            limit=24,
        )
        got_1 = permute(send_1, lambda d: d ^ (1 << bit))
        got_3 = permute(send_3, lambda d: d ^ (3 << bit))
        own, send_3, send_1 = call(
            second_kernel,
            (keep_1, got_1, keep_3, got_3),
            (shape(288, count, F32), shape(144, count, F32), shape(144, count, F32)),
            288 * count,
            limit=16,
        )
        got_3 = permute(send_3, lambda d: d ^ (3 << bit))
        got_1 = permute(send_1, lambda d: d ^ (1 << bit))
        outs = call(
            third_kernel,
            (jnp.stack([other, 0]), own, got_3, got_1),
            [shape(72, count, F32)] * 4,
            288 * count,
            [pltpu.VMEM((288, count), F32)],
            limit=16,
        )
        return [outs[0]] + [permute(outs[j], lambda d, j=j: d ^ (j << other_bit)) for j in (1, 2, 3)]

    left = reduce(left, 0, True)
    right = reduce(right, SPLIT, False)
    parts = call(
        z_pieces_kernel,
        (jnp.stack([z, 0]), *left, *right),
        [shape(9, width, F32)] * 8,
        6 * 72 * width,
        [pltpu.VMEM((72, width), F32), pltpu.VMEM((8, 16, width), F32)],
        limit=16,
    )
    parts = [parts[0]] + [permute(parts[j], lambda d, j=j: d ^ (j << 5)) for j in range(1, 8)]
    total, squares = call(
        sum_kernel, parts, (shape(9, width, F32), shape(1, 128, F32)), 10 * 9 * width, limit=16
    )

    def owner(d):
        z, x, y, s = d >> 5, d >> 3 & 3, d >> 1 & 3, d & 1
        return (4 * s + x) << 5 | y << 3 | (z >> 1) << 1 | z & 1

    mine = permute(total, owner)
    for bit in range(8):
        squares = squares + permute(squares, lambda d: d ^ (1 << bit))
    spread = jnp.sqrt(jnp.sum(squares) / (2 * width * width) + 1e-06)
    return mine / spread


def solution(mesh):
    return jax.shard_map(
        per_device,
        mesh=mesh,
        in_specs=(P("dp", None), P("dp", None), P(), P(), P(), P(), P("dp")),
        out_specs=P("dp", None),
        check_vma=False,
    )
```

```python
import functools

import jax
import jax.numpy as jnp
from jax import lax
from jax.experimental import pallas as pl
from jax.experimental.pallas import tpu as pltpu
from jax.sharding import PartitionSpec as P

SPLIT = 640
LIMIT = 62
F32, BF16 = jnp.float32, jnp.bfloat16
VMEM = pl.BlockSpec(memory_space=pltpu.VMEM)
SMEM = pl.BlockSpec(memory_space=pltpu.SMEM)
ANY = pl.BlockSpec(memory_space=pl.ANY)


def permute(value, target):
    pairs = [(source, target(source)) for source in range(lax.axis_size("dp"))]
    return lax.ppermute(value, "dp", pairs)


def sibling(value):
    return permute(value, lambda d: d ^ 1)


def dot(a, b):
    return jnp.dot(a, b, preferred_element_type=F32)


def call(kernel, ins, outs, flops, scratch=(), aliases=None, limit=48, anywhere=(), out_anywhere=False):
    moved = sum(v.size * v.dtype.itemsize for v in [*ins, *outs])
    return pl.pallas_call(
        kernel,
        out_shape=outs,
        in_specs=[SMEM if v.size <= 8 else ANY if at in anywhere else VMEM for at, v in enumerate(ins)],
        out_specs=[ANY if out_anywhere else VMEM] * len(outs),
        scratch_shapes=scratch,
        input_output_aliases=aliases or {},
        cost_estimate=pl.CostEstimate(
            flops=flops, bytes_accessed=moved if flops > 1 else 1, transcendentals=0
        ),
        compiler_params=pltpu.CompilerParams(vmem_limit_bytes=limit * 2**20),
    )(*ins)


def shape(rows, columns, kind):
    return jax.ShapeDtypeStruct((rows, columns), kind)


def embed(features, head):
    projected = dot(features, head)
    scale = jnp.sqrt(jnp.sum(projected * projected, axis=-1, keepdims=True) + 1e-06)
    return (projected / scale, scale)


def tile_slope(left, right, label_sign, temper, offset):
    scores = temper * dot(left, right.T) + offset
    margin = label_sign * scores
    return (-label_sign * jax.nn.sigmoid(-margin) * temper).astype(BF16)


def project(grad, unit, inverse):
    inner = jnp.sum(unit * grad, axis=-1, keepdims=True)
    return (grad - unit * inner) * inverse


def pairs_kernel(p_grad, p_unit, p_scale, q_grad, q_unit, q_scale, p_pair, q_pair):
    rows = p_grad.shape[0]
    for grad, unit, scale, out in ((q_grad, q_unit, q_scale, q_pair), (p_grad, p_unit, p_scale, p_pair)):
        for at in range(0, rows, 128):
            part = pl.ds(at, 128)
            value = project(grad[part, :], unit[part, :], 1.0 / scale[part, :])
            high = value.astype(BF16)
            out[part, :] = high
            out[pl.ds(rows + at, 128), :] = (value - high.astype(F32)).astype(BF16)


def early_kernel(p, sib_q, p_pair, left, right, sib_q_t, p_twice):
    rows, width = p.shape
    turned = p[...].T
    p_twice[:, :rows] = turned
    p_twice[:, rows:] = turned
    sib_q_t[...] = sib_q[...].T
    for at in range(0, width, 576):
        part = pl.ds(at, 576)
        left[part, :] = dot(p_twice[part, :], p_pair[:, :SPLIT])
        right[part, :] = dot(p_twice[part, :], p_pair[:, SPLIT:])


def far_kernel(
    scalars, place, far_img, far_txt, p_head_in, q_head_in, q_low_in, q_unit_in, q_scale_in,
    send, qf_t, pf_dz, pf_t,
    pf, qf, p_head, q_head, q_low, q_unit, q_scale, pf_unit, qf_unit, pf_inverse, qf_inverse,
    pf_low, qf_low, slope_a, slope_b, sems,
):
    rows = pf.shape[0]
    step = 256
    first = place[0] == 0

    def copy(source, target, at):
        return pltpu.make_async_copy(source, target, sems.at[at])

    @pl.when(first)
    def _():
        copy(far_img, pf, 0).start()

    @pl.when(jnp.logical_not(first))
    def _():
        copy(far_txt, pf, 0).start()

    copies = [copy(p_head_in, p_head, 1)]
    copies[0].start()

    @pl.when(first)
    def _():
        copy(far_txt, qf, 2).start()

    @pl.when(jnp.logical_not(first))
    def _():
        copy(far_img, qf, 2).start()

    for at, (source, target) in enumerate(
        ((q_low_in, q_low), (q_head_in, q_head), (q_unit_in, q_unit), (q_scale_in, q_scale)), 3
    ):
        copies.append(copy(source, target, at))
        copies[-1].start()

    temper, offset = scalars[0], scalars[1]

    def embed_far(feats, head, unit, inverse, low):
        for at in range(0, rows, step):
            part = pl.ds(at, step)
            projected = dot(feats[part, :], head[...])
            length = jnp.sqrt(jnp.sum(projected * projected, axis=-1, keepdims=True) + 1e-06)
            inverse[part, :] = 1.0 / length
            there = projected * (1.0 / length)
            unit[part, :] = there
            low[part, :] = there.astype(BF16)

    def slopes(low, slope):
        for at in range(0, rows, step):
            part = pl.ds(at, step)
            raw = lax.dot_general(
                pf_low[part, :], low[...], (((1,), (1,)), ((), ())), preferred_element_type=F32
            )
            slope[part, :] = (jax.nn.sigmoid(temper * raw + offset) * temper).astype(BF16)

    copy(far_img, pf, 0).wait()
    copies[0].wait()
    embed_far(pf, p_head, pf_unit, pf_inverse, pf_low)
    pf_t[...] = pf[...].T
    for at in (1, 2, 3, 4):
        copies[at].wait()
    copy(far_txt, qf, 2).wait()
    qf_t[...] = qf[...].T
    slopes(q_low, slope_a)
    embed_far(qf, q_head, qf_unit, qf_inverse, qf_low)
    slopes(qf_low, slope_b)
    for at in range(0, rows, step):
        part = pl.ds(at, step)
        grad = dot(slope_a[:, part].T, pf_low[...])
        send[part, :] = project(grad, q_unit[part, :], 1.0 / q_scale[part, :]).astype(BF16)
        grad = dot(slope_b[:, part].T, pf_low[...])
        send[pl.ds(rows + at, step), :] = project(grad, qf_unit[part, :], qf_inverse[part, :]).astype(BF16)
        grad = dot(slope_a[part, :], q_low[...]) + dot(slope_b[part, :], qf_low[...])
        pf_dz[part, :] = project(grad, pf_unit[part, :], pf_inverse[part, :]).astype(BF16)


def fetch(pairs, sems):
    copies = [pltpu.make_async_copy(*pair, sems.at[at]) for at, pair in enumerate(pairs)]
    for copy in copies:
        copy.start()
    return lambda at: copies[at].wait()


def near_kernel(*refs):
    ins, (left_out, right_out), held, (in_sems, out_sems) = refs[:6], refs[6:8], refs[8:14], refs[14:]
    pf_t, pf_dz, left, sib_q_t, sib_pair, right = held
    width, rows = pf_t.shape
    wait = fetch(list(zip(ins, held)), in_sems)
    stores = []
    for total, out, columns, ready in (
        (left, left_out, pl.ds(0, SPLIT), 3),
        (right, right_out, pl.ds(SPLIT, width - SPLIT), 6),
    ):
        for at in range(ready):
            if ready == 3 or at == 5:
                wait(at)
        for at in range(0, width, 576):
            part = pl.ds(at, 576)
            value = total[part, :] + dot(pf_t[part, :], pf_dz[:, columns])
            if ready == 3 and at == 0:
                wait(3)
                wait(4)
            total[part, :] = (
                value
                + dot(sib_q_t[part, :], sib_pair[pl.ds(0, rows), columns])
                + dot(sib_q_t[part, :], sib_pair[pl.ds(rows, rows), columns])
            )
            store = pltpu.make_async_copy(total.at[part, :], out.at[part, :], out_sems.at[len(stores)])
            store.start()
            stores.append(store)
    for store in stores:
        store.wait()


def cut_kernel(first, along_x, place, near_in, got, sib_q_t, sib_qf_t, *refs):
    (keep_1, send_1, keep_3, send_3), (near, total, sems) = refs[:4], refs[4:]
    width, count = near.shape
    rows = sib_q_t.shape[1]
    columns = pl.ds(first, count)
    wait = fetch([(near_in, near)], sems)
    for at in range(0, width, 576):
        part = pl.ds(at, 576)
        value = dot(sib_q_t[part, :], got[pl.ds(0, rows), columns])
        value = value + dot(sib_qf_t[part, :], got[pl.ds(rows, rows), columns])
        if at == 0:
            wait(0)
        total[part, :] = near[part, :] + value

    def half(target, which):
        if along_x:
            return total[pl.ds(pl.multiple_of(288 * target + 144 * which, 8), 144), :]
        starts = [288 * (2 * which + block) + 72 * target for block in (0, 1)]
        return jnp.concatenate([total[pl.ds(pl.multiple_of(at, 8), 72), :] for at in starts], axis=0)

    me = place[0]
    keep_1[pl.ds(0, 144), :] = half(me, 0)
    keep_1[pl.ds(144, 144), :] = half(me ^ 3, 0)
    send_1[pl.ds(0, 144), :] = half(me ^ 1, 0).astype(BF16)
    send_1[pl.ds(144, 144), :] = half(me ^ 2, 0).astype(BF16)
    keep_3[pl.ds(0, 144), :] = half(me, 1)
    keep_3[pl.ds(144, 144), :] = half(me ^ 1, 1)
    send_3[pl.ds(0, 144), :] = half(me ^ 3, 1).astype(BF16)
    send_3[pl.ds(144, 144), :] = half(me ^ 2, 1).astype(BF16)


def second_kernel(keep_1, got_1, keep_3, got_3, own, send_3, send_1):
    top, low = pl.ds(0, 144), pl.ds(144, 144)
    first = keep_1[...] + got_1[...].astype(F32)
    own[top, :] = first[:144]
    send_3[...] = first[144:]
    other = keep_3[...] + got_3[...].astype(F32)
    own[low, :] = other[:144]
    send_1[...] = other[144:]


def third_kernel(place, own, got_3, got_1, *rest):
    outs, total = rest[:4], rest[4]
    total[pl.ds(0, 144), :] = own[pl.ds(0, 144), :] + got_3[...]
    total[pl.ds(144, 144), :] = own[pl.ds(144, 144), :] + got_1[...]
    for j in range(4):
        outs[j][...] = total[pl.ds(pl.multiple_of(72 * (place[0] ^ j), 8), 72), :]


def z_pieces_kernel(place, *rest):
    left, right, outs, total, padded = rest[:4], rest[4:8], rest[8:12], rest[12], rest[13]
    total[:, :SPLIT] = left[0][...] + left[1][...] + left[2][...] + left[3][...]
    total[:, SPLIT:] = right[0][...] + right[1][...] + right[2][...] + right[3][...]
    for at in range(4):
        padded[at, 0:18, :] = total[18 * at : 18 * at + 18, :]
    for j in range(4):
        outs[j][...] = padded[place[0] ^ j, 0:18, :]


def sum_kernel(a, b, c, d, total):
    total[...] = a[...] + b[...] + c[...] + d[...]


def last_kernel(place, a, b, mine, squares):
    total = a[...] + b[...]

    @pl.when(place[0] == 0)
    def _():
        mine[...] = total[0:9]

    @pl.when(place[0] != 0)
    def _():
        mine[...] = total[9:18]

    line = jnp.sum(total * total, axis=0, keepdims=True)
    lanes = line[:, 0:128]
    for at in range(128, line.shape[1], 128):
        lanes = lanes + line[:, at : at + 128]
    squares[...] = lanes


def per_device(img_feats, txt_feats, img_head, txt_head, log_temp, logit_bias, caption_row):
    me = lax.axis_index("dp")
    core, y, x, z = me & 1, (me >> 1) & 3, (me >> 3) & 3, me >> 5
    first = core == 0
    rows, width = img_feats.shape

    far_img = permute(img_feats, lambda d: d ^ (192 if d & 1 else 64))
    far_txt = permute(txt_feats, lambda d: d ^ (64 if d & 1 else 192))
    p = jnp.where(first, img_feats, txt_feats)
    q = jnp.where(first, txt_feats, img_feats)
    p_head = jnp.where(first, img_head, txt_head)
    q_head = jnp.where(first, txt_head, img_head)
    sib_q = sibling(q)

    temper = jnp.exp(log_temp)
    index = jnp.arange(rows, dtype=jnp.int32)
    match = jnp.where(first, caption_row, index)[:, None] == jnp.where(first, index, caption_row)[None, :]
    label_sign = jnp.where(match, 1.0, -1.0).astype(F32)

    p_unit, p_scale = embed(p, p_head)
    q_unit, q_scale = embed(q, q_head)
    p_low = p_unit.astype(BF16)
    q_low = q_unit.astype(BF16)
    slope = tile_slope(p_low, q_low, label_sign, temper, logit_bias)
    p_grad = dot(slope, q_low)
    q_grad = dot(slope.T, p_low)
    scalars = jnp.stack([temper, logit_bias])
    p_pair, q_pair = call(
        pairs_kernel,
        (p_grad, p_unit, p_scale, q_grad, q_unit, q_scale),
        (shape(2 * rows, width, BF16), shape(2 * rows, width, BF16)),
        1,
        limit=20,
    )
    sib_pair = sibling(q_pair)
    left, right, sib_q_t = call(
        early_kernel,
        (p, sib_q, p_pair),
        (shape(width, SPLIT, F32), shape(width, width - SPLIT, F32), shape(width, rows, BF16)),
        1,
        [pltpu.VMEM((width, 2 * rows), BF16)],
        limit=20,
    )
    far_img, far_txt, left, right, sib_q_t = lax.optimization_barrier(
        (far_img, far_txt, left, right, sib_q_t)
    )

    wide, low, thin = (pltpu.VMEM(dims, kind) for dims, kind in (
        ((rows, width), F32), ((rows, width), BF16), ((rows, 1), F32),
    ))
    head, tile = pltpu.VMEM((width, width), BF16), pltpu.VMEM((rows, rows), BF16)
    send, qf_t, pf_dz, pf_t = call(
        far_kernel,
        (scalars, jnp.stack([core, 0]), far_img, far_txt, p_head, q_head, q_low, q_unit, q_scale),
        (shape(2 * rows, width, BF16), shape(width, rows, BF16), shape(rows, width, BF16), shape(width, rows, BF16)),
        4 * rows * width * width + 12 * rows * rows * width,
        [
            low, low, head, head, low, wide, thin, wide, wide, thin, thin,
            low, low, tile, tile, pltpu.SemaphoreType.DMA((7,)),
        ],
        limit=LIMIT,
        anywhere=range(9),
    )
    got, sib_qf_t = sibling(send), sibling(qf_t)
    left, right = call(
        near_kernel,
        (pf_t, pf_dz, left, sib_q_t, sib_pair, right),
        (shape(width, SPLIT, F32), shape(width, width - SPLIT, F32)),
        6 * rows * width * width,
        [
            pltpu.VMEM((width, rows), BF16), low, pltpu.VMEM((width, SPLIT), F32),
            pltpu.VMEM((width, rows), BF16), pltpu.VMEM((2 * rows, width), BF16),
            pltpu.VMEM((width, width - SPLIT), F32),
            pltpu.SemaphoreType.DMA((6,)), pltpu.SemaphoreType.DMA((4,)),
        ],
        limit=LIMIT,
        anywhere=range(6),
        out_anywhere=True,
    )

    def pieces(first, along_x, place, head_grad):
        count = head_grad.shape[1]
        return call(
            functools.partial(cut_kernel, first, along_x),
            (jnp.stack([place, 0]), head_grad, got, sib_q_t, sib_qf_t),
            (shape(288, count, F32), shape(288, count, BF16)) * 2,
            4 * rows * width * count,
            [pltpu.VMEM((width, count), F32)] * 2 + [pltpu.SemaphoreType.DMA((1,))],
            limit=24,
            anywhere=(1,),
        )

    def reduce(parts, along_x):
        keep_1, send_1, keep_3, send_3 = parts
        count = keep_1.shape[1]
        bit, other_bit, other = (3, 1, y) if along_x else (1, 3, x)
        got_1 = permute(send_1, lambda d: d ^ (1 << bit))
        got_3 = permute(send_3, lambda d: d ^ (3 << bit))
        own, send_3, send_1 = call(
            second_kernel,
            (keep_1, got_1, keep_3, got_3),
            (shape(288, count, F32), shape(144, count, F32), shape(144, count, F32)),
            288 * count,
            limit=8,
        )
        got_3 = permute(send_3, lambda d: d ^ (3 << bit))
        got_1 = permute(send_1, lambda d: d ^ (1 << bit))
        outs = call(
            third_kernel,
            (jnp.stack([other, 0]), own, got_3, got_1),
            [shape(72, count, F32)] * 4,
            288 * count,
            [pltpu.VMEM((288, count), F32)],
            limit=8,
        )
        return [outs[0]] + [permute(outs[j], lambda d, j=j: d ^ (j << other_bit)) for j in (1, 2, 3)]

    left = pieces(0, True, x, left)
    right = pieces(SPLIT, False, y, right)
    left = reduce(left, True)
    right = reduce(right, False)
    parts = call(
        z_pieces_kernel,
        (jnp.stack([z >> 1, 0]), *left, *right),
        [shape(18, width, F32)] * 4,
        6 * 72 * width,
        [pltpu.VMEM((72, width), F32), pltpu.VMEM((4, 24, width), F32)],
        limit=8,
    )
    parts = [parts[0]] + [permute(parts[j], lambda d, j=j: d ^ (j << 6)) for j in (1, 2, 3)]
    [part] = call(sum_kernel, parts, [shape(18, width, F32)], 3 * 18 * width, limit=8)
    other = permute(part, lambda d: d ^ 32)
    total, squares = call(
        last_kernel,
        (jnp.stack([z & 1, 0]), part, other),
        (shape(9, width, F32), shape(1, 128, F32)),
        10 * 18 * width,
        limit=8,
    )

    def owner(d):
        z, x, y, s = d >> 5, d >> 3 & 3, d >> 1 & 3, d & 1
        return (4 * s + x) << 5 | y << 3 | (z >> 1) << 1 | z & 1

    mine = permute(total, owner)
    for bit in (0, 1, 2, 3, 4, 6, 7):
        squares = squares + permute(squares, lambda d: d ^ (1 << bit))
        if bit == 3:
            squares, mine = lax.optimization_barrier((squares, mine))
    spread = jnp.sqrt(jnp.sum(squares) / (2 * width * width) + 1e-06)
    return mine / spread


def solution(mesh):
    return jax.shard_map(
        per_device,
        mesh=mesh,
        in_specs=(P("dp", None), P("dp", None), P(), P(), P(), P(), P("dp")),
        out_specs=P("dp", None),
        check_vma=False,
    )
```

```python
import functools

import jax
import jax.numpy as jnp
from jax import lax
from jax.experimental import pallas as pl
from jax.experimental.pallas import tpu as pltpu
from jax.sharding import PartitionSpec as P

SPLIT = 640
LIMIT = 62
F32, BF16 = jnp.float32, jnp.bfloat16
VMEM = pl.BlockSpec(memory_space=pltpu.VMEM)
SMEM = pl.BlockSpec(memory_space=pltpu.SMEM)
ANY = pl.BlockSpec(memory_space=pl.ANY)


def permute(value, target):
    pairs = [(source, target(source)) for source in range(lax.axis_size("dp"))]
    return lax.ppermute(value, "dp", pairs)


def sibling(value):
    return permute(value, lambda d: d ^ 1)


def dot(a, b):
    return jnp.dot(a, b, preferred_element_type=F32)


def call(kernel, ins, outs, flops, scratch=(), aliases=None, limit=48, anywhere=(), out_anywhere=False):
    moved = sum(v.size * v.dtype.itemsize for v in [*ins, *outs])
    return pl.pallas_call(
        kernel,
        out_shape=outs,
        in_specs=[SMEM if v.size <= 8 else ANY if at in anywhere else VMEM for at, v in enumerate(ins)],
        out_specs=[ANY if out_anywhere else VMEM] * len(outs),
        scratch_shapes=scratch,
        input_output_aliases=aliases or {},
        cost_estimate=pl.CostEstimate(
            flops=flops, bytes_accessed=moved if flops > 1 else 1, transcendentals=0
        ),
        compiler_params=pltpu.CompilerParams(vmem_limit_bytes=limit * 2**20),
    )(*ins)


def shape(rows, columns, kind):
    return jax.ShapeDtypeStruct((rows, columns), kind)


def embed(features, head):
    projected = dot(features, head)
    scale = jnp.sqrt(jnp.sum(projected * projected, axis=-1, keepdims=True) + 1e-06)
    return (projected / scale, scale)


def tile_slope(left, right, label_sign, temper, offset):
    scores = temper * dot(left, right.T) + offset
    margin = label_sign * scores
    return (-label_sign * jax.nn.sigmoid(-margin) * temper).astype(BF16)


def project(grad, unit, inverse):
    inner = jnp.sum(unit * grad, axis=-1, keepdims=True)
    return (grad - unit * inner) * inverse


def pairs_kernel(p_grad, p_unit, p_scale, q_grad, q_unit, q_scale, p_pair, q_pair):
    rows = p_grad.shape[0]
    for grad, unit, scale, out in ((q_grad, q_unit, q_scale, q_pair), (p_grad, p_unit, p_scale, p_pair)):
        for at in range(0, rows, 128):
            part = pl.ds(at, 128)
            value = project(grad[part, :], unit[part, :], 1.0 / scale[part, :])
            high = value.astype(BF16)
            out[part, :] = high
            out[pl.ds(rows + at, 128), :] = (value - high.astype(F32)).astype(BF16)


def early_kernel(p, sib_q, p_pair, left, right, sib_q_t, p_twice):
    rows, width = p.shape
    turned = p[...].T
    p_twice[:, :rows] = turned
    p_twice[:, rows:] = turned
    sib_q_t[...] = sib_q[...].T
    for at in range(0, width, 576):
        part = pl.ds(at, 576)
        left[part, :] = dot(p_twice[part, :], p_pair[:, :SPLIT])
        right[part, :] = dot(p_twice[part, :], p_pair[:, SPLIT:])


def other_early_kernel(sib_q_t, sib_pair, left, right, left_out, right_out):
    width, rows = sib_q_t.shape
    for at in range(0, width, 576):
        part = pl.ds(at, 576)
        for before, out, columns in (
            (left, left_out, pl.ds(0, SPLIT)),
            (right, right_out, pl.ds(SPLIT, width - SPLIT)),
        ):
            out[part, :] = (
                before[part, :]
                + dot(sib_q_t[part, :], sib_pair[pl.ds(0, rows), columns])
                + dot(sib_q_t[part, :], sib_pair[pl.ds(rows, rows), columns])
            )


def far_kernel(
    scalars, place, far_img, far_txt, p_head_in, q_head_in, q_low_in, q_unit_in, q_scale_in,
    send, qf_t, pf_dz, pf_t,
    pf, qf, p_head, q_head, q_low, q_unit, q_scale, pf_unit, qf_unit, pf_inverse, qf_inverse,
    pf_low, qf_low, slope_a, slope_b, sems,
):
    rows = pf.shape[0]
    step = 256
    first = place[0] == 0

    def copy(source, target, at):
        return pltpu.make_async_copy(source, target, sems.at[at])

    @pl.when(first)
    def _():
        copy(far_img, pf, 0).start()

    @pl.when(jnp.logical_not(first))
    def _():
        copy(far_txt, pf, 0).start()

    copies = [copy(p_head_in, p_head, 1)]
    copies[0].start()

    @pl.when(first)
    def _():
        copy(far_txt, qf, 2).start()

    @pl.when(jnp.logical_not(first))
    def _():
        copy(far_img, qf, 2).start()

    for at, (source, target) in enumerate(
        ((q_low_in, q_low), (q_head_in, q_head), (q_unit_in, q_unit), (q_scale_in, q_scale)), 3
    ):
        copies.append(copy(source, target, at))
        copies[-1].start()

    temper, offset = scalars[0], scalars[1]

    def embed_far(feats, head, unit, inverse, low):
        for at in range(0, rows, step):
            part = pl.ds(at, step)
            projected = dot(feats[part, :], head[...])
            length = jnp.sqrt(jnp.sum(projected * projected, axis=-1, keepdims=True) + 1e-06)
            inverse[part, :] = 1.0 / length
            there = projected * (1.0 / length)
            unit[part, :] = there
            low[part, :] = there.astype(BF16)

    def slopes(low, slope):
        for at in range(0, rows, step):
            part = pl.ds(at, step)
            raw = lax.dot_general(
                pf_low[part, :], low[...], (((1,), (1,)), ((), ())), preferred_element_type=F32
            )
            slope[part, :] = (jax.nn.sigmoid(temper * raw + offset) * temper).astype(BF16)

    copy(far_img, pf, 0).wait()
    copies[0].wait()
    embed_far(pf, p_head, pf_unit, pf_inverse, pf_low)
    pf_t[...] = pf[...].T
    for at in (1, 2, 3, 4):
        copies[at].wait()
    copy(far_txt, qf, 2).wait()
    qf_t[...] = qf[...].T
    slopes(q_low, slope_a)
    embed_far(qf, q_head, qf_unit, qf_inverse, qf_low)
    slopes(qf_low, slope_b)
    for at in range(0, rows, step):
        part = pl.ds(at, step)
        grad = dot(slope_a[:, part].T, pf_low[...])
        send[part, :] = project(grad, q_unit[part, :], 1.0 / q_scale[part, :]).astype(BF16)
        grad = dot(slope_b[:, part].T, pf_low[...])
        send[pl.ds(rows + at, step), :] = project(grad, qf_unit[part, :], qf_inverse[part, :]).astype(BF16)
        grad = dot(slope_a[part, :], q_low[...]) + dot(slope_b[part, :], qf_low[...])
        pf_dz[part, :] = project(grad, pf_unit[part, :], pf_inverse[part, :]).astype(BF16)


def fetch(pairs, sems):
    copies = [pltpu.make_async_copy(*pair, sems.at[at]) for at, pair in enumerate(pairs)]
    for copy in copies:
        copy.start()
    return lambda at: copies[at].wait()


def near_kernel(*refs):
    ins, outs, held, (in_sems, out_sems) = refs[:4], refs[4:6], refs[6:10], refs[10:]
    pf_t, pf_dz, left, right = held
    width = pf_t.shape[0]
    halves = [pl.ds(0, 576), pl.ds(576, 576)]
    wait = fetch(
        [(ins[1], pf_dz), (ins[0], pf_t)]
        + [(ins[2 + which].at[part, :], held[2 + which].at[part, :]) for part in halves for which in (0, 1)],
        in_sems,
    )
    wait(0)
    wait(1)
    stores = []
    for part in halves:
        for total, out, columns in (
            (left, outs[0], pl.ds(0, SPLIT)),
            (right, outs[1], pl.ds(SPLIT, width - SPLIT)),
        ):
            value = dot(pf_t[part, :], pf_dz[:, columns])
            at = len(stores)
            wait(2 + at)
            total[part, :] = total[part, :] + value
            stores.append(pltpu.make_async_copy(total.at[part, :], out.at[part, :], out_sems.at[at]))
            stores[-1].start()
    for store in stores:
        store.wait()


def cut_kernel(place, *refs):
    ins, outs, held, sends, (in_sems, out_sems) = refs[:5], refs[5:13], refs[13:18], refs[18:22], refs[22:]
    sib_q_t, got, sib_qf_t, left, right = held
    width, rows = sib_q_t.shape
    halves = [pl.ds(0, 576), pl.ds(576, 576)]
    wait = fetch(
        [(ins[at], held[at]) for at in range(3)]
        + [(ins[at].at[part, :], held[at].at[part, :]) for at in (3, 4) for part in halves],
        in_sems,
    )
    wait(0)
    wait(1)
    stores = []

    def store(source, target):
        stores.append(pltpu.make_async_copy(source, target, out_sems.at[len(stores)]))
        stores[-1].start()

    for along_x, total, columns in ((True, left, pl.ds(0, SPLIT)), (False, right, pl.ds(SPLIT, width - SPLIT))):
        for at, part in enumerate(halves):
            value = dot(sib_q_t[part, :], got[pl.ds(0, rows), columns])
            if along_x and at == 0:
                wait(2)
            value = value + dot(sib_qf_t[part, :], got[pl.ds(rows, rows), columns])
            wait((3 if along_x else 5) + at)
            total[part, :] = total[part, :] + value

        def starts(target, which):
            if along_x:
                return 144, [pl.multiple_of(288 * target + 144 * which, 8)]
            return 72, [pl.multiple_of(288 * (2 * which + block) + 72 * target, 8) for block in (0, 1)]

        me = place[0] if along_x else place[1]
        keep_1, send_1, keep_3, send_3 = outs[:4] if along_x else outs[4:]
        low_1, low_3 = sends[:2] if along_x else sends[2:]
        for low, out, which, targets in ((low_1, send_1, 0, (me ^ 1, me ^ 2)), (low_3, send_3, 1, (me ^ 3, me ^ 2))):
            for at, target in enumerate(targets):
                count, begins = starts(target, which)
                pieces = [total[pl.ds(begin, count), :] for begin in begins]
                piece = pieces[0] if len(pieces) == 1 else jnp.concatenate(pieces, axis=0)
                low[pl.ds(144 * at, 144), :] = piece.astype(BF16)
            store(low, out)
        for out, which, targets in ((keep_1, 0, (me, me ^ 3)), (keep_3, 1, (me, me ^ 1))):
            for at, target in enumerate(targets):
                count, begins = starts(target, which)
                for block, begin in enumerate(begins):
                    store(total.at[pl.ds(begin, count), :], out.at[pl.ds(144 * at + 72 * block, count), :])
    for copy in stores:
        copy.wait()


def second_kernel(keep_1, got_1, keep_3, got_3, own, send_3, send_1):
    top, low = pl.ds(0, 144), pl.ds(144, 144)
    first = keep_1[...] + got_1[...].astype(F32)
    own[top, :] = first[:144]
    send_3[...] = first[144:]
    other = keep_3[...] + got_3[...].astype(F32)
    own[low, :] = other[:144]
    send_1[...] = other[144:]


def third_kernel(place, own, got_3, got_1, *rest):
    outs, total = rest[:4], rest[4]
    total[pl.ds(0, 144), :] = own[pl.ds(0, 144), :] + got_3[...]
    total[pl.ds(144, 144), :] = own[pl.ds(144, 144), :] + got_1[...]
    for j in range(4):
        outs[j][...] = total[pl.ds(pl.multiple_of(72 * (place[0] ^ j), 8), 72), :]


def z_pieces_kernel(place, *rest):
    left, right, outs, total, padded = rest[:4], rest[4:8], rest[8:12], rest[12], rest[13]
    total[:, :SPLIT] = left[0][...] + left[1][...] + left[2][...] + left[3][...]
    total[:, SPLIT:] = right[0][...] + right[1][...] + right[2][...] + right[3][...]
    for at in range(4):
        padded[at, 0:18, :] = total[18 * at : 18 * at + 18, :]
    for j in range(4):
        outs[j][...] = padded[place[0] ^ j, 0:18, :]


def sum_kernel(a, b, c, d, total):
    total[...] = a[...] + b[...] + c[...] + d[...]


def last_kernel(place, a, b, mine, squares):
    total = a[...] + b[...]

    @pl.when(place[0] == 0)
    def _():
        mine[...] = total[0:9, :]

    @pl.when(place[0] != 0)
    def _():
        mine[...] = total[9:18, :]

    line = jnp.sum(total * total, axis=0, keepdims=True)
    lanes = line[:, 0:128]
    for at in range(128, line.shape[1], 128):
        lanes = lanes + line[:, at : at + 128]
    squares[...] = lanes


def per_device(img_feats, txt_feats, img_head, txt_head, log_temp, logit_bias, caption_row):
    me = lax.axis_index("dp")
    core, y, x, z = me & 1, (me >> 1) & 3, (me >> 3) & 3, me >> 5
    first = core == 0
    rows, width = img_feats.shape

    far_img = permute(img_feats, lambda d: d ^ (192 if d & 1 else 64))
    far_txt = permute(txt_feats, lambda d: d ^ (64 if d & 1 else 192))
    p = jnp.where(first, img_feats, txt_feats)
    q = jnp.where(first, txt_feats, img_feats)
    p_head = jnp.where(first, img_head, txt_head)
    q_head = jnp.where(first, txt_head, img_head)
    sib_q = sibling(q)

    temper = jnp.exp(log_temp)
    index = jnp.arange(rows, dtype=jnp.int32)
    match = jnp.where(first, caption_row, index)[:, None] == jnp.where(first, index, caption_row)[None, :]
    label_sign = jnp.where(match, 1.0, -1.0).astype(F32)

    p_unit, p_scale = embed(p, p_head)
    q_unit, q_scale = embed(q, q_head)
    p_low = p_unit.astype(BF16)
    q_low = q_unit.astype(BF16)
    slope = tile_slope(p_low, q_low, label_sign, temper, logit_bias)
    p_grad = dot(slope, q_low)
    q_grad = dot(slope.T, p_low)
    scalars = jnp.stack([temper, logit_bias])
    p_pair, q_pair = call(
        pairs_kernel,
        (p_grad, p_unit, p_scale, q_grad, q_unit, q_scale),
        (shape(2 * rows, width, BF16), shape(2 * rows, width, BF16)),
        1,
        limit=20,
    )
    sib_pair = sibling(q_pair)
    left, right, sib_q_t = call(
        early_kernel,
        (p, sib_q, p_pair),
        (shape(width, SPLIT, F32), shape(width, width - SPLIT, F32), shape(width, rows, BF16)),
        200 * rows * width * width,
        [pltpu.VMEM((width, 2 * rows), BF16)],
        limit=20,
    )
    left, right = call(
        other_early_kernel,
        (sib_q_t, sib_pair, left, right),
        (shape(width, SPLIT, F32), shape(width, width - SPLIT, F32)),
        1,
        (),
        {2: 0, 3: 1},
        limit=24,
    )
    far_img, far_txt, left, right, sib_q_t = lax.optimization_barrier(
        (far_img, far_txt, left, right, sib_q_t)
    )

    wide, low, thin = (pltpu.VMEM(dims, kind) for dims, kind in (
        ((rows, width), F32), ((rows, width), BF16), ((rows, 1), F32),
    ))
    head, tile = pltpu.VMEM((width, width), BF16), pltpu.VMEM((rows, rows), BF16)
    send, qf_t, pf_dz, pf_t = call(
        far_kernel,
        (scalars, jnp.stack([core, 0]), far_img, far_txt, p_head, q_head, q_low, q_unit, q_scale),
        (shape(2 * rows, width, BF16), shape(width, rows, BF16), shape(rows, width, BF16), shape(width, rows, BF16)),
        4 * rows * width * width + 12 * rows * rows * width,
        [
            low, low, head, head, low, wide, thin, wide, wide, thin, thin,
            low, low, tile, tile, pltpu.SemaphoreType.DMA((7,)),
        ],
        limit=LIMIT,
        anywhere=range(9),
    )
    got, sib_qf_t = sibling(send), sibling(qf_t)
    accumulators = [pltpu.VMEM((width, SPLIT), F32), pltpu.VMEM((width, width - SPLIT), F32)]
    turned = pltpu.VMEM((width, rows), BF16)
    left, right = call(
        near_kernel,
        (pf_t, pf_dz, left, right),
        (shape(width, SPLIT, F32), shape(width, width - SPLIT, F32)),
        2 * rows * width * width,
        [turned, low, *accumulators, pltpu.SemaphoreType.DMA((6,)), pltpu.SemaphoreType.DMA((4,))],
        limit=LIMIT,
        anywhere=range(4),
        out_anywhere=True,
    )

    kinds = (F32, BF16, F32, BF16)
    parts = call(
        cut_kernel,
        (jnp.stack([x, y]), sib_q_t, got, sib_qf_t, left, right),
        [shape(288, count, kind) for count in (SPLIT, width - SPLIT) for kind in kinds],
        4 * rows * width * width,
        [turned, pltpu.VMEM((2 * rows, width), BF16), turned, *accumulators]
        + [pltpu.VMEM((288, count), BF16) for count in (SPLIT, width - SPLIT) for _ in (1, 3)]
        + [pltpu.SemaphoreType.DMA((7,)), pltpu.SemaphoreType.DMA((16,))],
        limit=LIMIT,
        anywhere=range(1, 6),
        out_anywhere=True,
    )

    def reduce(parts, along_x):
        keep_1, send_1, keep_3, send_3 = parts
        count = keep_1.shape[1]
        bit, other_bit, other = (3, 1, y) if along_x else (1, 3, x)
        got_1 = permute(send_1, lambda d: d ^ (1 << bit))
        got_3 = permute(send_3, lambda d: d ^ (3 << bit))
        own, send_3, send_1 = call(
            second_kernel,
            (keep_1, got_1, keep_3, got_3),
            (shape(288, count, F32), shape(144, count, F32), shape(144, count, F32)),
            288 * count,
            limit=8,
        )
        got_3 = permute(send_3, lambda d: d ^ (3 << bit))
        got_1 = permute(send_1, lambda d: d ^ (1 << bit))
        outs = call(
            third_kernel,
            (jnp.stack([other, 0]), own, got_3, got_1),
            [shape(72, count, F32)] * 4,
            288 * count,
            [pltpu.VMEM((288, count), F32)],
            limit=8,
        )
        return [outs[0]] + [permute(outs[j], lambda d, j=j: d ^ (j << other_bit)) for j in (1, 2, 3)]

    left = reduce(parts[:4], True)
    right = reduce(parts[4:], False)
    parts = call(
        z_pieces_kernel,
        (jnp.stack([z >> 1, 0]), *left, *right),
        [shape(18, width, F32)] * 4,
        6 * 72 * width,
        [pltpu.VMEM((72, width), F32), pltpu.VMEM((4, 24, width), F32)],
        limit=8,
    )
    parts = [parts[0]] + [permute(parts[j], lambda d, j=j: d ^ (j << 6)) for j in (1, 2, 3)]
    [part] = call(sum_kernel, parts, [shape(18, width, F32)], 3 * 18 * width, limit=8)

    def owner(d, flip):
        z, x, y, s = d >> 5, d >> 3 & 3, d >> 1 & 3, d & 1
        return (4 * s + x) << 5 | y << 3 | (z >> 1) << 1 | (z & 1) ^ flip

    mine, squares = call(
        last_kernel,
        (jnp.stack([core, 0]), permute(part, lambda d: owner(d, 0)), permute(part, lambda d: owner(d, 1))),
        (shape(9, width, F32), shape(1, 128, F32)),
        10 * 18 * width,
        limit=8,
    )
    for bit in (1, 2, 3, 4, 5, 6, 7):
        squares = squares + permute(squares, lambda d: d ^ (1 << bit))
    spread = jnp.sqrt(jnp.sum(squares) / (2 * width * width) + 1e-06)
    return mine / spread


def solution(mesh):
    return jax.shard_map(
        per_device,
        mesh=mesh,
        in_specs=(P("dp", None), P("dp", None), P(), P(), P(), P(), P("dp")),
        out_specs=P("dp", None),
        check_vma=False,
    )
```

```python
import functools

import jax
import jax.numpy as jnp
from jax import lax
from jax.experimental import pallas as pl
from jax.experimental.pallas import tpu as pltpu
from jax.sharding import PartitionSpec as P

SPLIT = 640
LIMIT = 62
F32, BF16 = jnp.float32, jnp.bfloat16
VMEM = pl.BlockSpec(memory_space=pltpu.VMEM)
SMEM = pl.BlockSpec(memory_space=pltpu.SMEM)
HBM = pl.BlockSpec(memory_space=pltpu.HBM)


def permute(value, target):
    pairs = [(source, target(source)) for source in range(lax.axis_size("dp"))]
    return lax.ppermute(value, "dp", pairs)


def sibling(value):
    return permute(value, lambda d: d ^ 1)


def dot(a, b):
    return jnp.dot(a, b, preferred_element_type=F32)


def call(kernel, ins, outs, flops, scratch=(), aliases=None, limit=48, far_ins=(), far_outs=()):
    moved = sum(v.size * v.dtype.itemsize for v in [*ins, *outs])
    return pl.pallas_call(
        kernel,
        out_shape=outs,
        in_specs=[SMEM if v.size <= 8 else HBM if at in far_ins else VMEM for at, v in enumerate(ins)],
        out_specs=[HBM if at in far_outs else VMEM for at in range(len(outs))],
        scratch_shapes=scratch,
        input_output_aliases=aliases or {},
        cost_estimate=pl.CostEstimate(
            flops=flops, bytes_accessed=moved if flops > 1 else 1, transcendentals=0
        ),
        compiler_params=pltpu.CompilerParams(vmem_limit_bytes=limit * 2**20),
    )(*ins)


def shape(rows, columns, kind):
    return jax.ShapeDtypeStruct((rows, columns), kind)


def embed(features, head):
    projected = dot(features, head)
    scale = jnp.sqrt(jnp.sum(projected * projected, axis=-1, keepdims=True) + 1e-06)
    return (projected / scale, scale)


def tile_slope(left, right, label_sign, temper, offset):
    scores = temper * dot(left, right.T) + offset
    margin = label_sign * scores
    return (-label_sign * jax.nn.sigmoid(-margin) * temper).astype(BF16)


def project(grad, unit, inverse):
    inner = jnp.sum(unit * grad, axis=-1, keepdims=True)
    return (grad - unit * inner) * inverse


def pairs_kernel(p_grad, p_unit, p_scale, q_grad, q_unit, q_scale, p_pair, q_pair):
    rows = p_grad.shape[0]
    for grad, unit, scale, out in ((q_grad, q_unit, q_scale, q_pair), (p_grad, p_unit, p_scale, p_pair)):
        for at in range(0, rows, 128):
            part = pl.ds(at, 128)
            value = project(grad[part, :], unit[part, :], 1.0 / scale[part, :])
            high = value.astype(BF16)
            out[part, :] = high
            out[pl.ds(rows + at, 128), :] = (value - high.astype(F32)).astype(BF16)


def early_kernel(p, sib_q, p_pair, left, right, sib_q_t, p_twice):
    rows, width = p.shape
    turned = p[...].T
    p_twice[:, :rows] = turned
    p_twice[:, rows:] = turned
    sib_q_t[...] = sib_q[...].T
    for at in range(0, width, 576):
        part = pl.ds(at, 576)
        left[part, :] = dot(p_twice[part, :], p_pair[:, :SPLIT])
        right[part, :] = dot(p_twice[part, :], p_pair[:, SPLIT:])


def other_early_kernel(sib_q_t, sib_pair, left, right, left_out, right_out):
    width, rows = sib_q_t.shape
    for at in range(0, width, 576):
        part = pl.ds(at, 576)
        for before, out, columns in (
            (left, left_out, pl.ds(0, SPLIT)),
            (right, right_out, pl.ds(SPLIT, width - SPLIT)),
        ):
            out[part, :] = (
                before[part, :]
                + dot(sib_q_t[part, :], sib_pair[pl.ds(0, rows), columns])
                + dot(sib_q_t[part, :], sib_pair[pl.ds(rows, rows), columns])
            )


def far_kernel(
    scalars, place, far_img, far_txt, p_head_in, q_head_in, q_low_in, q_unit_in, q_scale_in,
    send, qf_t, pf_dz, pf_t,
    pf, qf, p_head, q_head, q_low, q_unit, q_scale, pf_unit, qf_unit, pf_inverse, qf_inverse,
    pf_low, qf_low, slope_a, slope_b, sems,
):
    rows = pf.shape[0]
    step = 256
    first = place[0] == 0

    def copy(source, target, at):
        return pltpu.make_async_copy(source, target, sems.at[at])

    @pl.when(first)
    def _():
        copy(far_img, pf, 0).start()

    @pl.when(jnp.logical_not(first))
    def _():
        copy(far_txt, pf, 0).start()

    copies = [copy(p_head_in, p_head, 1)]
    copies[0].start()

    @pl.when(first)
    def _():
        copy(far_txt, qf, 2).start()

    @pl.when(jnp.logical_not(first))
    def _():
        copy(far_img, qf, 2).start()

    for at, (source, target) in enumerate(
        ((q_low_in, q_low), (q_head_in, q_head), (q_unit_in, q_unit), (q_scale_in, q_scale)), 3
    ):
        copies.append(copy(source, target, at))
        copies[-1].start()

    temper, offset = scalars[0], scalars[1]

    def embed_far(feats, head, unit, inverse, low):
        for at in range(0, rows, step):
            part = pl.ds(at, step)
            projected = dot(feats[part, :], head[...])
            length = jnp.sqrt(jnp.sum(projected * projected, axis=-1, keepdims=True) + 1e-06)
            inverse[part, :] = 1.0 / length
            there = projected * (1.0 / length)
            unit[part, :] = there
            low[part, :] = there.astype(BF16)

    def slopes(low, slope):
        for at in range(0, rows, step):
            part = pl.ds(at, step)
            raw = lax.dot_general(
                pf_low[part, :], low[...], (((1,), (1,)), ((), ())), preferred_element_type=F32
            )
            slope[part, :] = (jax.nn.sigmoid(temper * raw + offset) * temper).astype(BF16)

    copy(far_img, pf, 0).wait()
    copies[0].wait()
    embed_far(pf, p_head, pf_unit, pf_inverse, pf_low)
    pf_t[...] = pf[...].T
    for at in (1, 2, 3, 4):
        copies[at].wait()
    copy(far_txt, qf, 2).wait()
    qf_t[...] = qf[...].T
    slopes(q_low, slope_a)
    embed_far(qf, q_head, qf_unit, qf_inverse, qf_low)
    slopes(qf_low, slope_b)
    for at in range(0, rows, step):
        part = pl.ds(at, step)
        grad = dot(slope_a[:, part].T, pf_low[...])
        send[part, :] = project(grad, q_unit[part, :], 1.0 / q_scale[part, :]).astype(BF16)
        grad = dot(slope_b[:, part].T, pf_low[...])
        send[pl.ds(rows + at, step), :] = project(grad, qf_unit[part, :], qf_inverse[part, :]).astype(BF16)
        grad = dot(slope_a[part, :], q_low[...]) + dot(slope_b[part, :], qf_low[...])
        pf_dz[part, :] = project(grad, pf_unit[part, :], pf_inverse[part, :]).astype(BF16)


def fetch(pairs, sems):
    copies = [pltpu.make_async_copy(*pair, sems.at[at]) for at, pair in enumerate(pairs)]
    for copy in copies:
        copy.start()
    return lambda at: copies[at].wait()


def near_kernel(*refs):
    ins, outs, held, (in_sems, out_sems) = refs[:4], refs[4:6], refs[6:10], refs[10:]
    pf_t, pf_dz, left, right = held
    width = pf_t.shape[0]
    halves = [pl.ds(0, 576), pl.ds(576, 576)]
    wait = fetch(
        [(ins[1], pf_dz), (ins[0], pf_t)]
        + [(ins[2 + which].at[part, :], held[2 + which].at[part, :]) for part in halves for which in (0, 1)],
        in_sems,
    )
    wait(0)
    wait(1)
    stores = []
    for part in halves:
        for total, out, columns in (
            (left, outs[0], pl.ds(0, SPLIT)),
            (right, outs[1], pl.ds(SPLIT, width - SPLIT)),
        ):
            value = dot(pf_t[part, :], pf_dz[:, columns])
            at = len(stores)
            wait(2 + at)
            total[part, :] = total[part, :] + value
            stores.append(pltpu.make_async_copy(total.at[part, :], out.at[part, :], out_sems.at[at]))
            stores[-1].start()
    for store in stores:
        store.wait()


def cut_kernel(place, *refs):
    ins, outs, held, (in_sems,) = refs[:5], refs[5:13], refs[13:18], refs[18:]
    sib_q_t, got, sib_qf_t, left, right = held
    width, rows = sib_q_t.shape
    halves = [pl.ds(0, 576), pl.ds(576, 576)]
    wait = fetch(
        [(ins[at], held[at]) for at in range(3)]
        + [(ins[at].at[part, :], held[at].at[part, :]) for at in (3, 4) for part in halves],
        in_sems,
    )
    wait(0)
    wait(1)
    for along_x, total, columns in ((True, left, pl.ds(0, SPLIT)), (False, right, pl.ds(SPLIT, width - SPLIT))):
        for at, part in enumerate(halves):
            value = dot(sib_q_t[part, :], got[pl.ds(0, rows), columns])
            if along_x and at == 0:
                wait(2)
            value = value + dot(sib_qf_t[part, :], got[pl.ds(rows, rows), columns])
            wait((3 if along_x else 5) + at)
            total[part, :] = total[part, :] + value

        def half(target, which):
            if along_x:
                return total[pl.ds(pl.multiple_of(288 * target + 144 * which, 8), 144), :]
            starts = [288 * (2 * which + block) + 72 * target for block in (0, 1)]
            return jnp.concatenate([total[pl.ds(pl.multiple_of(at, 8), 72), :] for at in starts], axis=0)

        me = place[0] if along_x else place[1]
        keep_1, send_1, keep_3, send_3 = outs[:4] if along_x else outs[4:]
        top, low = pl.ds(0, 144), pl.ds(144, 144)
        keep_1[top, :] = half(me, 0)
        keep_1[low, :] = half(me ^ 3, 0)
        send_1[top, :] = half(me ^ 1, 0).astype(BF16)
        send_1[low, :] = half(me ^ 2, 0).astype(BF16)
        keep_3[top, :] = half(me, 1)
        keep_3[low, :] = half(me ^ 1, 1)
        send_3[top, :] = half(me ^ 3, 1).astype(BF16)
        send_3[low, :] = half(me ^ 2, 1).astype(BF16)


def second_kernel(keep_1, got_1, keep_3, got_3, own, send_3, send_1):
    top, low = pl.ds(0, 144), pl.ds(144, 144)
    first = keep_1[...] + got_1[...].astype(F32)
    own[top, :] = first[:144]
    send_3[...] = first[144:]
    other = keep_3[...] + got_3[...].astype(F32)
    own[low, :] = other[:144]
    send_1[...] = other[144:]


def third_kernel(place, own, got_3, got_1, *rest):
    outs, total = rest[:4], rest[4]
    total[pl.ds(0, 144), :] = own[pl.ds(0, 144), :] + got_3[...]
    total[pl.ds(144, 144), :] = own[pl.ds(144, 144), :] + got_1[...]
    for j in range(4):
        outs[j][...] = total[pl.ds(pl.multiple_of(72 * (place[0] ^ j), 8), 72), :]


def z_pieces_kernel(place, *rest):
    left, right, outs, total, padded = rest[:4], rest[4:8], rest[8:12], rest[12], rest[13]
    total[:, :SPLIT] = left[0][...] + left[1][...] + left[2][...] + left[3][...]
    total[:, SPLIT:] = right[0][...] + right[1][...] + right[2][...] + right[3][...]
    for at in range(4):
        padded[at, 0:18, :] = total[18 * at : 18 * at + 18, :]
    for j in range(4):
        outs[j][...] = padded[place[0] ^ j, 0:18, :]


def sum_kernel(a, b, c, d, total):
    total[...] = a[...] + b[...] + c[...] + d[...]


def last_kernel(place, a, b, mine, squares):
    total = a[...] + b[...]

    @pl.when(place[0] == 0)
    def _():
        mine[...] = total[0:9, :]

    @pl.when(place[0] != 0)
    def _():
        mine[...] = total[9:18, :]

    line = jnp.sum(total * total, axis=0, keepdims=True)
    lanes = line[:, 0:128]
    for at in range(128, line.shape[1], 128):
        lanes = lanes + line[:, at : at + 128]
    squares[...] = lanes


def spread_sum(value, bits):
    masks = [sum(1 << bit for at, bit in enumerate(bits) if k >> at & 1) for k in range(2 ** len(bits))]
    groups = [[d | mask for mask in masks] for d in range(lax.axis_size("dp")) if not d & masks[-1]]
    sent = jnp.broadcast_to(value, (8 * len(masks), 128))
    got = lax.all_to_all(sent, "dp", 0, 0, axis_index_groups=groups, tiled=True)
    return jnp.sum(got.reshape(len(masks), 8, 128)[:, :1], axis=0)


def per_device(img_feats, txt_feats, img_head, txt_head, log_temp, logit_bias, caption_row):
    me = lax.axis_index("dp")
    core, y, x, z = me & 1, (me >> 1) & 3, (me >> 3) & 3, me >> 5
    first = core == 0
    rows, width = img_feats.shape

    far_img = permute(img_feats, lambda d: d ^ (192 if d & 1 else 64))
    far_txt = permute(txt_feats, lambda d: d ^ (64 if d & 1 else 192))
    p = jnp.where(first, img_feats, txt_feats)
    q = jnp.where(first, txt_feats, img_feats)
    p_head = jnp.where(first, img_head, txt_head)
    q_head = jnp.where(first, txt_head, img_head)
    sib_q = sibling(q)

    temper = jnp.exp(log_temp)
    index = jnp.arange(rows, dtype=jnp.int32)
    match = jnp.where(first, caption_row, index)[:, None] == jnp.where(first, index, caption_row)[None, :]
    label_sign = jnp.where(match, 1.0, -1.0).astype(F32)

    p_unit, p_scale = embed(p, p_head)
    q_unit, q_scale = embed(q, q_head)
    p_low = p_unit.astype(BF16)
    q_low = q_unit.astype(BF16)
    slope = tile_slope(p_low, q_low, label_sign, temper, logit_bias)
    p_grad = dot(slope, q_low)
    q_grad = dot(slope.T, p_low)
    scalars = jnp.stack([temper, logit_bias])
    p_pair, q_pair = call(
        pairs_kernel,
        (p_grad, p_unit, p_scale, q_grad, q_unit, q_scale),
        (shape(2 * rows, width, BF16), shape(2 * rows, width, BF16)),
        1,
        limit=20,
    )
    sib_pair = sibling(q_pair)
    left, right, sib_q_t = call(
        early_kernel,
        (p, sib_q, p_pair),
        (shape(width, SPLIT, F32), shape(width, width - SPLIT, F32), shape(width, rows, BF16)),
        200 * rows * width * width,
        [pltpu.VMEM((width, 2 * rows), BF16)],
        limit=20,
    )
    left, right = call(
        other_early_kernel,
        (sib_q_t, sib_pair, left, right),
        (shape(width, SPLIT, F32), shape(width, width - SPLIT, F32)),
        1,
        (),
        {2: 0, 3: 1},
        limit=24,
    )
    far_img, far_txt, left, right, sib_q_t = lax.optimization_barrier(
        (far_img, far_txt, left, right, sib_q_t)
    )

    wide, low, thin = (pltpu.VMEM(dims, kind) for dims, kind in (
        ((rows, width), F32), ((rows, width), BF16), ((rows, 1), F32),
    ))
    head, tile = pltpu.VMEM((width, width), BF16), pltpu.VMEM((rows, rows), BF16)
    send, qf_t, pf_dz, pf_t = call(
        far_kernel,
        (scalars, jnp.stack([core, 0]), far_img, far_txt, p_head, q_head, q_low, q_unit, q_scale),
        (shape(2 * rows, width, BF16), shape(width, rows, BF16), shape(rows, width, BF16), shape(width, rows, BF16)),
        4 * rows * width * width + 12 * rows * rows * width,
        [
            low, low, head, head, low, wide, thin, wide, wide, thin, thin,
            low, low, tile, tile, pltpu.SemaphoreType.DMA((7,)),
        ],
        limit=LIMIT,
        far_ins=range(9),
    )
    got, sib_qf_t = sibling(send), sibling(qf_t)
    accumulators = [pltpu.VMEM((width, SPLIT), F32), pltpu.VMEM((width, width - SPLIT), F32)]
    turned = pltpu.VMEM((width, rows), BF16)
    left, right = call(
        near_kernel,
        (pf_t, pf_dz, left, right),
        (shape(width, SPLIT, F32), shape(width, width - SPLIT, F32)),
        2 * rows * width * width,
        [turned, low, *accumulators, pltpu.SemaphoreType.DMA((6,)), pltpu.SemaphoreType.DMA((4,))],
        limit=LIMIT,
        far_ins=range(4),
        far_outs=range(2),
    )

    kinds = (F32, BF16, F32, BF16)
    parts = call(
        cut_kernel,
        (jnp.stack([x, y]), sib_q_t, got, sib_qf_t, left, right),
        [shape(288, count, kind) for count in (SPLIT, width - SPLIT) for kind in kinds],
        4 * rows * width * width,
        [turned, pltpu.VMEM((2 * rows, width), BF16), turned, *accumulators, pltpu.SemaphoreType.DMA((7,))],
        limit=32,
        far_ins=range(1, 6),
    )

    def reduce(parts, along_x):
        keep_1, send_1, keep_3, send_3 = parts
        count = keep_1.shape[1]
        bit, other_bit, other = (3, 1, y) if along_x else (1, 3, x)
        got_1 = permute(send_1, lambda d: d ^ (1 << bit))
        got_3 = permute(send_3, lambda d: d ^ (3 << bit))
        own, send_3, send_1 = call(
            second_kernel,
            (keep_1, got_1, keep_3, got_3),
            (shape(288, count, F32), shape(144, count, F32), shape(144, count, F32)),
            288 * count,
            limit=8,
        )
        got_3 = permute(send_3, lambda d: d ^ (3 << bit))
        got_1 = permute(send_1, lambda d: d ^ (1 << bit))
        outs = call(
            third_kernel,
            (jnp.stack([other, 0]), own, got_3, got_1),
            [shape(72, count, F32)] * 4,
            288 * count,
            [pltpu.VMEM((288, count), F32)],
            limit=8,
        )
        return [outs[0]] + [permute(outs[j], lambda d, j=j: d ^ (j << other_bit)) for j in (1, 2, 3)]

    left = reduce(parts[:4], True)
    right = reduce(parts[4:], False)
    parts = call(
        z_pieces_kernel,
        (jnp.stack([z >> 1, 0]), *left, *right),
        [shape(18, width, F32)] * 4,
        6 * 72 * width,
        [pltpu.VMEM((72, width), F32), pltpu.VMEM((4, 24, width), F32)],
        limit=8,
    )
    parts = [parts[0]] + [permute(parts[j], lambda d, j=j: d ^ (j << 6)) for j in (1, 2, 3)]
    [part] = call(sum_kernel, parts, [shape(18, width, F32)], 3 * 18 * width, limit=8)

    other = permute(part, lambda d: d ^ 32)
    total, squares = call(
        last_kernel,
        (jnp.stack([z & 1, 0]), part, other),
        (shape(9, width, F32), shape(1, 128, F32)),
        10 * 18 * width,
        limit=8,
    )

    def owner(d):
        z, x, y, s = d >> 5, d >> 3 & 3, d >> 1 & 3, d & 1
        return (4 * s + x) << 5 | y << 3 | (z >> 1) << 1 | z & 1

    mine = permute(total, owner)
    for bits in ((0, 6, 7), (3, 4), (1, 2)):
        squares = spread_sum(squares, bits)
    spread = jnp.sqrt(jnp.sum(squares) / (2 * width * width) + 1e-06)
    return mine / spread


def solution(mesh):
    return jax.shard_map(
        per_device,
        mesh=mesh,
        in_specs=(P("dp", None), P("dp", None), P(), P(), P(), P(), P("dp")),
        out_specs=P("dp", None),
        check_vma=False,
    )
```

```python
import functools

import jax
import jax.numpy as jnp
from jax import lax
from jax.experimental import pallas as pl
from jax.experimental.pallas import tpu as pltpu
from jax.sharding import PartitionSpec as P

SPLIT = 640
LIMIT = 62
F32, BF16 = jnp.float32, jnp.bfloat16
VMEM = pl.BlockSpec(memory_space=pltpu.VMEM)
SMEM = pl.BlockSpec(memory_space=pltpu.SMEM)
HBM = pl.BlockSpec(memory_space=pltpu.HBM)


def permute(value, target):
    pairs = [(source, target(source)) for source in range(lax.axis_size("dp"))]
    return lax.ppermute(value, "dp", pairs)


def sibling(value):
    return permute(value, lambda d: d ^ 1)


def dot(a, b):
    return jnp.dot(a, b, preferred_element_type=F32)


def call(kernel, ins, outs, flops, scratch=(), aliases=None, limit=48, far_ins=(), far_outs=()):
    moved = sum(v.size * v.dtype.itemsize for v in [*ins, *outs])
    return pl.pallas_call(
        kernel,
        out_shape=outs,
        in_specs=[SMEM if v.size <= 8 else HBM if at in far_ins else VMEM for at, v in enumerate(ins)],
        out_specs=[HBM if at in far_outs else VMEM for at in range(len(outs))],
        scratch_shapes=scratch,
        input_output_aliases=aliases or {},
        cost_estimate=pl.CostEstimate(
            flops=flops, bytes_accessed=moved if flops > 1 else 1, transcendentals=0
        ),
        compiler_params=pltpu.CompilerParams(vmem_limit_bytes=limit * 2**20),
    )(*ins)


def shape(rows, columns, kind):
    return jax.ShapeDtypeStruct((rows, columns), kind)


def embed(features, head):
    projected = dot(features, head)
    scale = jnp.sqrt(jnp.sum(projected * projected, axis=-1, keepdims=True) + 1e-06)
    return (projected / scale, scale)


def tile_slope(left, right, label_sign, temper, offset):
    scores = temper * dot(left, right.T) + offset
    margin = label_sign * scores
    return (-label_sign * jax.nn.sigmoid(-margin) * temper).astype(BF16)


def project(grad, unit, inverse):
    inner = jnp.sum(unit * grad, axis=-1, keepdims=True)
    return (grad - unit * inner) * inverse


def pairs_kernel(p_grad, p_unit, p_scale, q_grad, q_unit, q_scale, p_pair, q_pair):
    rows = p_grad.shape[0]
    for grad, unit, scale, out in ((q_grad, q_unit, q_scale, q_pair), (p_grad, p_unit, p_scale, p_pair)):
        for at in range(0, rows, 128):
            part = pl.ds(at, 128)
            value = project(grad[part, :], unit[part, :], 1.0 / scale[part, :])
            high = value.astype(BF16)
            out[part, :] = high
            out[pl.ds(rows + at, 128), :] = (value - high.astype(F32)).astype(BF16)


def early_kernel(p, sib_q, p_pair, left, right, sib_q_t, p_twice):
    rows, width = p.shape
    turned = p[...].T
    p_twice[:, :rows] = turned
    p_twice[:, rows:] = turned
    sib_q_t[...] = sib_q[...].T
    for at in range(0, width, 576):
        part = pl.ds(at, 576)
        left[part, :] = dot(p_twice[part, :], p_pair[:, :SPLIT])
        right[part, :] = dot(p_twice[part, :], p_pair[:, SPLIT:])


def other_early_kernel(sib_q_t, sib_pair, left, right, left_out, right_out):
    width, rows = sib_q_t.shape
    for at in range(0, width, 576):
        part = pl.ds(at, 576)
        for before, out, columns in (
            (left, left_out, pl.ds(0, SPLIT)),
            (right, right_out, pl.ds(SPLIT, width - SPLIT)),
        ):
            out[part, :] = (
                before[part, :]
                + dot(sib_q_t[part, :], sib_pair[pl.ds(0, rows), columns])
                + dot(sib_q_t[part, :], sib_pair[pl.ds(rows, rows), columns])
            )


def far_kernel(
    scalars, place, far_img, far_txt, p_head_in, q_head_in, q_low_in, q_unit_in, q_scale_in,
    send_out, qf_t_out, pf_dz_out, pf_t_out,
    send, qf_t, pf_dz, pf_t, pf, qf, p_head, q_head, q_low, q_unit, q_scale, pf_unit, qf_unit, pf_inverse, qf_inverse,
    pf_low, qf_low, slope_a, slope_b, sems, out_sems,
):
    rows = pf.shape[0]
    step = 256
    first = place[0] == 0

    def copy(source, target, at):
        return pltpu.make_async_copy(source, target, sems.at[at])

    @pl.when(first)
    def _():
        copy(far_img, pf, 0).start()

    @pl.when(jnp.logical_not(first))
    def _():
        copy(far_txt, pf, 0).start()

    copies = [copy(p_head_in, p_head, 1)]
    copies[0].start()

    @pl.when(first)
    def _():
        copy(far_txt, qf, 2).start()

    @pl.when(jnp.logical_not(first))
    def _():
        copy(far_img, qf, 2).start()

    for at, (source, target) in enumerate(
        ((q_low_in, q_low), (q_head_in, q_head), (q_unit_in, q_unit), (q_scale_in, q_scale)), 3
    ):
        copies.append(copy(source, target, at))
        copies[-1].start()

    temper, offset = scalars[0], scalars[1]
    stores = []

    def store(source, target, *part):
        if part:
            source, target = source.at[part], target.at[part]
        stores.append(pltpu.make_async_copy(source, target, out_sems.at[len(stores)]))
        stores[-1].start()

    def embed_far(feats, head, unit, inverse, low):
        for at in range(0, rows, step):
            part = pl.ds(at, step)
            projected = dot(feats[part, :], head[...])
            length = jnp.sqrt(jnp.sum(projected * projected, axis=-1, keepdims=True) + 1e-06)
            inverse[part, :] = 1.0 / length
            there = projected * (1.0 / length)
            unit[part, :] = there
            low[part, :] = there.astype(BF16)

    def slopes(low, slope):
        for at in range(0, rows, step):
            part = pl.ds(at, step)
            raw = lax.dot_general(
                pf_low[part, :], low[...], (((1,), (1,)), ((), ())), preferred_element_type=F32
            )
            slope[part, :] = (jax.nn.sigmoid(temper * raw + offset) * temper).astype(BF16)

    copy(far_img, pf, 0).wait()
    copies[0].wait()
    embed_far(pf, p_head, pf_unit, pf_inverse, pf_low)
    pf_t[...] = pf[...].T
    store(pf_t, pf_t_out)
    for at in (1, 2, 3, 4):
        copies[at].wait()
    copy(far_txt, qf, 2).wait()
    qf_t[...] = qf[...].T
    store(qf_t, qf_t_out)
    slopes(q_low, slope_a)
    embed_far(qf, q_head, qf_unit, qf_inverse, qf_low)
    slopes(qf_low, slope_b)
    for at in range(0, rows, step):
        part = pl.ds(at, step)
        grad = dot(slope_a[:, part].T, pf_low[...])
        send[part, :] = project(grad, q_unit[part, :], 1.0 / q_scale[part, :]).astype(BF16)
        store(send, send_out, part)
        again = pl.ds(rows + at, step)
        grad = dot(slope_b[:, part].T, pf_low[...])
        send[again, :] = project(grad, qf_unit[part, :], qf_inverse[part, :]).astype(BF16)
        store(send, send_out, again)
        grad = dot(slope_a[part, :], q_low[...]) + dot(slope_b[part, :], qf_low[...])
        pf_dz[part, :] = project(grad, pf_unit[part, :], pf_inverse[part, :]).astype(BF16)
        store(pf_dz, pf_dz_out, part)
    for copy_out in stores:
        copy_out.wait()


def fetch(pairs, sems):
    copies = [pltpu.make_async_copy(*pair, sems.at[at]) for at, pair in enumerate(pairs)]
    for copy in copies:
        copy.start()
    return lambda at: copies[at].wait()


def near_kernel(*refs):
    ins, outs, held, (in_sems, out_sems) = refs[:4], refs[4:6], refs[6:10], refs[10:]
    pf_t, pf_dz, left, right = held
    width = pf_t.shape[0]
    halves = [pl.ds(0, 576), pl.ds(576, 576)]
    wait = fetch(
        [(ins[1], pf_dz), (ins[0], pf_t)]
        + [(ins[2 + which].at[part, :], held[2 + which].at[part, :]) for part in halves for which in (0, 1)],
        in_sems,
    )
    wait(0)
    wait(1)
    stores = []
    for part in halves:
        for total, out, columns in (
            (left, outs[0], pl.ds(0, SPLIT)),
            (right, outs[1], pl.ds(SPLIT, width - SPLIT)),
        ):
            value = dot(pf_t[part, :], pf_dz[:, columns])
            at = len(stores)
            wait(2 + at)
            total[part, :] = total[part, :] + value
            stores.append(pltpu.make_async_copy(total.at[part, :], out.at[part, :], out_sems.at[at]))
            stores[-1].start()
    for store in stores:
        store.wait()


def cut_kernel(place, *refs):
    ins, outs, held, (in_sems,) = refs[:5], refs[5:13], refs[13:18], refs[18:]
    sib_q_t, got, sib_qf_t, left, right = held
    width, rows = sib_q_t.shape
    halves = [pl.ds(0, 576), pl.ds(576, 576)]
    wait = fetch(
        [(ins[at], held[at]) for at in range(3)]
        + [(ins[at].at[part, :], held[at].at[part, :]) for at in (3, 4) for part in halves],
        in_sems,
    )
    wait(0)
    wait(1)
    for along_x, total, columns in ((True, left, pl.ds(0, SPLIT)), (False, right, pl.ds(SPLIT, width - SPLIT))):
        for at, part in enumerate(halves):
            value = dot(sib_q_t[part, :], got[pl.ds(0, rows), columns])
            if along_x and at == 0:
                wait(2)
            value = value + dot(sib_qf_t[part, :], got[pl.ds(rows, rows), columns])
            wait((3 if along_x else 5) + at)
            total[part, :] = total[part, :] + value

        def half(target, which):
            if along_x:
                return total[pl.ds(pl.multiple_of(288 * target + 144 * which, 8), 144), :]
            starts = [288 * (2 * which + block) + 72 * target for block in (0, 1)]
            return jnp.concatenate([total[pl.ds(pl.multiple_of(at, 8), 72), :] for at in starts], axis=0)

        me = place[0] if along_x else place[1]
        keep_1, send_1, keep_3, send_3 = outs[:4] if along_x else outs[4:]
        top, low = pl.ds(0, 144), pl.ds(144, 144)
        keep_1[top, :] = half(me, 0)
        keep_1[low, :] = half(me ^ 3, 0)
        send_1[top, :] = half(me ^ 1, 0).astype(BF16)
        send_1[low, :] = half(me ^ 2, 0).astype(BF16)
        keep_3[top, :] = half(me, 1)
        keep_3[low, :] = half(me ^ 1, 1)
        send_3[top, :] = half(me ^ 3, 1).astype(BF16)
        send_3[low, :] = half(me ^ 2, 1).astype(BF16)


def second_kernel(keep_1, got_1, keep_3, got_3, own, send_3, send_1):
    top, low = pl.ds(0, 144), pl.ds(144, 144)
    first = keep_1[...] + got_1[...].astype(F32)
    own[top, :] = first[:144]
    send_3[...] = first[144:]
    other = keep_3[...] + got_3[...].astype(F32)
    own[low, :] = other[:144]
    send_1[...] = other[144:]


def third_kernel(place, own, got_3, got_1, *rest):
    outs, total = rest[:4], rest[4]
    total[pl.ds(0, 144), :] = own[pl.ds(0, 144), :] + got_3[...]
    total[pl.ds(144, 144), :] = own[pl.ds(144, 144), :] + got_1[...]
    for j in range(4):
        outs[j][...] = total[pl.ds(pl.multiple_of(72 * (place[0] ^ j), 8), 72), :]


def z_pieces_kernel(place, *rest):
    left, right, outs, total, padded = rest[:4], rest[4:8], rest[8:12], rest[12], rest[13]
    total[:, :SPLIT] = left[0][...] + left[1][...] + left[2][...] + left[3][...]
    total[:, SPLIT:] = right[0][...] + right[1][...] + right[2][...] + right[3][...]
    for at in range(4):
        padded[at, 0:18, :] = total[18 * at : 18 * at + 18, :]
    for j in range(4):
        outs[j][...] = padded[place[0] ^ j, 0:18, :]


def sum_kernel(a, b, c, d, total):
    total[...] = a[...] + b[...] + c[...] + d[...]


def last_kernel(place, a, b, mine, squares):
    total = a[...] + b[...]

    @pl.when(place[0] == 0)
    def _():
        mine[...] = total[0:9, :]

    @pl.when(place[0] != 0)
    def _():
        mine[...] = total[9:18, :]

    line = jnp.sum(total * total, axis=0, keepdims=True)
    lanes = line[:, 0:128]
    for at in range(128, line.shape[1], 128):
        lanes = lanes + line[:, at : at + 128]
    squares[...] = jnp.broadcast_to(lanes, squares.shape)


def lanes_kernel(got, squares):
    lanes = jnp.sum(got[...], axis=0, keepdims=True) * 0.125
    squares[...] = jnp.broadcast_to(lanes, squares.shape)


def scale_kernel(rows, got, out):
    total = jnp.sum(jnp.sum(got[...], axis=0, keepdims=True), axis=1, keepdims=True) * 0.125
    entries = 2 * rows.shape[1] * rows.shape[1]
    out[...] = rows[...] / jnp.sqrt(total / entries + 1e-06)


def swap_all(value, bits):
    masks = [sum(1 << bit for at, bit in enumerate(bits) if k >> at & 1) for k in range(2 ** len(bits))]
    groups = [[d | mask for mask in masks] for d in range(lax.axis_size("dp")) if not d & masks[-1]]
    return lax.all_to_all(value, "dp", 0, 0, axis_index_groups=groups, tiled=True)


def per_device(img_feats, txt_feats, img_head, txt_head, log_temp, logit_bias, caption_row):
    me = lax.axis_index("dp")
    core, y, x, z = me & 1, (me >> 1) & 3, (me >> 3) & 3, me >> 5
    first = core == 0
    rows, width = img_feats.shape

    far_img = permute(img_feats, lambda d: d ^ (192 if d & 1 else 64))
    far_txt = permute(txt_feats, lambda d: d ^ (64 if d & 1 else 192))
    p = jnp.where(first, img_feats, txt_feats)
    q = jnp.where(first, txt_feats, img_feats)
    p_head = jnp.where(first, img_head, txt_head)
    q_head = jnp.where(first, txt_head, img_head)
    sib_q = sibling(q)

    temper = jnp.exp(log_temp)
    index = jnp.arange(rows, dtype=jnp.int32)
    match = jnp.where(first, caption_row, index)[:, None] == jnp.where(first, index, caption_row)[None, :]
    label_sign = jnp.where(match, 1.0, -1.0).astype(F32)

    p_unit, p_scale = embed(p, p_head)
    q_unit, q_scale = embed(q, q_head)
    p_low = p_unit.astype(BF16)
    q_low = q_unit.astype(BF16)
    slope = tile_slope(p_low, q_low, label_sign, temper, logit_bias)
    p_grad = dot(slope, q_low)
    q_grad = dot(slope.T, p_low)
    scalars = jnp.stack([temper, logit_bias])
    p_pair, q_pair = call(
        pairs_kernel,
        (p_grad, p_unit, p_scale, q_grad, q_unit, q_scale),
        (shape(2 * rows, width, BF16), shape(2 * rows, width, BF16)),
        1,
        limit=20,
    )
    sib_pair = sibling(q_pair)
    left, right, sib_q_t = call(
        early_kernel,
        (p, sib_q, p_pair),
        (shape(width, SPLIT, F32), shape(width, width - SPLIT, F32), shape(width, rows, BF16)),
        200 * rows * width * width,
        [pltpu.VMEM((width, 2 * rows), BF16)],
        limit=20,
    )
    left, right = call(
        other_early_kernel,
        (sib_q_t, sib_pair, left, right),
        (shape(width, SPLIT, F32), shape(width, width - SPLIT, F32)),
        1,
        (),
        {2: 0, 3: 1},
        limit=24,
    )
    far_img, far_txt, left, right, sib_q_t = lax.optimization_barrier(
        (far_img, far_txt, left, right, sib_q_t)
    )

    wide, low, thin = (pltpu.VMEM(dims, kind) for dims, kind in (
        ((rows, width), F32), ((rows, width), BF16), ((rows, 1), F32),
    ))
    head, tile = pltpu.VMEM((width, width), BF16), pltpu.VMEM((rows, rows), BF16)
    turned = pltpu.VMEM((width, rows), BF16)
    send, qf_t, pf_dz, pf_t = call(
        far_kernel,
        (scalars, jnp.stack([core, 0]), far_img, far_txt, p_head, q_head, q_low, q_unit, q_scale),
        (shape(2 * rows, width, BF16), shape(width, rows, BF16), shape(rows, width, BF16), shape(width, rows, BF16)),
        4 * rows * width * width + 12 * rows * rows * width,
        [
            pltpu.VMEM((2 * rows, width), BF16), turned, low, turned,
            low, low, head, head, low, wide, thin, wide, wide, thin, thin,
            low, low, tile, tile, pltpu.SemaphoreType.DMA((7,)), pltpu.SemaphoreType.DMA((8,)),
        ],
        limit=LIMIT,
        far_ins=range(9),
        far_outs=range(4),
    )
    got, sib_qf_t = sibling(send), sibling(qf_t)
    accumulators = [pltpu.VMEM((width, SPLIT), F32), pltpu.VMEM((width, width - SPLIT), F32)]
    left, right = call(
        near_kernel,
        (pf_t, pf_dz, left, right),
        (shape(width, SPLIT, F32), shape(width, width - SPLIT, F32)),
        2 * rows * width * width,
        [turned, low, *accumulators, pltpu.SemaphoreType.DMA((6,)), pltpu.SemaphoreType.DMA((4,))],
        limit=LIMIT,
        far_ins=range(4),
        far_outs=range(2),
    )

    kinds = (F32, BF16, F32, BF16)
    parts = call(
        cut_kernel,
        (jnp.stack([x, y]), sib_q_t, got, sib_qf_t, left, right),
        [shape(288, count, kind) for count in (SPLIT, width - SPLIT) for kind in kinds],
        4 * rows * width * width,
        [turned, pltpu.VMEM((2 * rows, width), BF16), turned, *accumulators, pltpu.SemaphoreType.DMA((7,))],
        limit=32,
        far_ins=range(1, 6),
    )

    def reduce(parts, along_x):
        keep_1, send_1, keep_3, send_3 = parts
        count = keep_1.shape[1]
        bit, other_bit, other = (3, 1, y) if along_x else (1, 3, x)
        got_1 = permute(send_1, lambda d: d ^ (1 << bit))
        got_3 = permute(send_3, lambda d: d ^ (3 << bit))
        own, send_3, send_1 = call(
            second_kernel,
            (keep_1, got_1, keep_3, got_3),
            (shape(288, count, F32), shape(144, count, F32), shape(144, count, F32)),
            288 * count,
            limit=8,
        )
        got_3 = permute(send_3, lambda d: d ^ (3 << bit))
        got_1 = permute(send_1, lambda d: d ^ (1 << bit))
        outs = call(
            third_kernel,
            (jnp.stack([other, 0]), own, got_3, got_1),
            [shape(72, count, F32)] * 4,
            288 * count,
            [pltpu.VMEM((288, count), F32)],
            limit=8,
        )
        return [outs[0]] + [permute(outs[j], lambda d, j=j: d ^ (j << other_bit)) for j in (1, 2, 3)]

    left = reduce(parts[:4], True)
    right = reduce(parts[4:], False)
    parts = call(
        z_pieces_kernel,
        (jnp.stack([z >> 1, 0]), *left, *right),
        [shape(18, width, F32)] * 4,
        6 * 72 * width,
        [pltpu.VMEM((72, width), F32), pltpu.VMEM((4, 24, width), F32)],
        limit=8,
    )
    parts = [parts[0]] + [permute(parts[j], lambda d, j=j: d ^ (j << 6)) for j in (1, 2, 3)]
    [part] = call(sum_kernel, parts, [shape(18, width, F32)], 3 * 18 * width, limit=8)

    other = permute(part, lambda d: d ^ 32)
    total, squares = call(
        last_kernel,
        (jnp.stack([z & 1, 0]), part, other),
        (shape(9, width, F32), shape(64, 128, F32)),
        10 * 18 * width,
        limit=8,
    )

    def owner(d):
        z, x, y, s = d >> 5, d >> 3 & 3, d >> 1 & 3, d & 1
        return (4 * s + x) << 5 | y << 3 | (z >> 1) << 1 | z & 1

    mine = permute(total, owner)
    [squares] = call(lanes_kernel, (swap_all(squares, (0, 6, 7)),), [shape(128, 128, F32)], 10000, limit=8)
    got = swap_all(squares, (1, 2, 3, 4))
    [out] = call(scale_kernel, (mine, got), [shape(9, width, F32)], 10 * 9 * width, limit=8)
    return out


def solution(mesh):
    return jax.shard_map(
        per_device,
        mesh=mesh,
        in_specs=(P("dp", None), P("dp", None), P(), P(), P(), P(), P("dp")),
        out_specs=P("dp", None),
        check_vma=False,
    )
```

```python
import functools

import jax
import jax.numpy as jnp
from jax import lax
from jax.experimental import pallas as pl
from jax.experimental.pallas import tpu as pltpu
from jax.sharding import PartitionSpec as P

SPLIT = 640
LIMIT = 62
F32, BF16 = jnp.float32, jnp.bfloat16
VMEM = pl.BlockSpec(memory_space=pltpu.VMEM)
SMEM = pl.BlockSpec(memory_space=pltpu.SMEM)
HBM = pl.BlockSpec(memory_space=pltpu.HBM)


def permute(value, target):
    pairs = [(source, target(source)) for source in range(lax.axis_size("dp"))]
    return lax.ppermute(value, "dp", pairs)


def sibling(value):
    return permute(value, lambda d: d ^ 1)


def dot(a, b):
    return jnp.dot(a, b, preferred_element_type=F32)


def call(kernel, ins, outs, flops, scratch=(), aliases=None, limit=48, far_ins=(), far_outs=()):
    moved = sum(v.size * v.dtype.itemsize for v in [*ins, *outs])
    return pl.pallas_call(
        kernel,
        out_shape=outs,
        in_specs=[SMEM if v.size <= 8 else HBM if at in far_ins else VMEM for at, v in enumerate(ins)],
        out_specs=[HBM if at in far_outs else VMEM for at in range(len(outs))],
        scratch_shapes=scratch,
        input_output_aliases=aliases or {},
        cost_estimate=pl.CostEstimate(
            flops=flops, bytes_accessed=moved if flops > 1 else 1, transcendentals=0
        ),
        compiler_params=pltpu.CompilerParams(vmem_limit_bytes=limit * 2**20),
    )(*ins)


def shape(rows, columns, kind):
    return jax.ShapeDtypeStruct((rows, columns), kind)


def embed(features, head):
    projected = dot(features, head)
    scale = jnp.sqrt(jnp.sum(projected * projected, axis=-1, keepdims=True) + 1e-06)
    return (projected / scale, scale)


def tile_slope(left, right, label_sign, temper, offset):
    scores = temper * dot(left, right.T) + offset
    margin = label_sign * scores
    return (-label_sign * jax.nn.sigmoid(-margin) * temper).astype(BF16)


def project(grad, unit, inverse):
    inner = jnp.sum(unit * grad, axis=-1, keepdims=True)
    return (grad - unit * inner) * inverse


def pairs_kernel(p_grad, p_unit, p_scale, q_grad, q_unit, q_scale, p_pair, q_pair):
    rows = p_grad.shape[0]
    for grad, unit, scale, out in ((q_grad, q_unit, q_scale, q_pair), (p_grad, p_unit, p_scale, p_pair)):
        for at in range(0, rows, 128):
            part = pl.ds(at, 128)
            value = project(grad[part, :], unit[part, :], 1.0 / scale[part, :])
            high = value.astype(BF16)
            out[part, :] = high
            out[pl.ds(rows + at, 128), :] = (value - high.astype(F32)).astype(BF16)


def early_kernel(p, sib_q, p_pair, left, right, sib_q_t, p_twice):
    rows, width = p.shape
    turned = p[...].T
    p_twice[:, :rows] = turned
    p_twice[:, rows:] = turned
    sib_q_t[...] = sib_q[...].T
    for at in range(0, width, 576):
        part = pl.ds(at, 576)
        left[part, :] = dot(p_twice[part, :], p_pair[:, :SPLIT])
        right[part, :] = dot(p_twice[part, :], p_pair[:, SPLIT:])


def other_early_kernel(sib_q_t, sib_pair, left, right, left_out, right_out):
    width, rows = sib_q_t.shape
    for at in range(0, width, 576):
        part = pl.ds(at, 576)
        for before, out, columns in (
            (left, left_out, pl.ds(0, SPLIT)),
            (right, right_out, pl.ds(SPLIT, width - SPLIT)),
        ):
            out[part, :] = (
                before[part, :]
                + dot(sib_q_t[part, :], sib_pair[pl.ds(0, rows), columns])
                + dot(sib_q_t[part, :], sib_pair[pl.ds(rows, rows), columns])
            )


def far_kernel(
    scalars, place, far_img, far_txt, p_head_in, q_head_in, q_low_in, q_unit_in, q_scale_in,
    send_out, qf_t_out, pf_dz_out, pf_t_out,
    send, qf_t, pf_dz, pf_t, pf, qf, p_head, q_head, q_low, q_unit, q_scale, pf_unit, qf_unit, pf_inverse, qf_inverse,
    pf_low, qf_low, slope_a, slope_b, sems, out_sems,
):
    rows = pf.shape[0]
    step = 256
    first = place[0] == 0

    def copy(source, target, at):
        return pltpu.make_async_copy(source, target, sems.at[at])

    @pl.when(first)
    def _():
        copy(far_img, pf, 0).start()

    @pl.when(jnp.logical_not(first))
    def _():
        copy(far_txt, pf, 0).start()

    copies = [copy(p_head_in, p_head, 1)]
    copies[0].start()

    @pl.when(first)
    def _():
        copy(far_txt, qf, 2).start()

    @pl.when(jnp.logical_not(first))
    def _():
        copy(far_img, qf, 2).start()

    for at, (source, target) in enumerate(
        ((q_low_in, q_low), (q_head_in, q_head), (q_unit_in, q_unit), (q_scale_in, q_scale)), 3
    ):
        copies.append(copy(source, target, at))
        copies[-1].start()

    temper, offset = scalars[0], scalars[1]
    stores = []

    def store(source, target, *part):
        if part:
            source, target = source.at[part], target.at[part]
        stores.append(pltpu.make_async_copy(source, target, out_sems.at[len(stores)]))
        stores[-1].start()

    def embed_far(feats, head, unit, inverse, low):
        for at in range(0, rows, step):
            part = pl.ds(at, step)
            projected = dot(feats[part, :], head[...])
            length = jnp.sqrt(jnp.sum(projected * projected, axis=-1, keepdims=True) + 1e-06)
            inverse[part, :] = 1.0 / length
            there = projected * (1.0 / length)
            unit[part, :] = there
            low[part, :] = there.astype(BF16)

    def slopes(low, slope):
        for at in range(0, rows, step):
            part = pl.ds(at, step)
            raw = lax.dot_general(
                pf_low[part, :], low[...], (((1,), (1,)), ((), ())), preferred_element_type=F32
            )
            slope[part, :] = (jax.nn.sigmoid(temper * raw + offset) * temper).astype(BF16)

    copy(far_img, pf, 0).wait()
    copies[0].wait()
    embed_far(pf, p_head, pf_unit, pf_inverse, pf_low)
    pf_t[...] = pf[...].T
    store(pf_t, pf_t_out)
    for at in (1, 2, 3, 4):
        copies[at].wait()
    copy(far_txt, qf, 2).wait()
    qf_t[...] = qf[...].T
    store(qf_t, qf_t_out)
    slopes(q_low, slope_a)
    embed_far(qf, q_head, qf_unit, qf_inverse, qf_low)
    slopes(qf_low, slope_b)
    for at in range(0, rows, step):
        part = pl.ds(at, step)
        grad = dot(slope_a[:, part].T, pf_low[...])
        send[part, :] = project(grad, q_unit[part, :], 1.0 / q_scale[part, :]).astype(BF16)
        store(send, send_out, part)
        again = pl.ds(rows + at, step)
        grad = dot(slope_b[:, part].T, pf_low[...])
        send[again, :] = project(grad, qf_unit[part, :], qf_inverse[part, :]).astype(BF16)
        store(send, send_out, again)
        grad = dot(slope_a[part, :], q_low[...]) + dot(slope_b[part, :], qf_low[...])
        pf_dz[part, :] = project(grad, pf_unit[part, :], pf_inverse[part, :]).astype(BF16)
        store(pf_dz, pf_dz_out, part)
    for copy_out in stores:
        copy_out.wait()


def fetch(pairs, sems):
    copies = [pltpu.make_async_copy(*pair, sems.at[at]) for at, pair in enumerate(pairs)]
    for copy in copies:
        copy.start()
    return lambda at: copies[at].wait()


def near_kernel(*refs):
    ins, outs, held, (in_sems, out_sems) = refs[:4], refs[4:6], refs[6:10], refs[10:]
    pf_t, pf_dz, left, right = held
    width = pf_t.shape[0]
    halves = [pl.ds(0, 576), pl.ds(576, 576)]
    wait = fetch(
        [(ins[1], pf_dz), (ins[0], pf_t)]
        + [(ins[2 + which].at[part, :], held[2 + which].at[part, :]) for part in halves for which in (0, 1)],
        in_sems,
    )
    wait(0)
    wait(1)
    stores = []
    for part in halves:
        for total, out, columns in (
            (left, outs[0], pl.ds(0, SPLIT)),
            (right, outs[1], pl.ds(SPLIT, width - SPLIT)),
        ):
            value = dot(pf_t[part, :], pf_dz[:, columns])
            at = len(stores)
            wait(2 + at)
            total[part, :] = total[part, :] + value
            stores.append(pltpu.make_async_copy(total.at[part, :], out.at[part, :], out_sems.at[at]))
            stores[-1].start()
    for store in stores:
        store.wait()


def cut_kernel(place, *refs):
    ins, outs, held, (in_sems,) = refs[:5], refs[5:13], refs[13:18], refs[18:]
    sib_q_t, got, sib_qf_t, left, right = held
    width, rows = sib_q_t.shape
    halves = [pl.ds(0, 576), pl.ds(576, 576)]
    wait = fetch(
        [(ins[at], held[at]) for at in range(3)]
        + [(ins[at].at[part, :], held[at].at[part, :]) for at in (3, 4) for part in halves],
        in_sems,
    )
    wait(0)
    wait(1)
    for along_x, total, columns in ((True, left, pl.ds(0, SPLIT)), (False, right, pl.ds(SPLIT, width - SPLIT))):
        for at, part in enumerate(halves):
            value = dot(sib_q_t[part, :], got[pl.ds(0, rows), columns])
            if along_x and at == 0:
                wait(2)
            value = value + dot(sib_qf_t[part, :], got[pl.ds(rows, rows), columns])
            wait((3 if along_x else 5) + at)
            total[part, :] = total[part, :] + value

        def half(target, which):
            if along_x:
                return total[pl.ds(pl.multiple_of(288 * target + 144 * which, 8), 144), :]
            starts = [288 * (2 * which + block) + 72 * target for block in (0, 1)]
            return jnp.concatenate([total[pl.ds(pl.multiple_of(at, 8), 72), :] for at in starts], axis=0)

        me = place[0] if along_x else place[1]
        keep_1, send_1, keep_3, send_3 = outs[:4] if along_x else outs[4:]
        top, low = pl.ds(0, 144), pl.ds(144, 144)
        keep_1[top, :] = half(me, 0)
        keep_1[low, :] = half(me ^ 3, 0)
        send_1[top, :] = half(me ^ 1, 0).astype(BF16)
        send_1[low, :] = half(me ^ 2, 0).astype(BF16)
        keep_3[top, :] = half(me, 1)
        keep_3[low, :] = half(me ^ 1, 1)
        send_3[top, :] = half(me ^ 3, 1).astype(BF16)
        send_3[low, :] = half(me ^ 2, 1).astype(BF16)


def second_kernel(keep_1, got_1, keep_3, got_3, own, send_3, send_1):
    top, low = pl.ds(0, 144), pl.ds(144, 144)
    first = keep_1[...] + got_1[...].astype(F32)
    own[top, :] = first[:144]
    send_3[...] = first[144:]
    other = keep_3[...] + got_3[...].astype(F32)
    own[low, :] = other[:144]
    send_1[...] = other[144:]


def third_kernel(place, own, got_3, got_1, *rest):
    outs, total = rest[:4], rest[4]
    total[pl.ds(0, 144), :] = own[pl.ds(0, 144), :] + got_3[...]
    total[pl.ds(144, 144), :] = own[pl.ds(144, 144), :] + got_1[...]
    for j in range(4):
        outs[j][...] = total[pl.ds(pl.multiple_of(72 * (place[0] ^ j), 8), 72), :]


def z_pieces_kernel(place, *rest):
    left, right, outs, total, packed = rest[:4], rest[4:8], rest[8:12], rest[12], rest[13]
    total[:, :SPLIT] = left[0][...] + left[1][...] + left[2][...] + left[3][...]
    total[:, SPLIT:] = right[0][...] + right[1][...] + right[2][...] + right[3][...]
    for at in range(4):
        for tile in range(9):
            packed[at, 18 * tile : 18 * tile + 18, :] = total[18 * at : 18 * at + 18, 128 * tile : 128 * tile + 128]
    for j in range(4):
        outs[j][...] = packed[place[0] ^ j, 0:162, :]


def sum_kernel(a, b, c, d, total):
    total[...] = a[...] + b[...] + c[...] + d[...]


def last_kernel(place, a, b, mine, squares, total):
    total[...] = a[...] + b[...]

    def take(first):
        for tile in range(9):
            mine[9 * tile : 9 * tile + 9, :] = total[18 * tile + first : 18 * tile + first + 9, :]

    @pl.when(place[0] == 0)
    def _():
        take(0)

    @pl.when(place[0] != 0)
    def _():
        take(9)

    value = total[...]
    squares[...] = jnp.broadcast_to(jnp.sum(value * value, axis=0, keepdims=True), squares.shape)


def lanes_kernel(got, squares):
    lanes = jnp.sum(got[...], axis=0, keepdims=True) * 0.125
    squares[...] = jnp.broadcast_to(lanes, squares.shape)


def scale_kernel(rows, got, out):
    total = jnp.sum(jnp.sum(got[...], axis=0, keepdims=True), axis=1, keepdims=True) * 0.125
    entries = 2 * out.shape[1] * out.shape[1]
    spread = jnp.sqrt(total / entries + 1e-06)
    for tile in range(9):
        out[:, 128 * tile : 128 * tile + 128] = rows[9 * tile : 9 * tile + 9, :] / spread


def swap_all(value, bits):
    masks = [sum(1 << bit for at, bit in enumerate(bits) if k >> at & 1) for k in range(2 ** len(bits))]
    groups = [[d | mask for mask in masks] for d in range(lax.axis_size("dp")) if not d & masks[-1]]
    return lax.all_to_all(value, "dp", 0, 0, axis_index_groups=groups, tiled=True)


def per_device(img_feats, txt_feats, img_head, txt_head, log_temp, logit_bias, caption_row):
    me = lax.axis_index("dp")
    core, y, x, z = me & 1, (me >> 1) & 3, (me >> 3) & 3, me >> 5
    first = core == 0
    rows, width = img_feats.shape

    far_img = permute(img_feats, lambda d: d ^ (192 if d & 1 else 64))
    far_txt = permute(txt_feats, lambda d: d ^ (64 if d & 1 else 192))
    p = jnp.where(first, img_feats, txt_feats)
    q = jnp.where(first, txt_feats, img_feats)
    p_head = jnp.where(first, img_head, txt_head)
    q_head = jnp.where(first, txt_head, img_head)
    sib_q = sibling(q)

    temper = jnp.exp(log_temp)
    index = jnp.arange(rows, dtype=jnp.int32)
    match = jnp.where(first, caption_row, index)[:, None] == jnp.where(first, index, caption_row)[None, :]
    label_sign = jnp.where(match, 1.0, -1.0).astype(F32)

    p_unit, p_scale = embed(p, p_head)
    q_unit, q_scale = embed(q, q_head)
    p_low = p_unit.astype(BF16)
    q_low = q_unit.astype(BF16)
    slope = tile_slope(p_low, q_low, label_sign, temper, logit_bias)
    p_grad = dot(slope, q_low)
    q_grad = dot(slope.T, p_low)
    scalars = jnp.stack([temper, logit_bias])
    p_pair, q_pair = call(
        pairs_kernel,
        (p_grad, p_unit, p_scale, q_grad, q_unit, q_scale),
        (shape(2 * rows, width, BF16), shape(2 * rows, width, BF16)),
        1,
        limit=20,
    )
    sib_pair = sibling(q_pair)
    left, right, sib_q_t = call(
        early_kernel,
        (p, sib_q, p_pair),
        (shape(width, SPLIT, F32), shape(width, width - SPLIT, F32), shape(width, rows, BF16)),
        200 * rows * width * width,
        [pltpu.VMEM((width, 2 * rows), BF16)],
        limit=20,
    )
    left, right = call(
        other_early_kernel,
        (sib_q_t, sib_pair, left, right),
        (shape(width, SPLIT, F32), shape(width, width - SPLIT, F32)),
        1,
        (),
        {2: 0, 3: 1},
        limit=24,
    )
    far_img, far_txt, left, right, sib_q_t = lax.optimization_barrier(
        (far_img, far_txt, left, right, sib_q_t)
    )

    wide, low, thin = (pltpu.VMEM(dims, kind) for dims, kind in (
        ((rows, width), F32), ((rows, width), BF16), ((rows, 1), F32),
    ))
    head, tile = pltpu.VMEM((width, width), BF16), pltpu.VMEM((rows, rows), BF16)
    turned = pltpu.VMEM((width, rows), BF16)
    send, qf_t, pf_dz, pf_t = call(
        far_kernel,
        (scalars, jnp.stack([core, 0]), far_img, far_txt, p_head, q_head, q_low, q_unit, q_scale),
        (shape(2 * rows, width, BF16), shape(width, rows, BF16), shape(rows, width, BF16), shape(width, rows, BF16)),
        4 * rows * width * width + 12 * rows * rows * width,
        [
            pltpu.VMEM((2 * rows, width), BF16), turned, low, turned,
            low, low, head, head, low, wide, thin, wide, wide, thin, thin,
            low, low, tile, tile, pltpu.SemaphoreType.DMA((7,)), pltpu.SemaphoreType.DMA((8,)),
        ],
        limit=LIMIT,
        far_ins=range(9),
        far_outs=range(4),
    )
    got, sib_qf_t = sibling(send), sibling(qf_t)
    accumulators = [pltpu.VMEM((width, SPLIT), F32), pltpu.VMEM((width, width - SPLIT), F32)]
    left, right = call(
        near_kernel,
        (pf_t, pf_dz, left, right),
        (shape(width, SPLIT, F32), shape(width, width - SPLIT, F32)),
        2 * rows * width * width,
        [turned, low, *accumulators, pltpu.SemaphoreType.DMA((6,)), pltpu.SemaphoreType.DMA((4,))],
        limit=LIMIT,
        far_ins=range(4),
        far_outs=range(2),
    )

    kinds = (F32, BF16, F32, BF16)
    parts = call(
        cut_kernel,
        (jnp.stack([x, y]), sib_q_t, got, sib_qf_t, left, right),
        [shape(288, count, kind) for count in (SPLIT, width - SPLIT) for kind in kinds],
        4 * rows * width * width,
        [turned, pltpu.VMEM((2 * rows, width), BF16), turned, *accumulators, pltpu.SemaphoreType.DMA((7,))],
        limit=32,
        far_ins=range(1, 6),
    )

    def reduce(parts, along_x):
        keep_1, send_1, keep_3, send_3 = parts
        count = keep_1.shape[1]
        bit, other_bit, other = (3, 1, y) if along_x else (1, 3, x)
        got_1 = permute(send_1, lambda d: d ^ (1 << bit))
        got_3 = permute(send_3, lambda d: d ^ (3 << bit))
        own, send_3, send_1 = call(
            second_kernel,
            (keep_1, got_1, keep_3, got_3),
            (shape(288, count, F32), shape(144, count, F32), shape(144, count, F32)),
            288 * count,
            limit=8,
        )
        got_3 = permute(send_3, lambda d: d ^ (3 << bit))
        got_1 = permute(send_1, lambda d: d ^ (1 << bit))
        outs = call(
            third_kernel,
            (jnp.stack([other, 0]), own, got_3, got_1),
            [shape(72, count, F32)] * 4,
            288 * count,
            [pltpu.VMEM((288, count), F32)],
            limit=8,
        )
        return [outs[0]] + [permute(outs[j], lambda d, j=j: d ^ (j << other_bit)) for j in (1, 2, 3)]

    left = reduce(parts[:4], True)
    right = reduce(parts[4:], False)
    parts = call(
        z_pieces_kernel,
        (jnp.stack([z >> 1, 0]), *left, *right),
        [shape(162, 128, F32)] * 4,
        6 * 72 * width,
        [pltpu.VMEM((72, width), F32), pltpu.VMEM((4, 168, 128), F32)],
        limit=8,
    )
    parts = [parts[0]] + [permute(parts[j], lambda d, j=j: d ^ (j << 6)) for j in (1, 2, 3)]
    [part] = call(sum_kernel, parts, [shape(162, 128, F32)], 3 * 18 * width, limit=8)

    other = permute(part, lambda d: d ^ 32)
    total, squares = call(
        last_kernel,
        (jnp.stack([z & 1, 0]), part, other),
        (shape(81, 128, F32), shape(64, 128, F32)),
        10 * 18 * width,
        [pltpu.VMEM((162, 128), F32)],
        limit=8,
    )

    def owner(d):
        z, x, y, s = d >> 5, d >> 3 & 3, d >> 1 & 3, d & 1
        return (4 * s + x) << 5 | y << 3 | (z >> 1) << 1 | z & 1

    mine = permute(total, owner)
    [squares] = call(lanes_kernel, (swap_all(squares, (0, 6, 7)),), [shape(128, 128, F32)], 10000, limit=8)
    squares, mine = lax.optimization_barrier((squares, mine))
    got = swap_all(squares, (1, 2, 3, 4))
    [out] = call(scale_kernel, (mine, got), [shape(9, width, F32)], 10 * 9 * width, limit=8)
    return out


def solution(mesh):
    return jax.shard_map(
        per_device,
        mesh=mesh,
        in_specs=(P("dp", None), P("dp", None), P(), P(), P(), P(), P("dp")),
        out_specs=P("dp", None),
        check_vma=False,
    )
```

```python
import functools

import jax
import jax.numpy as jnp
from jax import lax
from jax.experimental import pallas as pl
from jax.experimental.pallas import tpu as pltpu
from jax.sharding import PartitionSpec as P

SPLIT = 640
LIMIT = 62
F32, BF16 = jnp.float32, jnp.bfloat16
VMEM = pl.BlockSpec(memory_space=pltpu.VMEM)
SMEM = pl.BlockSpec(memory_space=pltpu.SMEM)
HBM = pl.BlockSpec(memory_space=pltpu.HBM)


def permute(value, target):
    pairs = [(source, target(source)) for source in range(lax.axis_size("dp"))]
    return lax.ppermute(value, "dp", pairs)


def sibling(value):
    return permute(value, lambda d: d ^ 1)


def dot(a, b):
    return jnp.dot(a, b, preferred_element_type=F32)


def call(kernel, ins, outs, flops, scratch=(), aliases=None, limit=48, far_ins=(), far_outs=()):
    moved = sum(v.size * v.dtype.itemsize for v in [*ins, *outs])
    return pl.pallas_call(
        kernel,
        out_shape=outs,
        in_specs=[SMEM if v.size <= 8 else HBM if at in far_ins else VMEM for at, v in enumerate(ins)],
        out_specs=[HBM if at in far_outs else VMEM for at in range(len(outs))],
        scratch_shapes=scratch,
        input_output_aliases=aliases or {},
        cost_estimate=pl.CostEstimate(
            flops=flops, bytes_accessed=moved if flops > 1 else 1, transcendentals=0
        ),
        compiler_params=pltpu.CompilerParams(vmem_limit_bytes=limit * 2**20),
    )(*ins)


def shape(rows, columns, kind):
    return jax.ShapeDtypeStruct((rows, columns), kind)


def embed(features, head):
    projected = dot(features, head)
    scale = jnp.sqrt(jnp.sum(projected * projected, axis=-1, keepdims=True) + 1e-06)
    return (projected / scale, scale)


def tile_slope(left, right, label_sign, temper, offset):
    scores = temper * dot(left, right.T) + offset
    margin = label_sign * scores
    return (-label_sign * jax.nn.sigmoid(-margin) * temper).astype(BF16)


def project(grad, unit, inverse):
    inner = jnp.sum(unit * grad, axis=-1, keepdims=True)
    return (grad - unit * inner) * inverse


def pairs_kernel(p_grad, p_unit, p_scale, q_grad, q_unit, q_scale, p_pair, q_pair):
    rows = p_grad.shape[0]
    for grad, unit, scale, out in ((q_grad, q_unit, q_scale, q_pair), (p_grad, p_unit, p_scale, p_pair)):
        for at in range(0, rows, 128):
            part = pl.ds(at, 128)
            value = project(grad[part, :], unit[part, :], 1.0 / scale[part, :])
            high = value.astype(BF16)
            out[part, :] = high
            out[pl.ds(rows + at, 128), :] = (value - high.astype(F32)).astype(BF16)


def early_kernel(p, sib_q, p_pair, left, right, sib_q_t, p_twice):
    rows, width = p.shape
    turned = p[...].T
    p_twice[:, :rows] = turned
    p_twice[:, rows:] = turned
    sib_q_t[...] = sib_q[...].T
    for at in range(0, width, 576):
        part = pl.ds(at, 576)
        left[part, :] = dot(p_twice[part, :], p_pair[:, :SPLIT])
        right[part, :] = dot(p_twice[part, :], p_pair[:, SPLIT:])


def other_early_kernel(sib_q_t, sib_pair, left, right, left_out, right_out):
    width, rows = sib_q_t.shape
    for at in range(0, width, 576):
        part = pl.ds(at, 576)
        for before, out, columns in (
            (left, left_out, pl.ds(0, SPLIT)),
            (right, right_out, pl.ds(SPLIT, width - SPLIT)),
        ):
            out[part, :] = (
                before[part, :]
                + dot(sib_q_t[part, :], sib_pair[pl.ds(0, rows), columns])
                + dot(sib_q_t[part, :], sib_pair[pl.ds(rows, rows), columns])
            )


def far_kernel(
    scalars, place, far_img, far_txt, p_head_in, q_head_in, q_low_in, q_unit_in, q_scale_in,
    send_out, qf_t_out, pf_dz_out, pf_t_out,
    send, qf_t, pf_dz, pf_t, pf, qf, p_head, q_head, q_low, q_unit, q_scale, pf_unit, qf_unit, pf_inverse, qf_inverse,
    pf_low, qf_low, slope_a, slope_b, sems, out_sems,
):
    rows = pf.shape[0]
    step = 256
    first = place[0] == 0

    def copy(source, target, at):
        return pltpu.make_async_copy(source, target, sems.at[at])

    @pl.when(first)
    def _():
        copy(far_img, pf, 0).start()

    @pl.when(jnp.logical_not(first))
    def _():
        copy(far_txt, pf, 0).start()

    copies = [copy(p_head_in, p_head, 1)]
    copies[0].start()

    @pl.when(first)
    def _():
        copy(far_txt, qf, 2).start()

    @pl.when(jnp.logical_not(first))
    def _():
        copy(far_img, qf, 2).start()

    for at, (source, target) in enumerate(
        ((q_low_in, q_low), (q_head_in, q_head), (q_unit_in, q_unit), (q_scale_in, q_scale)), 3
    ):
        copies.append(copy(source, target, at))
        copies[-1].start()

    temper, offset = scalars[0], scalars[1]
    stores = []

    def store(source, target, *part):
        if part:
            source, target = source.at[part], target.at[part]
        stores.append(pltpu.make_async_copy(source, target, out_sems.at[len(stores)]))
        stores[-1].start()

    def embed_far(feats, head, unit, inverse, low):
        for at in range(0, rows, step):
            part = pl.ds(at, step)
            projected = dot(feats[part, :], head[...])
            length = jnp.sqrt(jnp.sum(projected * projected, axis=-1, keepdims=True) + 1e-06)
            inverse[part, :] = 1.0 / length
            there = projected * (1.0 / length)
            unit[part, :] = there
            low[part, :] = there.astype(BF16)

    def slopes(low, slope):
        for at in range(0, rows, step):
            part = pl.ds(at, step)
            raw = lax.dot_general(
                pf_low[part, :], low[...], (((1,), (1,)), ((), ())), preferred_element_type=F32
            )
            slope[part, :] = (jax.nn.sigmoid(temper * raw + offset) * temper).astype(BF16)

    copy(far_img, pf, 0).wait()
    copies[0].wait()
    embed_far(pf, p_head, pf_unit, pf_inverse, pf_low)
    pf_t[...] = pf[...].T
    store(pf_t, pf_t_out)
    for at in (1, 2, 3, 4):
        copies[at].wait()
    copy(far_txt, qf, 2).wait()
    qf_t[...] = qf[...].T
    store(qf_t, qf_t_out)
    slopes(q_low, slope_a)
    embed_far(qf, q_head, qf_unit, qf_inverse, qf_low)
    slopes(qf_low, slope_b)
    for at in range(0, rows, step):
        part = pl.ds(at, step)
        grad = dot(slope_a[:, part].T, pf_low[...])
        send[part, :] = project(grad, q_unit[part, :], 1.0 / q_scale[part, :]).astype(BF16)
        store(send, send_out, part)
        again = pl.ds(rows + at, step)
        grad = dot(slope_b[:, part].T, pf_low[...])
        send[again, :] = project(grad, qf_unit[part, :], qf_inverse[part, :]).astype(BF16)
        store(send, send_out, again)
        grad = dot(slope_a[part, :], q_low[...]) + dot(slope_b[part, :], qf_low[...])
        pf_dz[part, :] = project(grad, pf_unit[part, :], pf_inverse[part, :]).astype(BF16)
        store(pf_dz, pf_dz_out, part)
    for copy_out in stores:
        copy_out.wait()


def fetch(pairs, sems):
    copies = [pltpu.make_async_copy(*pair, sems.at[at]) for at, pair in enumerate(pairs)]
    for copy in copies:
        copy.start()
    return lambda at: copies[at].wait()


def near_kernel(*refs):
    ins, outs, held, (in_sems, out_sems) = refs[:4], refs[4:6], refs[6:10], refs[10:]
    pf_t, pf_dz, left, right = held
    width = pf_t.shape[0]
    halves = [pl.ds(0, 576), pl.ds(576, 576)]
    wait = fetch(
        [(ins[1], pf_dz), (ins[0], pf_t)]
        + [(ins[2 + which].at[part, :], held[2 + which].at[part, :]) for part in halves for which in (0, 1)],
        in_sems,
    )
    wait(0)
    wait(1)
    stores = []
    for part in halves:
        for total, out, columns in (
            (left, outs[0], pl.ds(0, SPLIT)),
            (right, outs[1], pl.ds(SPLIT, width - SPLIT)),
        ):
            value = dot(pf_t[part, :], pf_dz[:, columns])
            at = len(stores)
            wait(2 + at)
            total[part, :] = total[part, :] + value
            stores.append(pltpu.make_async_copy(total.at[part, :], out.at[part, :], out_sems.at[at]))
            stores[-1].start()
    for store in stores:
        store.wait()


def cut_kernel(place, *refs):
    ins, outs, held, (in_sems,) = refs[:5], refs[5:13], refs[13:17], refs[17:]
    both_t, got, left, right = held
    width = both_t.shape[0]
    rows = both_t.shape[1] // 2
    halves = [pl.ds(0, 576), pl.ds(576, 576)]
    wait = fetch(
        [(ins[0], both_t.at[:, pl.ds(0, rows)]), (ins[1], got), (ins[2], both_t.at[:, pl.ds(rows, rows)])]
        + [(ins[at].at[part, :], held[at - 1].at[part, :]) for at in (3, 4) for part in halves],
        in_sems,
    )
    for at in range(3):
        wait(at)
    for along_x, total, columns in ((True, left, pl.ds(0, SPLIT)), (False, right, pl.ds(SPLIT, width - SPLIT))):
        for at, part in enumerate(halves):
            value = dot(both_t[part, :], got[:, columns])
            wait((3 if along_x else 5) + at)
            total[part, :] = total[part, :] + value

        def half(target, which):
            if along_x:
                return total[pl.ds(pl.multiple_of(288 * target + 144 * which, 8), 144), :]
            starts = [288 * (2 * which + block) + 72 * target for block in (0, 1)]
            return jnp.concatenate([total[pl.ds(pl.multiple_of(at, 8), 72), :] for at in starts], axis=0)

        me = place[0] if along_x else place[1]
        keep_1, send_1, keep_3, send_3 = outs[:4] if along_x else outs[4:]
        top, low = pl.ds(0, 144), pl.ds(144, 144)
        keep_1[top, :] = half(me, 0)
        keep_1[low, :] = half(me ^ 3, 0)
        send_1[top, :] = half(me ^ 1, 0).astype(BF16)
        send_1[low, :] = half(me ^ 2, 0).astype(BF16)
        keep_3[top, :] = half(me, 1)
        keep_3[low, :] = half(me ^ 1, 1)
        send_3[top, :] = half(me ^ 3, 1).astype(BF16)
        send_3[low, :] = half(me ^ 2, 1).astype(BF16)


def second_kernel(keep_1, got_1, keep_3, got_3, own, send_3, send_1):
    top, low = pl.ds(0, 144), pl.ds(144, 144)
    first = keep_1[...] + got_1[...].astype(F32)
    own[top, :] = first[:144]
    send_3[...] = first[144:]
    other = keep_3[...] + got_3[...].astype(F32)
    own[low, :] = other[:144]
    send_1[...] = other[144:]


def third_kernel(place, own, got_3, got_1, *rest):
    outs, total = rest[:4], rest[4]
    total[pl.ds(0, 144), :] = own[pl.ds(0, 144), :] + got_3[...]
    total[pl.ds(144, 144), :] = own[pl.ds(144, 144), :] + got_1[...]
    for j in range(4):
        outs[j][...] = total[pl.ds(pl.multiple_of(72 * (place[0] ^ j), 8), 72), :]


def z_pieces_kernel(place, *rest):
    left, right, outs, total, packed = rest[:4], rest[4:8], rest[8:12], rest[12], rest[13]
    total[:, :SPLIT] = left[0][...] + left[1][...] + left[2][...] + left[3][...]
    total[:, SPLIT:] = right[0][...] + right[1][...] + right[2][...] + right[3][...]
    for at in range(4):
        for tile in range(9):
            packed[at, 18 * tile : 18 * tile + 18, :] = total[18 * at : 18 * at + 18, 128 * tile : 128 * tile + 128]
    for j in range(4):
        outs[j][...] = packed[place[0] ^ j, 0:162, :]


def sum_kernel(a, b, c, d, total):
    total[...] = a[...] + b[...] + c[...] + d[...]


def last_kernel(place, a, b, mine, squares, total):
    total[...] = a[...] + b[...]

    def take(first):
        for tile in range(9):
            mine[9 * tile : 9 * tile + 9, :] = total[18 * tile + first : 18 * tile + first + 9, :]

    @pl.when(place[0] == 0)
    def _():
        take(0)

    @pl.when(place[0] != 0)
    def _():
        take(9)

    value = total[...]
    squares[...] = jnp.broadcast_to(jnp.sum(value * value, axis=0, keepdims=True), squares.shape)


def lanes_kernel(got, squares):
    lanes = jnp.sum(got[...], axis=0, keepdims=True) * 0.125
    squares[...] = jnp.broadcast_to(lanes, squares.shape)


def scale_kernel(rows, got, out):
    total = jnp.sum(jnp.sum(got[...], axis=0, keepdims=True), axis=1, keepdims=True) * 0.125
    entries = 2 * out.shape[1] * out.shape[1]
    spread = jnp.sqrt(total / entries + 1e-06)
    for tile in range(9):
        out[:, 128 * tile : 128 * tile + 128] = rows[9 * tile : 9 * tile + 9, :] / spread


def swap_all(value, bits):
    masks = [sum(1 << bit for at, bit in enumerate(bits) if k >> at & 1) for k in range(2 ** len(bits))]
    groups = [[d | mask for mask in masks] for d in range(lax.axis_size("dp")) if not d & masks[-1]]
    return lax.all_to_all(value, "dp", 0, 0, axis_index_groups=groups, tiled=True)


def per_device(img_feats, txt_feats, img_head, txt_head, log_temp, logit_bias, caption_row):
    me = lax.axis_index("dp")
    core, y, x, z = me & 1, (me >> 1) & 3, (me >> 3) & 3, me >> 5
    first = core == 0
    rows, width = img_feats.shape

    far_img = permute(img_feats, lambda d: d ^ (192 if d & 1 else 64))
    far_txt = permute(txt_feats, lambda d: d ^ (64 if d & 1 else 192))
    p = jnp.where(first, img_feats, txt_feats)
    q = jnp.where(first, txt_feats, img_feats)
    p_head = jnp.where(first, img_head, txt_head)
    q_head = jnp.where(first, txt_head, img_head)
    sib_q = sibling(q)

    temper = jnp.exp(log_temp)
    index = jnp.arange(rows, dtype=jnp.int32)
    match = jnp.where(first, caption_row, index)[:, None] == jnp.where(first, index, caption_row)[None, :]
    label_sign = jnp.where(match, 1.0, -1.0).astype(F32)

    p_unit, p_scale = embed(p, p_head)
    q_unit, q_scale = embed(q, q_head)
    p_low = p_unit.astype(BF16)
    q_low = q_unit.astype(BF16)
    slope = tile_slope(p_low, q_low, label_sign, temper, logit_bias)
    p_grad = dot(slope, q_low)
    q_grad = dot(slope.T, p_low)
    scalars = jnp.stack([temper, logit_bias])
    p_pair, q_pair = call(
        pairs_kernel,
        (p_grad, p_unit, p_scale, q_grad, q_unit, q_scale),
        (shape(2 * rows, width, BF16), shape(2 * rows, width, BF16)),
        1,
        limit=20,
    )
    sib_pair = sibling(q_pair)
    left, right, sib_q_t = call(
        early_kernel,
        (p, sib_q, p_pair),
        (shape(width, SPLIT, F32), shape(width, width - SPLIT, F32), shape(width, rows, BF16)),
        200 * rows * width * width,
        [pltpu.VMEM((width, 2 * rows), BF16)],
        limit=20,
    )
    left, right = call(
        other_early_kernel,
        (sib_q_t, sib_pair, left, right),
        (shape(width, SPLIT, F32), shape(width, width - SPLIT, F32)),
        1,
        (),
        {2: 0, 3: 1},
        limit=24,
    )
    far_img, far_txt, left, right, sib_q_t = lax.optimization_barrier(
        (far_img, far_txt, left, right, sib_q_t)
    )

    wide, low, thin = (pltpu.VMEM(dims, kind) for dims, kind in (
        ((rows, width), F32), ((rows, width), BF16), ((rows, 1), F32),
    ))
    head, tile = pltpu.VMEM((width, width), BF16), pltpu.VMEM((rows, rows), BF16)
    turned = pltpu.VMEM((width, rows), BF16)
    send, qf_t, pf_dz, pf_t = call(
        far_kernel,
        (scalars, jnp.stack([core, 0]), far_img, far_txt, p_head, q_head, q_low, q_unit, q_scale),
        (shape(2 * rows, width, BF16), shape(width, rows, BF16), shape(rows, width, BF16), shape(width, rows, BF16)),
        4 * rows * width * width + 12 * rows * rows * width,
        [
            pltpu.VMEM((2 * rows, width), BF16), turned, low, turned,
            low, low, head, head, low, wide, thin, wide, wide, thin, thin,
            low, low, tile, tile, pltpu.SemaphoreType.DMA((7,)), pltpu.SemaphoreType.DMA((8,)),
        ],
        limit=LIMIT,
        far_ins=range(9),
        far_outs=range(4),
    )
    got, sib_qf_t = sibling(send), sibling(qf_t)
    accumulators = [pltpu.VMEM((width, SPLIT), F32), pltpu.VMEM((width, width - SPLIT), F32)]
    left, right = call(
        near_kernel,
        (pf_t, pf_dz, left, right),
        (shape(width, SPLIT, F32), shape(width, width - SPLIT, F32)),
        2 * rows * width * width,
        [turned, low, *accumulators, pltpu.SemaphoreType.DMA((6,)), pltpu.SemaphoreType.DMA((4,))],
        limit=LIMIT,
        far_ins=range(4),
        far_outs=range(2),
    )

    kinds = (F32, BF16, F32, BF16)
    parts = call(
        cut_kernel,
        (jnp.stack([x, y]), sib_q_t, got, sib_qf_t, left, right),
        [shape(288, count, kind) for count in (SPLIT, width - SPLIT) for kind in kinds],
        4 * rows * width * width,
        [
            pltpu.VMEM((width, 2 * rows), BF16), pltpu.VMEM((2 * rows, width), BF16), *accumulators,
            pltpu.SemaphoreType.DMA((7,)),
        ],
        limit=32,
        far_ins=range(1, 6),
    )

    def first_step(parts, bit):
        keep_1, send_1, keep_3, send_3 = parts
        return keep_1, permute(send_1, lambda d: d ^ (1 << bit)), keep_3, permute(send_3, lambda d: d ^ (3 << bit))

    def second_step(parts):
        count = parts[0].shape[1]
        return call(
            second_kernel,
            parts,
            (shape(288, count, F32), shape(144, count, F32), shape(144, count, F32)),
            288 * count,
            limit=8,
        )

    def last_step(parts, bit, other, other_bit):
        own, send_3, send_1 = parts
        count = own.shape[1]
        got_3 = permute(send_3, lambda d: d ^ (3 << bit))
        got_1 = permute(send_1, lambda d: d ^ (1 << bit))
        outs = call(
            third_kernel,
            (jnp.stack([other, 0]), own, got_3, got_1),
            [shape(72, count, F32)] * 4,
            288 * count,
            [pltpu.VMEM((288, count), F32)],
            limit=8,
        )
        return outs[0], [permute(outs[j], lambda d, j=j: d ^ (j << other_bit)) for j in (1, 2, 3)]

    own, *left = second_step(first_step(parts[:4], 3))
    keep, *right = first_step(parts[4:], 1)
    own, keep = lax.optimization_barrier((own, keep))
    left, right = (own, *left), second_step((keep, *right))
    own, left = last_step(left, 3, y, 1)
    own, keep = lax.optimization_barrier((own, right[0]))
    left = [own, *left]
    own, right = last_step((keep, *right[1:]), 1, x, 3)
    right = [own, *right]
    parts = call(
        z_pieces_kernel,
        (jnp.stack([z >> 1, 0]), *left, *right),
        [shape(162, 128, F32)] * 4,
        6 * 72 * width,
        [pltpu.VMEM((72, width), F32), pltpu.VMEM((4, 168, 128), F32)],
        limit=8,
    )
    parts = [parts[0]] + [permute(parts[j], lambda d, j=j: d ^ (j << 6)) for j in (1, 2, 3)]
    [part] = call(sum_kernel, parts, [shape(162, 128, F32)], 3 * 18 * width, limit=8)

    other = permute(part, lambda d: d ^ 32)
    total, squares = call(
        last_kernel,
        (jnp.stack([z & 1, 0]), part, other),
        (shape(81, 128, F32), shape(64, 128, F32)),
        10 * 18 * width,
        [pltpu.VMEM((162, 128), F32)],
        limit=8,
    )

    def owner(d):
        z, x, y, s = d >> 5, d >> 3 & 3, d >> 1 & 3, d & 1
        return (4 * s + x) << 5 | y << 3 | (z >> 1) << 1 | z & 1

    mine = permute(total, owner)
    [squares] = call(lanes_kernel, (swap_all(squares, (0, 6, 7)),), [shape(128, 128, F32)], 10000, limit=8)
    squares, mine = lax.optimization_barrier((squares, mine))
    got = swap_all(squares, (1, 2, 3, 4))
    [out] = call(scale_kernel, (mine, got), [shape(9, width, F32)], 10 * 9 * width, limit=8)
    return out


def solution(mesh):
    return jax.shard_map(
        per_device,
        mesh=mesh,
        in_specs=(P("dp", None), P("dp", None), P(), P(), P(), P(), P("dp")),
        out_specs=P("dp", None),
        check_vma=False,
    )
```

```python
import functools

import jax
import jax.numpy as jnp
from jax import lax
from jax.experimental import pallas as pl
from jax.experimental.pallas import tpu as pltpu
from jax.sharding import PartitionSpec as P

SPLIT = 640
LIMIT = 62
F32, BF16 = jnp.float32, jnp.bfloat16
VMEM = pl.BlockSpec(memory_space=pltpu.VMEM)
SMEM = pl.BlockSpec(memory_space=pltpu.SMEM)
HBM = pl.BlockSpec(memory_space=pltpu.HBM)


def permute(value, target):
    pairs = [(source, target(source)) for source in range(lax.axis_size("dp"))]
    return lax.ppermute(value, "dp", pairs)


def sibling(value):
    return permute(value, lambda d: d ^ 1)


def dot(a, b):
    return jnp.dot(a, b, preferred_element_type=F32)


def call(kernel, ins, outs, flops, scratch=(), aliases=None, limit=48, far_ins=(), far_outs=()):
    moved = sum(v.size * v.dtype.itemsize for v in [*ins, *outs])
    return pl.pallas_call(
        kernel,
        out_shape=outs,
        in_specs=[SMEM if v.size <= 8 else HBM if at in far_ins else VMEM for at, v in enumerate(ins)],
        out_specs=[HBM if at in far_outs else VMEM for at in range(len(outs))],
        scratch_shapes=scratch,
        input_output_aliases=aliases or {},
        cost_estimate=pl.CostEstimate(
            flops=flops, bytes_accessed=moved if flops > 1 else 1, transcendentals=0
        ),
        compiler_params=pltpu.CompilerParams(vmem_limit_bytes=limit * 2**20),
    )(*ins)


def shape(rows, columns, kind):
    return jax.ShapeDtypeStruct((rows, columns), kind)


def embed(features, head):
    projected = dot(features, head)
    scale = jnp.sqrt(jnp.sum(projected * projected, axis=-1, keepdims=True) + 1e-06)
    return (projected / scale, scale)


def tile_slope(left, right, label_sign, temper, offset):
    scores = temper * dot(left, right.T) + offset
    margin = label_sign * scores
    return (-label_sign * jax.nn.sigmoid(-margin) * temper).astype(BF16)


def project(grad, unit, inverse):
    inner = jnp.sum(unit * grad, axis=-1, keepdims=True)
    return (grad - unit * inner) * inverse


def pairs_kernel(p_grad, p_unit, p_scale, q_grad, q_unit, q_scale, p_pair, q_pair):
    rows = p_grad.shape[0]
    for grad, unit, scale, out in ((q_grad, q_unit, q_scale, q_pair), (p_grad, p_unit, p_scale, p_pair)):
        for at in range(0, rows, 128):
            part = pl.ds(at, 128)
            value = project(grad[part, :], unit[part, :], 1.0 / scale[part, :])
            high = value.astype(BF16)
            out[part, :] = high
            out[pl.ds(rows + at, 128), :] = (value - high.astype(F32)).astype(BF16)


def early_kernel(p, sib_q, p_pair, left, right, sib_q_t, p_twice):
    rows, width = p.shape
    turned = p[...].T
    p_twice[:, :rows] = turned
    p_twice[:, rows:] = turned
    sib_q_t[...] = sib_q[...].T
    for at in range(0, width, 576):
        part = pl.ds(at, 576)
        left[part, :] = dot(p_twice[part, :], p_pair[:, :SPLIT])
        right[part, :] = dot(p_twice[part, :], p_pair[:, SPLIT:])


def other_early_kernel(sib_q_t, sib_pair, left, right, left_out, right_out):
    width, rows = sib_q_t.shape
    for at in range(0, width, 576):
        part = pl.ds(at, 576)
        for before, out, columns in (
            (left, left_out, pl.ds(0, SPLIT)),
            (right, right_out, pl.ds(SPLIT, width - SPLIT)),
        ):
            out[part, :] = (
                before[part, :]
                + dot(sib_q_t[part, :], sib_pair[pl.ds(0, rows), columns])
                + dot(sib_q_t[part, :], sib_pair[pl.ds(rows, rows), columns])
            )


def far_kernel(
    scalars, place, far_img, far_txt, p_head_in, q_head_in, q_low_in, q_unit_in, q_scale_in,
    send_out, qf_t_out, pf_dz_out, pf_t_out,
    send, qf_t, pf_dz, pf_t, pf, qf, p_head, q_head, q_low, q_unit, q_scale, pf_unit, qf_unit, pf_inverse, qf_inverse,
    pf_low, qf_low, slope_a, slope_b, sems, out_sems,
):
    rows = pf.shape[0]
    step = 256
    first = place[0] == 0

    def copy(source, target, at):
        return pltpu.make_async_copy(source, target, sems.at[at])

    @pl.when(first)
    def _():
        copy(far_img, pf, 0).start()

    @pl.when(jnp.logical_not(first))
    def _():
        copy(far_txt, pf, 0).start()

    copies = [copy(p_head_in, p_head, 1)]
    copies[0].start()

    @pl.when(first)
    def _():
        copy(far_txt, qf, 2).start()

    @pl.when(jnp.logical_not(first))
    def _():
        copy(far_img, qf, 2).start()

    for at, (source, target) in enumerate(
        ((q_low_in, q_low), (q_head_in, q_head), (q_unit_in, q_unit), (q_scale_in, q_scale)), 3
    ):
        copies.append(copy(source, target, at))
        copies[-1].start()

    temper, offset = scalars[0], scalars[1]
    stores = []

    def store(source, target, *part):
        if part:
            source, target = source.at[part], target.at[part]
        stores.append(pltpu.make_async_copy(source, target, out_sems.at[len(stores)]))
        stores[-1].start()

    def embed_far(feats, head, unit, inverse, low):
        for at in range(0, rows, step):
            part = pl.ds(at, step)
            projected = dot(feats[part, :], head[...])
            length = jnp.sqrt(jnp.sum(projected * projected, axis=-1, keepdims=True) + 1e-06)
            inverse[part, :] = 1.0 / length
            there = projected * (1.0 / length)
            unit[part, :] = there
            low[part, :] = there.astype(BF16)

    def slopes(low, slope):
        for at in range(0, rows, step):
            part = pl.ds(at, step)
            raw = lax.dot_general(
                pf_low[part, :], low[...], (((1,), (1,)), ((), ())), preferred_element_type=F32
            )
            slope[part, :] = (jax.nn.sigmoid(temper * raw + offset) * temper).astype(BF16)

    copy(far_img, pf, 0).wait()
    copies[0].wait()
    embed_far(pf, p_head, pf_unit, pf_inverse, pf_low)
    pf_t[...] = pf[...].T
    store(pf_t, pf_t_out)
    for at in (1, 2, 3, 4):
        copies[at].wait()
    copy(far_txt, qf, 2).wait()
    qf_t[...] = qf[...].T
    store(qf_t, qf_t_out)
    slopes(q_low, slope_a)
    embed_far(qf, q_head, qf_unit, qf_inverse, qf_low)
    slopes(qf_low, slope_b)
    for at in range(0, rows, step):
        part = pl.ds(at, step)
        grad = dot(slope_a[:, part].T, pf_low[...])
        send[part, :] = project(grad, q_unit[part, :], 1.0 / q_scale[part, :]).astype(BF16)
        store(send, send_out, part)
        again = pl.ds(rows + at, step)
        grad = dot(slope_b[:, part].T, pf_low[...])
        send[again, :] = project(grad, qf_unit[part, :], qf_inverse[part, :]).astype(BF16)
        store(send, send_out, again)
        grad = dot(slope_a[part, :], q_low[...]) + dot(slope_b[part, :], qf_low[...])
        pf_dz[part, :] = project(grad, pf_unit[part, :], pf_inverse[part, :]).astype(BF16)
        store(pf_dz, pf_dz_out, part)
    for copy_out in stores:
        copy_out.wait()


def fetch(pairs, sems):
    copies = [pltpu.make_async_copy(*pair, sems.at[at]) for at, pair in enumerate(pairs)]
    for copy in copies:
        copy.start()
    return lambda at: copies[at].wait()


def near_kernel(*refs):
    ins, outs, held, (in_sems, out_sems) = refs[:4], refs[4:6], refs[6:10], refs[10:]
    pf_t, pf_dz, left, right = held
    width = pf_t.shape[0]
    halves = [pl.ds(0, 576), pl.ds(576, 576)]
    wait = fetch(
        [(ins[1], pf_dz), (ins[0], pf_t)]
        + [(ins[2 + which].at[part, :], held[2 + which].at[part, :]) for part in halves for which in (0, 1)],
        in_sems,
    )
    wait(0)
    wait(1)
    stores = []
    for part in halves:
        for total, out, columns in (
            (left, outs[0], pl.ds(0, SPLIT)),
            (right, outs[1], pl.ds(SPLIT, width - SPLIT)),
        ):
            value = dot(pf_t[part, :], pf_dz[:, columns])
            at = len(stores)
            wait(2 + at)
            total[part, :] = total[part, :] + value
            stores.append(pltpu.make_async_copy(total.at[part, :], out.at[part, :], out_sems.at[at]))
            stores[-1].start()
    for store in stores:
        store.wait()


def cut_kernel(first, along_x, place, *refs):
    ins, (keep_1, send_1, keep_3, send_3), (both_t, got, total, in_sems) = refs[:4], refs[4:8], refs[8:]
    width, count = total.shape
    rows = both_t.shape[1] // 2
    halves = [pl.ds(0, 576), pl.ds(576, 576)]
    wait = fetch(
        [
            (ins[0], both_t.at[:, pl.ds(0, rows)]), (ins[1].at[:, pl.ds(first, count)], got),
            (ins[2], both_t.at[:, pl.ds(rows, rows)]),
        ]
        + [(ins[3].at[part, :], total.at[part, :]) for part in halves],
        in_sems,
    )
    for at in range(3):
        wait(at)
    for at, part in enumerate(halves):
        value = dot(both_t[part, :], got[...])
        wait(3 + at)
        total[part, :] = total[part, :] + value

    def half(target, which):
        if along_x:
            return total[pl.ds(pl.multiple_of(288 * target + 144 * which, 8), 144), :]
        starts = [288 * (2 * which + block) + 72 * target for block in (0, 1)]
        return jnp.concatenate([total[pl.ds(pl.multiple_of(at, 8), 72), :] for at in starts], axis=0)

    me = place[0]
    top, low = pl.ds(0, 144), pl.ds(144, 144)
    keep_1[top, :] = half(me, 0)
    keep_1[low, :] = half(me ^ 3, 0)
    send_1[top, :] = half(me ^ 1, 0).astype(BF16)
    send_1[low, :] = half(me ^ 2, 0).astype(BF16)
    keep_3[top, :] = half(me, 1)
    keep_3[low, :] = half(me ^ 1, 1)
    send_3[top, :] = half(me ^ 3, 1).astype(BF16)
    send_3[low, :] = half(me ^ 2, 1).astype(BF16)


def second_kernel(keep_1, got_1, keep_3, got_3, own, send_3, send_1):
    top, low = pl.ds(0, 144), pl.ds(144, 144)
    first = keep_1[...] + got_1[...].astype(F32)
    own[top, :] = first[:144]
    send_3[...] = first[144:]
    other = keep_3[...] + got_3[...].astype(F32)
    own[low, :] = other[:144]
    send_1[...] = other[144:]


def third_kernel(place, own, got_3, got_1, *rest):
    outs, total = rest[:4], rest[4]
    total[pl.ds(0, 144), :] = own[pl.ds(0, 144), :] + got_3[...]
    total[pl.ds(144, 144), :] = own[pl.ds(144, 144), :] + got_1[...]
    for j in range(4):
        outs[j][...] = total[pl.ds(pl.multiple_of(72 * (place[0] ^ j), 8), 72), :]


def z_pieces_kernel(place, *rest):
    left, right, outs, total, packed = rest[:4], rest[4:8], rest[8:12], rest[12], rest[13]
    total[:, :SPLIT] = left[0][...] + left[1][...] + left[2][...] + left[3][...]
    total[:, SPLIT:] = right[0][...] + right[1][...] + right[2][...] + right[3][...]
    for at in range(4):
        for tile in range(9):
            packed[at, 18 * tile : 18 * tile + 18, :] = total[18 * at : 18 * at + 18, 128 * tile : 128 * tile + 128]
    for j in range(4):
        outs[j][...] = packed[place[0] ^ j, 0:162, :]


def sum_kernel(a, b, c, d, total):
    total[...] = a[...] + b[...] + c[...] + d[...]


def last_kernel(place, a, b, mine, more, squares, total):
    total[...] = a[...] + b[...]

    def take(first):
        for tile in range(9):
            out, at = (mine, tile) if tile < 5 else (more, tile - 5)
            out[9 * at : 9 * at + 9, :] = total[18 * tile + first : 18 * tile + first + 9, :]

    @pl.when(place[0] == 0)
    def _():
        take(0)

    @pl.when(place[0] != 0)
    def _():
        take(9)

    value = total[...]
    squares[...] = jnp.broadcast_to(jnp.sum(value * value, axis=0, keepdims=True), squares.shape)


def lanes_kernel(got, squares):
    lanes = jnp.sum(got[...], axis=0, keepdims=True) * 0.125
    squares[...] = jnp.broadcast_to(lanes, squares.shape)


def scale_kernel(rows, more, got, out):
    total = jnp.sum(jnp.sum(got[...], axis=0, keepdims=True), axis=1, keepdims=True) * 0.125
    entries = 2 * out.shape[1] * out.shape[1]
    spread = jnp.sqrt(total / entries + 1e-06)
    for tile in range(9):
        source, at = (rows, tile) if tile < 5 else (more, tile - 5)
        out[:, 128 * tile : 128 * tile + 128] = source[9 * at : 9 * at + 9, :] / spread


def swap_all(value, bits):
    masks = [sum(1 << bit for at, bit in enumerate(bits) if k >> at & 1) for k in range(2 ** len(bits))]
    groups = [[d | mask for mask in masks] for d in range(lax.axis_size("dp")) if not d & masks[-1]]
    return lax.all_to_all(value, "dp", 0, 0, axis_index_groups=groups, tiled=True)


def per_device(img_feats, txt_feats, img_head, txt_head, log_temp, logit_bias, caption_row):
    me = lax.axis_index("dp")
    core, y, x, z = me & 1, (me >> 1) & 3, (me >> 3) & 3, me >> 5
    first = core == 0
    rows, width = img_feats.shape

    far_img = permute(img_feats, lambda d: d ^ (192 if d & 1 else 64))
    far_txt = permute(txt_feats, lambda d: d ^ (64 if d & 1 else 192))
    p = jnp.where(first, img_feats, txt_feats)
    q = jnp.where(first, txt_feats, img_feats)
    p_head = jnp.where(first, img_head, txt_head)
    q_head = jnp.where(first, txt_head, img_head)
    sib_q = sibling(q)

    temper = jnp.exp(log_temp)
    index = jnp.arange(rows, dtype=jnp.int32)
    match = jnp.where(first, caption_row, index)[:, None] == jnp.where(first, index, caption_row)[None, :]
    label_sign = jnp.where(match, 1.0, -1.0).astype(F32)

    p_unit, p_scale = embed(p, p_head)
    q_unit, q_scale = embed(q, q_head)
    p_low = p_unit.astype(BF16)
    q_low = q_unit.astype(BF16)
    slope = tile_slope(p_low, q_low, label_sign, temper, logit_bias)
    p_grad = dot(slope, q_low)
    q_grad = dot(slope.T, p_low)
    scalars = jnp.stack([temper, logit_bias])
    p_pair, q_pair = call(
        pairs_kernel,
        (p_grad, p_unit, p_scale, q_grad, q_unit, q_scale),
        (shape(2 * rows, width, BF16), shape(2 * rows, width, BF16)),
        1,
        limit=20,
    )
    sib_pair = sibling(q_pair)
    left, right, sib_q_t = call(
        early_kernel,
        (p, sib_q, p_pair),
        (shape(width, SPLIT, F32), shape(width, width - SPLIT, F32), shape(width, rows, BF16)),
        200 * rows * width * width,
        [pltpu.VMEM((width, 2 * rows), BF16)],
        limit=20,
    )
    left, right = call(
        other_early_kernel,
        (sib_q_t, sib_pair, left, right),
        (shape(width, SPLIT, F32), shape(width, width - SPLIT, F32)),
        1,
        (),
        {2: 0, 3: 1},
        limit=24,
    )
    far_img, far_txt, left, right, sib_q_t = lax.optimization_barrier(
        (far_img, far_txt, left, right, sib_q_t)
    )

    wide, low, thin = (pltpu.VMEM(dims, kind) for dims, kind in (
        ((rows, width), F32), ((rows, width), BF16), ((rows, 1), F32),
    ))
    head, tile = pltpu.VMEM((width, width), BF16), pltpu.VMEM((rows, rows), BF16)
    turned = pltpu.VMEM((width, rows), BF16)
    send, qf_t, pf_dz, pf_t = call(
        far_kernel,
        (scalars, jnp.stack([core, 0]), far_img, far_txt, p_head, q_head, q_low, q_unit, q_scale),
        (shape(2 * rows, width, BF16), shape(width, rows, BF16), shape(rows, width, BF16), shape(width, rows, BF16)),
        4 * rows * width * width + 12 * rows * rows * width,
        [
            pltpu.VMEM((2 * rows, width), BF16), turned, low, turned,
            low, low, head, head, low, wide, thin, wide, wide, thin, thin,
            low, low, tile, tile, pltpu.SemaphoreType.DMA((7,)), pltpu.SemaphoreType.DMA((8,)),
        ],
        limit=LIMIT,
        far_ins=range(9),
        far_outs=range(4),
    )
    got, sib_qf_t = sibling(send), sibling(qf_t)
    accumulators = [pltpu.VMEM((width, SPLIT), F32), pltpu.VMEM((width, width - SPLIT), F32)]
    left, right = call(
        near_kernel,
        (pf_t, pf_dz, left, right),
        (shape(width, SPLIT, F32), shape(width, width - SPLIT, F32)),
        2 * rows * width * width,
        [turned, low, *accumulators, pltpu.SemaphoreType.DMA((6,)), pltpu.SemaphoreType.DMA((4,))],
        limit=LIMIT,
        far_ins=range(4),
        far_outs=range(2),
    )

    def cut(first, along_x, place, head_grad):
        count = head_grad.shape[1]
        return call(
            functools.partial(cut_kernel, first, along_x),
            (jnp.stack([place, 0]), sib_q_t, got, sib_qf_t, head_grad),
            (shape(288, count, F32), shape(288, count, BF16)) * 2,
            4 * rows * width * count,
            [
                pltpu.VMEM((width, 2 * rows), BF16), pltpu.VMEM((2 * rows, count), BF16),
                pltpu.VMEM((width, count), F32), pltpu.SemaphoreType.DMA((5,)),
            ],
            limit=24,
            far_ins=range(1, 5),
        )

    def first_step(parts, bit):
        keep_1, send_1, keep_3, send_3 = parts
        return keep_1, permute(send_1, lambda d: d ^ (1 << bit)), keep_3, permute(send_3, lambda d: d ^ (3 << bit))

    def second_step(parts):
        count = parts[0].shape[1]
        return call(
            second_kernel,
            parts,
            (shape(288, count, F32), shape(144, count, F32), shape(144, count, F32)),
            288 * count,
            limit=8,
        )

    def last_step(parts, bit, other, other_bit):
        own, send_3, send_1 = parts
        count = own.shape[1]
        got_3 = permute(send_3, lambda d: d ^ (3 << bit))
        got_1 = permute(send_1, lambda d: d ^ (1 << bit))
        outs = call(
            third_kernel,
            (jnp.stack([other, 0]), own, got_3, got_1),
            [shape(72, count, F32)] * 4,
            288 * count,
            [pltpu.VMEM((288, count), F32)],
            limit=8,
        )
        return outs[0], [permute(outs[j], lambda d, j=j: d ^ (j << other_bit)) for j in (1, 2, 3)]

    own, *left = second_step(first_step(cut(0, True, x, left), 3))
    keep, *right = first_step(cut(SPLIT, False, y, right), 1)
    own, keep = lax.optimization_barrier((own, keep))
    left, right = (own, *left), second_step((keep, *right))
    own, left = last_step(left, 3, y, 1)
    own, keep = lax.optimization_barrier((own, right[0]))
    left = [own, *left]
    own, right = last_step((keep, *right[1:]), 1, x, 3)
    right = [own, *right]
    parts = call(
        z_pieces_kernel,
        (jnp.stack([z >> 1, 0]), *left, *right),
        [shape(162, 128, F32)] * 4,
        6 * 72 * width,
        [pltpu.VMEM((72, width), F32), pltpu.VMEM((4, 168, 128), F32)],
        limit=8,
    )
    parts = [parts[0]] + [permute(parts[j], lambda d, j=j: d ^ (j << 6)) for j in (1, 2, 3)]
    [part] = call(sum_kernel, parts, [shape(162, 128, F32)], 3 * 18 * width, limit=8)

    other = permute(part, lambda d: d ^ 32)
    total, more, squares = call(
        last_kernel,
        (jnp.stack([z & 1, 0]), part, other),
        (shape(45, 128, F32), shape(36, 128, F32), shape(64, 128, F32)),
        10 * 18 * width,
        [pltpu.VMEM((162, 128), F32)],
        limit=8,
    )

    def owner(d):
        z, x, y, s = d >> 5, d >> 3 & 3, d >> 1 & 3, d & 1
        return (4 * s + x) << 5 | y << 3 | (z >> 1) << 1 | z & 1

    mine = permute(total, owner)
    [squares] = call(lanes_kernel, (swap_all(squares, (0, 6, 7)),), [shape(128, 128, F32)], 10000, limit=8)
    squares, mine = lax.optimization_barrier((squares, mine))
    got = swap_all(squares, (1, 2, 3, 4))
    more = permute(more, owner)
    [out] = call(scale_kernel, (mine, more, got), [shape(9, width, F32)], 10 * 9 * width, limit=8)
    return out


def solution(mesh):
    return jax.shard_map(
        per_device,
        mesh=mesh,
        in_specs=(P("dp", None), P("dp", None), P(), P(), P(), P(), P("dp")),
        out_specs=P("dp", None),
        check_vma=False,
    )
```

```python
import functools

import jax
import jax.numpy as jnp
from jax import lax
from jax.experimental import pallas as pl
from jax.experimental.pallas import tpu as pltpu
from jax.sharding import PartitionSpec as P

SPLIT = 640
LIMIT = 62
F32, BF16 = jnp.float32, jnp.bfloat16
VMEM = pl.BlockSpec(memory_space=pltpu.VMEM)
SMEM = pl.BlockSpec(memory_space=pltpu.SMEM)
HBM = pl.BlockSpec(memory_space=pltpu.HBM)


def permute(value, target):
    pairs = [(source, target(source)) for source in range(lax.axis_size("dp"))]
    return lax.ppermute(value, "dp", pairs)


def sibling(value):
    return permute(value, lambda d: d ^ 1)


def dot(a, b):
    return jnp.dot(a, b, preferred_element_type=F32)


def call(kernel, ins, outs, flops, scratch=(), aliases=None, limit=48, far_ins=(), far_outs=()):
    moved = sum(v.size * v.dtype.itemsize for v in [*ins, *outs])
    return pl.pallas_call(
        kernel,
        out_shape=outs,
        in_specs=[SMEM if v.size <= 8 else HBM if at in far_ins else VMEM for at, v in enumerate(ins)],
        out_specs=[HBM if at in far_outs else VMEM for at in range(len(outs))],
        scratch_shapes=scratch,
        input_output_aliases=aliases or {},
        cost_estimate=pl.CostEstimate(
            flops=flops, bytes_accessed=moved if flops > 1 else 1, transcendentals=0
        ),
        compiler_params=pltpu.CompilerParams(vmem_limit_bytes=limit * 2**20),
    )(*ins)


def shape(rows, columns, kind):
    return jax.ShapeDtypeStruct((rows, columns), kind)


def embed(features, head):
    projected = dot(features, head)
    scale = jnp.sqrt(jnp.sum(projected * projected, axis=-1, keepdims=True) + 1e-06)
    return (projected / scale, scale)


def tile_slope(left, right, label_sign, temper, offset):
    scores = temper * dot(left, right.T) + offset
    margin = label_sign * scores
    return (-label_sign * jax.nn.sigmoid(-margin) * temper).astype(BF16)


def project(grad, unit, inverse):
    inner = jnp.sum(unit * grad, axis=-1, keepdims=True)
    return (grad - unit * inner) * inverse


def pairs_kernel(p_grad, p_unit, p_scale, q_grad, q_unit, q_scale, p_pair, q_pair):
    rows = p_grad.shape[0]
    for grad, unit, scale, out in ((q_grad, q_unit, q_scale, q_pair), (p_grad, p_unit, p_scale, p_pair)):
        for at in range(0, rows, 128):
            part = pl.ds(at, 128)
            value = project(grad[part, :], unit[part, :], 1.0 / scale[part, :])
            high = value.astype(BF16)
            out[part, :] = high
            out[pl.ds(rows + at, 128), :] = (value - high.astype(F32)).astype(BF16)


def early_kernel(p, sib_q, p_pair, left, right, sib_q_t, p_twice):
    rows, width = p.shape
    turned = p[...].T
    p_twice[:, :rows] = turned
    p_twice[:, rows:] = turned
    sib_q_t[...] = sib_q[...].T
    for at in range(0, width, 576):
        part = pl.ds(at, 576)
        left[part, :] = dot(p_twice[part, :], p_pair[:, :SPLIT])
        right[part, :] = dot(p_twice[part, :], p_pair[:, SPLIT:])


def other_early_kernel(sib_q_t, sib_pair, left, right, left_out, right_out):
    width, rows = sib_q_t.shape
    for at in range(0, width, 576):
        part = pl.ds(at, 576)
        for before, out, columns in (
            (left, left_out, pl.ds(0, SPLIT)),
            (right, right_out, pl.ds(SPLIT, width - SPLIT)),
        ):
            out[part, :] = (
                before[part, :]
                + dot(sib_q_t[part, :], sib_pair[pl.ds(0, rows), columns])
                + dot(sib_q_t[part, :], sib_pair[pl.ds(rows, rows), columns])
            )


def far_kernel(
    scalars, place, far_img, far_txt, p_head_in, q_head_in, q_low_in, q_unit_in, q_scale_in,
    send_out, qf_t_out, pf_dz_out, pf_t_out,
    send, qf_t, pf_dz, pf_t, pf, qf, p_head, q_head, q_low, q_unit, q_scale, pf_unit, qf_unit, pf_inverse, qf_inverse,
    pf_low, qf_low, slope_a, slope_b, sems, out_sems,
):
    rows = pf.shape[0]
    step = 256
    first = place[0] == 0

    def copy(source, target, at):
        return pltpu.make_async_copy(source, target, sems.at[at])

    @pl.when(first)
    def _():
        copy(far_img, pf, 0).start()

    @pl.when(jnp.logical_not(first))
    def _():
        copy(far_txt, pf, 0).start()

    copies = [copy(p_head_in, p_head, 1)]
    copies[0].start()

    @pl.when(first)
    def _():
        copy(far_txt, qf, 2).start()

    @pl.when(jnp.logical_not(first))
    def _():
        copy(far_img, qf, 2).start()

    for at, (source, target) in enumerate(
        ((q_low_in, q_low), (q_head_in, q_head), (q_unit_in, q_unit), (q_scale_in, q_scale)), 3
    ):
        copies.append(copy(source, target, at))
        copies[-1].start()

    temper, offset = scalars[0], scalars[1]
    stores = []

    def store(source, target, *part):
        if part:
            source, target = source.at[part], target.at[part]
        stores.append(pltpu.make_async_copy(source, target, out_sems.at[len(stores)]))
        stores[-1].start()

    def embed_far(feats, head, unit, inverse, low):
        for at in range(0, rows, step):
            part = pl.ds(at, step)
            projected = dot(feats[part, :], head[...])
            length = jnp.sqrt(jnp.sum(projected * projected, axis=-1, keepdims=True) + 1e-06)
            inverse[part, :] = 1.0 / length
            there = projected * (1.0 / length)
            unit[part, :] = there
            low[part, :] = there.astype(BF16)

    def slopes(low, slope):
        for at in range(0, rows, step):
            part = pl.ds(at, step)
            raw = lax.dot_general(
                pf_low[part, :], low[...], (((1,), (1,)), ((), ())), preferred_element_type=F32
            )
            slope[part, :] = (jax.nn.sigmoid(temper * raw + offset) * temper).astype(BF16)

    copy(far_img, pf, 0).wait()
    copies[0].wait()
    embed_far(pf, p_head, pf_unit, pf_inverse, pf_low)
    pf_t[...] = pf[...].T
    store(pf_t, pf_t_out)
    for at in (1, 2, 3, 4):
        copies[at].wait()
    copy(far_txt, qf, 2).wait()
    qf_t[...] = qf[...].T
    store(qf_t, qf_t_out)
    slopes(q_low, slope_a)
    embed_far(qf, q_head, qf_unit, qf_inverse, qf_low)
    slopes(qf_low, slope_b)
    for at in range(0, rows, step):
        part = pl.ds(at, step)
        grad = dot(slope_a[:, part].T, pf_low[...])
        send[part, :] = project(grad, q_unit[part, :], 1.0 / q_scale[part, :]).astype(BF16)
        store(send, send_out, part)
        again = pl.ds(rows + at, step)
        grad = dot(slope_b[:, part].T, pf_low[...])
        send[again, :] = project(grad, qf_unit[part, :], qf_inverse[part, :]).astype(BF16)
        store(send, send_out, again)
        grad = dot(slope_a[part, :], q_low[...]) + dot(slope_b[part, :], qf_low[...])
        pf_dz[part, :] = project(grad, pf_unit[part, :], pf_inverse[part, :]).astype(BF16)
        store(pf_dz, pf_dz_out, part)
    for copy_out in stores:
        copy_out.wait()


def fetch(pairs, sems):
    copies = [pltpu.make_async_copy(*pair, sems.at[at]) for at, pair in enumerate(pairs)]
    for copy in copies:
        copy.start()
    return lambda at: copies[at].wait()


def near_kernel(*refs):
    ins, outs, held, (in_sems, out_sems) = refs[:4], refs[4:6], refs[6:10], refs[10:]
    pf_t, pf_dz, left, right = held
    width = pf_t.shape[0]
    halves = [pl.ds(0, 576), pl.ds(576, 576)]
    wait = fetch(
        [(ins[1], pf_dz), (ins[0], pf_t)]
        + [(ins[2 + which].at[part, :], held[2 + which].at[part, :]) for part in halves for which in (0, 1)],
        in_sems,
    )
    wait(0)
    wait(1)
    stores = []
    for part in halves:
        for total, out, columns in (
            (left, outs[0], pl.ds(0, SPLIT)),
            (right, outs[1], pl.ds(SPLIT, width - SPLIT)),
        ):
            value = dot(pf_t[part, :], pf_dz[:, columns])
            at = len(stores)
            wait(2 + at)
            total[part, :] = total[part, :] + value
            stores.append(pltpu.make_async_copy(total.at[part, :], out.at[part, :], out_sems.at[at]))
            stores[-1].start()
    for store in stores:
        store.wait()


def cut_kernel(first, along_x, place, *refs):
    ins, (keep_1, send_1, keep_3, send_3), (both_t, got, total, in_sems) = refs[:4], refs[4:8], refs[8:]
    width, count = total.shape
    rows = both_t.shape[1] // 2
    halves = [pl.ds(0, 576), pl.ds(576, 576)]
    wait = fetch(
        [
            (ins[0], both_t.at[:, pl.ds(0, rows)]), (ins[1].at[:, pl.ds(first, count)], got),
            (ins[2], both_t.at[:, pl.ds(rows, rows)]),
        ]
        + [(ins[3].at[part, :], total.at[part, :]) for part in halves],
        in_sems,
    )
    for at in range(3):
        wait(at)
    for at, part in enumerate(halves):
        value = dot(both_t[part, :], got[...])
        wait(3 + at)
        total[part, :] = total[part, :] + value

    def half(target, which):
        if along_x:
            return total[pl.ds(pl.multiple_of(288 * target + 144 * which, 8), 144), :]
        starts = [288 * (2 * which + block) + 72 * target for block in (0, 1)]
        return jnp.concatenate([total[pl.ds(pl.multiple_of(at, 8), 72), :] for at in starts], axis=0)

    me = place[0]
    top, low = pl.ds(0, 144), pl.ds(144, 144)
    keep_1[top, :] = half(me, 0)
    keep_1[low, :] = half(me ^ 3, 0)
    send_1[top, :] = half(me ^ 1, 0).astype(BF16)
    send_1[low, :] = half(me ^ 2, 0).astype(BF16)
    keep_3[top, :] = half(me, 1)
    keep_3[low, :] = half(me ^ 1, 1)
    send_3[top, :] = half(me ^ 3, 1).astype(BF16)
    send_3[low, :] = half(me ^ 2, 1).astype(BF16)


def second_kernel(keep_1, got_1, keep_3, got_3, own, send_3, send_1):
    top, low = pl.ds(0, 144), pl.ds(144, 144)
    first = keep_1[...] + got_1[...].astype(F32)
    own[top, :] = first[:144]
    send_3[...] = first[144:]
    other = keep_3[...] + got_3[...].astype(F32)
    own[low, :] = other[:144]
    send_1[...] = other[144:]


def third_kernel(place, own, got_3, got_1, *rest):
    outs, total = rest[:4], rest[4]
    total[pl.ds(0, 144), :] = own[pl.ds(0, 144), :] + got_3[...]
    total[pl.ds(144, 144), :] = own[pl.ds(144, 144), :] + got_1[...]
    for j in range(4):
        outs[j][...] = total[pl.ds(pl.multiple_of(72 * (place[0] ^ j), 8), 72), :]


def z_pieces_kernel(place, *rest):
    left, right, outs, total, packed = rest[:4], rest[4:8], rest[8:12], rest[12], rest[13]
    total[:, :SPLIT] = left[0][...] + left[1][...] + left[2][...] + left[3][...]
    total[:, SPLIT:] = right[0][...] + right[1][...] + right[2][...] + right[3][...]
    for at in range(4):
        for tile in range(9):
            packed[at, 18 * tile : 18 * tile + 18, :] = total[18 * at : 18 * at + 18, 128 * tile : 128 * tile + 128]
    for j in range(4):
        outs[j][...] = packed[place[0] ^ j, 0:162, :]


def sum_kernel(a, b, c, d, total):
    total[...] = a[...] + b[...] + c[...] + d[...]


def last_kernel(place, a, b, mine, squares, total):
    total[...] = a[...] + b[...]

    def take(first):
        for tile in range(9):
            mine[9 * tile : 9 * tile + 9, :] = total[18 * tile + first : 18 * tile + first + 9, :]

    @pl.when(place[0] == 0)
    def _():
        take(0)

    @pl.when(place[0] != 0)
    def _():
        take(9)

    value = total[...]
    squares[...] = jnp.broadcast_to(jnp.sum(value * value, axis=0, keepdims=True), squares.shape)


def lanes_kernel(got, squares):
    lanes = jnp.sum(got[...], axis=0, keepdims=True) * 0.125
    squares[...] = jnp.broadcast_to(lanes, squares.shape)


def scale_kernel(rows, got, out):
    total = jnp.sum(jnp.sum(got[...], axis=0, keepdims=True), axis=1, keepdims=True) * 0.125
    entries = 2 * out.shape[1] * out.shape[1]
    spread = jnp.sqrt(total / entries + 1e-06)
    for tile in range(9):
        out[:, 128 * tile : 128 * tile + 128] = rows[9 * tile : 9 * tile + 9, :] / spread


def swap_all(value, bits):
    masks = [sum(1 << bit for at, bit in enumerate(bits) if k >> at & 1) for k in range(2 ** len(bits))]
    groups = [[d | mask for mask in masks] for d in range(lax.axis_size("dp")) if not d & masks[-1]]
    return lax.all_to_all(value, "dp", 0, 0, axis_index_groups=groups, tiled=True)


def per_device(img_feats, txt_feats, img_head, txt_head, log_temp, logit_bias, caption_row):
    me = lax.axis_index("dp")
    core, y, x, z = me & 1, (me >> 1) & 3, (me >> 3) & 3, me >> 5
    first = core == 0
    rows, width = img_feats.shape

    far_img = permute(img_feats, lambda d: d ^ (192 if d & 1 else 64))
    far_txt = permute(txt_feats, lambda d: d ^ (64 if d & 1 else 192))
    p = jnp.where(first, img_feats, txt_feats)
    q = jnp.where(first, txt_feats, img_feats)
    p_head = jnp.where(first, img_head, txt_head)
    q_head = jnp.where(first, txt_head, img_head)
    sib_q = sibling(q)

    temper = jnp.exp(log_temp)
    index = jnp.arange(rows, dtype=jnp.int32)
    match = jnp.where(first, caption_row, index)[:, None] == jnp.where(first, index, caption_row)[None, :]
    label_sign = jnp.where(match, 1.0, -1.0).astype(F32)

    p_unit, p_scale = embed(p, p_head)
    q_unit, q_scale = embed(q, q_head)
    p_low = p_unit.astype(BF16)
    q_low = q_unit.astype(BF16)
    slope = tile_slope(p_low, q_low, label_sign, temper, logit_bias)
    p_grad = dot(slope, q_low)
    q_grad = dot(slope.T, p_low)
    scalars = jnp.stack([temper, logit_bias])
    p_pair, q_pair = call(
        pairs_kernel,
        (p_grad, p_unit, p_scale, q_grad, q_unit, q_scale),
        (shape(2 * rows, width, BF16), shape(2 * rows, width, BF16)),
        1,
        limit=20,
    )
    sib_pair = sibling(q_pair)
    left, right, sib_q_t = call(
        early_kernel,
        (p, sib_q, p_pair),
        (shape(width, SPLIT, F32), shape(width, width - SPLIT, F32), shape(width, rows, BF16)),
        200 * rows * width * width,
        [pltpu.VMEM((width, 2 * rows), BF16)],
        limit=20,
    )
    left, right = call(
        other_early_kernel,
        (sib_q_t, sib_pair, left, right),
        (shape(width, SPLIT, F32), shape(width, width - SPLIT, F32)),
        1,
        (),
        {2: 0, 3: 1},
        limit=24,
    )
    far_img, far_txt, left, right, sib_q_t = lax.optimization_barrier(
        (far_img, far_txt, left, right, sib_q_t)
    )

    wide, low, thin = (pltpu.VMEM(dims, kind) for dims, kind in (
        ((rows, width), F32), ((rows, width), BF16), ((rows, 1), F32),
    ))
    head, tile = pltpu.VMEM((width, width), BF16), pltpu.VMEM((rows, rows), BF16)
    turned = pltpu.VMEM((width, rows), BF16)
    send, qf_t, pf_dz, pf_t = call(
        far_kernel,
        (scalars, jnp.stack([core, 0]), far_img, far_txt, p_head, q_head, q_low, q_unit, q_scale),
        (shape(2 * rows, width, BF16), shape(width, rows, BF16), shape(rows, width, BF16), shape(width, rows, BF16)),
        4 * rows * width * width + 12 * rows * rows * width,
        [
            pltpu.VMEM((2 * rows, width), BF16), turned, low, turned,
            low, low, head, head, low, wide, thin, wide, wide, thin, thin,
            low, low, tile, tile, pltpu.SemaphoreType.DMA((7,)), pltpu.SemaphoreType.DMA((8,)),
        ],
        limit=LIMIT,
        far_ins=range(9),
        far_outs=range(4),
    )
    got, sib_qf_t = sibling(send), sibling(qf_t)
    accumulators = [pltpu.VMEM((width, SPLIT), F32), pltpu.VMEM((width, width - SPLIT), F32)]
    left, right = call(
        near_kernel,
        (pf_t, pf_dz, left, right),
        (shape(width, SPLIT, F32), shape(width, width - SPLIT, F32)),
        2 * rows * width * width,
        [turned, low, *accumulators, pltpu.SemaphoreType.DMA((6,)), pltpu.SemaphoreType.DMA((4,))],
        limit=LIMIT,
        far_ins=range(4),
        far_outs=range(2),
    )

    def cut(first, along_x, place, head_grad):
        count = head_grad.shape[1]
        return call(
            functools.partial(cut_kernel, first, along_x),
            (jnp.stack([place, 0]), sib_q_t, got, sib_qf_t, head_grad),
            (shape(288, count, F32), shape(288, count, BF16)) * 2,
            4 * rows * width * count,
            [
                pltpu.VMEM((width, 2 * rows), BF16), pltpu.VMEM((2 * rows, count), BF16),
                pltpu.VMEM((width, count), F32), pltpu.SemaphoreType.DMA((5,)),
            ],
            limit=24,
            far_ins=range(1, 5),
        )

    def first_step(parts, bit):
        keep_1, send_1, keep_3, send_3 = parts
        return keep_1, permute(send_1, lambda d: d ^ (1 << bit)), keep_3, permute(send_3, lambda d: d ^ (3 << bit))

    def second_step(parts):
        count = parts[0].shape[1]
        return call(
            second_kernel,
            parts,
            (shape(288, count, F32), shape(144, count, F32), shape(144, count, F32)),
            288 * count,
            limit=8,
        )

    def last_step(parts, bit, other, other_bit):
        own, send_3, send_1 = parts
        count = own.shape[1]
        got_3 = permute(send_3, lambda d: d ^ (3 << bit))
        got_1 = permute(send_1, lambda d: d ^ (1 << bit))
        outs = call(
            third_kernel,
            (jnp.stack([other, 0]), own, got_3, got_1),
            [shape(72, count, F32)] * 4,
            288 * count,
            [pltpu.VMEM((288, count), F32)],
            limit=8,
        )
        return outs[0], [permute(outs[j], lambda d, j=j: d ^ (j << other_bit)) for j in (1, 2, 3)]

    own, *left = second_step(first_step(cut(0, True, x, left), 3))
    keep, *right = first_step(cut(SPLIT, False, y, right), 1)
    own, keep = lax.optimization_barrier((own, keep))
    left, right = (own, *left), second_step((keep, *right))
    own, left = last_step(left, 3, y, 1)
    own, keep = lax.optimization_barrier((own, right[0]))
    left = [own, *left]
    own, right = last_step((keep, *right[1:]), 1, x, 3)
    right = [own, *right]
    parts = call(
        z_pieces_kernel,
        (jnp.stack([z >> 1, 0]), *left, *right),
        [shape(162, 128, F32)] * 4,
        6 * 72 * width,
        [pltpu.VMEM((72, width), F32), pltpu.VMEM((4, 168, 128), F32)],
        limit=8,
    )
    parts = [parts[0]] + [permute(parts[j], lambda d, j=j: d ^ (j << 6)) for j in (1, 2, 3)]
    [part] = call(sum_kernel, parts, [shape(162, 128, F32)], 3 * 18 * width, limit=8)

    other = permute(part, lambda d: d ^ 32)
    total, squares = call(
        last_kernel,
        (jnp.stack([z & 1, 0]), part, other),
        (shape(81, 128, F32), shape(64, 128, F32)),
        10 * 18 * width,
        [pltpu.VMEM((162, 128), F32)],
        limit=8,
    )

    def owner(d):
        z, x, y, s = d >> 5, d >> 3 & 3, d >> 1 & 3, d & 1
        return (4 * s + x) << 5 | y << 3 | (z >> 1) << 1 | z & 1

    mine = permute(total, owner)
    [squares] = call(lanes_kernel, (swap_all(squares, (0, 6, 7)),), [shape(128, 128, F32)], 10000, limit=8)
    squares, mine = lax.optimization_barrier((squares, mine))
    got = swap_all(squares, (1, 2, 3, 4))
    [out] = call(scale_kernel, (mine, got), [shape(9, width, F32)], 10 * 9 * width, limit=8)
    return out


def solution(mesh):
    return jax.shard_map(
        per_device,
        mesh=mesh,
        in_specs=(P("dp", None), P("dp", None), P(), P(), P(), P(), P("dp")),
        out_specs=P("dp", None),
        check_vma=False,
    )
```

```python
import functools

import jax
import jax.numpy as jnp
from jax import lax
from jax.experimental import pallas as pl
from jax.experimental.pallas import tpu as pltpu
from jax.sharding import PartitionSpec as P

SPLIT = 640
LIMIT = 62
F32, BF16 = jnp.float32, jnp.bfloat16
VMEM = pl.BlockSpec(memory_space=pltpu.VMEM)
SMEM = pl.BlockSpec(memory_space=pltpu.SMEM)
HBM = pl.BlockSpec(memory_space=pltpu.HBM)


def permute(value, target):
    pairs = [(source, target(source)) for source in range(lax.axis_size("dp"))]
    return lax.ppermute(value, "dp", pairs)


def sibling(value):
    return permute(value, lambda d: d ^ 1)


def dot(a, b):
    return jnp.dot(a, b, preferred_element_type=F32)


def call(kernel, ins, outs, flops, scratch=(), aliases=None, limit=48, far_ins=(), far_outs=()):
    moved = sum(v.size * v.dtype.itemsize for v in [*ins, *outs])
    return pl.pallas_call(
        kernel,
        out_shape=outs,
        in_specs=[SMEM if v.size <= 8 else HBM if at in far_ins else VMEM for at, v in enumerate(ins)],
        out_specs=[HBM if at in far_outs else VMEM for at in range(len(outs))],
        scratch_shapes=scratch,
        input_output_aliases=aliases or {},
        cost_estimate=pl.CostEstimate(
            flops=flops, bytes_accessed=moved if flops > 1 else 1, transcendentals=0
        ),
        compiler_params=pltpu.CompilerParams(vmem_limit_bytes=limit * 2**20),
    )(*ins)


def shape(rows, columns, kind):
    return jax.ShapeDtypeStruct((rows, columns), kind)


def embed(features, head):
    projected = dot(features, head)
    scale = jnp.sqrt(jnp.sum(projected * projected, axis=-1, keepdims=True) + 1e-06)
    return (projected / scale, scale)


def tile_slope(left, right, label_sign, temper, offset):
    scores = temper * dot(left, right.T) + offset
    margin = label_sign * scores
    return (-label_sign * jax.nn.sigmoid(-margin) * temper).astype(BF16)


def project(grad, unit, inverse):
    inner = jnp.sum(unit * grad, axis=-1, keepdims=True)
    return (grad - unit * inner) * inverse


def pairs_kernel(p_grad, p_unit, p_scale, q_grad, q_unit, q_scale, p_pair, q_pair):
    rows = p_grad.shape[0]
    for grad, unit, scale, out in ((q_grad, q_unit, q_scale, q_pair), (p_grad, p_unit, p_scale, p_pair)):
        for at in range(0, rows, 128):
            part = pl.ds(at, 128)
            value = project(grad[part, :], unit[part, :], 1.0 / scale[part, :])
            high = value.astype(BF16)
            out[part, :] = high
            out[pl.ds(rows + at, 128), :] = (value - high.astype(F32)).astype(BF16)


def early_kernel(p, sib_q, p_pair, left, right, sib_q_t, p_twice):
    rows, width = p.shape
    turned = p[...].T
    p_twice[:, :rows] = turned
    p_twice[:, rows:] = turned
    sib_q_t[...] = sib_q[...].T
    for at in range(0, width, 576):
        part = pl.ds(at, 576)
        left[part, :] = dot(p_twice[part, :], p_pair[:, :SPLIT])
        right[part, :] = dot(p_twice[part, :], p_pair[:, SPLIT:])


def other_early_kernel(sib_q_t, sib_pair, left, right, left_out, right_out):
    width, rows = sib_q_t.shape
    for at in range(0, width, 576):
        part = pl.ds(at, 576)
        for before, out, columns in (
            (left, left_out, pl.ds(0, SPLIT)),
            (right, right_out, pl.ds(SPLIT, width - SPLIT)),
        ):
            out[part, :] = (
                before[part, :]
                + dot(sib_q_t[part, :], sib_pair[pl.ds(0, rows), columns])
                + dot(sib_q_t[part, :], sib_pair[pl.ds(rows, rows), columns])
            )


def far_kernel(
    scalars, place, far_img, far_txt, p_head_in, q_head_in, q_low_in, q_unit_in, q_scale_in,
    send_out, qf_t_out, pf_dz_out, pf_t_out,
    send, qf_t, pf_dz, pf_t, pf, qf, p_head, q_head, q_low, q_unit, q_scale, pf_unit, qf_unit, pf_inverse, qf_inverse,
    pf_low, qf_low, slope_a, slope_b, sems, out_sems,
):
    rows = pf.shape[0]
    step = 256
    first = place[0] == 0

    def copy(source, target, at):
        return pltpu.make_async_copy(source, target, sems.at[at])

    @pl.when(first)
    def _():
        copy(far_img, pf, 0).start()

    @pl.when(jnp.logical_not(first))
    def _():
        copy(far_txt, pf, 0).start()

    copies = [copy(p_head_in, p_head, 1)]
    copies[0].start()

    @pl.when(first)
    def _():
        copy(far_txt, qf, 2).start()

    @pl.when(jnp.logical_not(first))
    def _():
        copy(far_img, qf, 2).start()

    for at, (source, target) in enumerate(
        ((q_low_in, q_low), (q_head_in, q_head), (q_unit_in, q_unit), (q_scale_in, q_scale)), 3
    ):
        copies.append(copy(source, target, at))
        copies[-1].start()

    temper, offset = scalars[0], scalars[1]
    stores = []

    def store(source, target, *part):
        if part:
            source, target = source.at[part], target.at[part]
        stores.append(pltpu.make_async_copy(source, target, out_sems.at[len(stores)]))
        stores[-1].start()

    def embed_far(feats, head, unit, inverse, low):
        projected = dot(feats[...], head[...])
        length = jnp.sqrt(jnp.sum(projected * projected, axis=-1, keepdims=True) + 1e-06)
        inverse[...] = 1.0 / length
        there = projected * (1.0 / length)
        unit[...] = there
        low[...] = there.astype(BF16)

    def slopes(low, slope):
        for at in range(0, rows, step):
            part = pl.ds(at, step)
            raw = lax.dot_general(
                pf_low[part, :], low[...], (((1,), (1,)), ((), ())), preferred_element_type=F32
            )
            slope[part, :] = (jax.nn.sigmoid(temper * raw + offset) * temper).astype(BF16)

    copy(far_img, pf, 0).wait()
    copies[0].wait()
    embed_far(pf, p_head, pf_unit, pf_inverse, pf_low)
    pf_t[...] = pf[...].T
    store(pf_t, pf_t_out)
    for at in (1, 2, 3, 4):
        copies[at].wait()
    copy(far_txt, qf, 2).wait()
    qf_t[...] = qf[...].T
    store(qf_t, qf_t_out)
    slopes(q_low, slope_a)
    embed_far(qf, q_head, qf_unit, qf_inverse, qf_low)
    slopes(qf_low, slope_b)
    for at in range(0, rows, step):
        part = pl.ds(at, step)
        grad = dot(slope_a[:, part].T, pf_low[...])
        send[part, :] = project(grad, q_unit[part, :], 1.0 / q_scale[part, :]).astype(BF16)
        store(send, send_out, part)
        again = pl.ds(rows + at, step)
        grad = dot(slope_b[:, part].T, pf_low[...])
        send[again, :] = project(grad, qf_unit[part, :], qf_inverse[part, :]).astype(BF16)
        store(send, send_out, again)
        grad = dot(slope_a[part, :], q_low[...]) + dot(slope_b[part, :], qf_low[...])
        pf_dz[part, :] = project(grad, pf_unit[part, :], pf_inverse[part, :]).astype(BF16)
        store(pf_dz, pf_dz_out, part)
    for copy_out in stores:
        copy_out.wait()


def fetch(pairs, sems):
    copies = [pltpu.make_async_copy(*pair, sems.at[at]) for at, pair in enumerate(pairs)]
    for copy in copies:
        copy.start()
    return lambda at: copies[at].wait()


def near_kernel(*refs):
    ins, outs, held, (in_sems, out_sems) = refs[:4], refs[4:6], refs[6:10], refs[10:]
    pf_t, pf_dz, left, right = held
    width = pf_t.shape[0]
    halves = [pl.ds(0, 576), pl.ds(576, 576)]
    wait = fetch(
        [(ins[1], pf_dz), (ins[0], pf_t)]
        + [(ins[2 + which].at[part, :], held[2 + which].at[part, :]) for part in halves for which in (0, 1)],
        in_sems,
    )
    wait(0)
    wait(1)
    stores = []
    for part in halves:
        for total, out, columns in (
            (left, outs[0], pl.ds(0, SPLIT)),
            (right, outs[1], pl.ds(SPLIT, width - SPLIT)),
        ):
            value = dot(pf_t[part, :], pf_dz[:, columns])
            at = len(stores)
            wait(2 + at)
            total[part, :] = total[part, :] + value
            stores.append(pltpu.make_async_copy(total.at[part, :], out.at[part, :], out_sems.at[at]))
            stores[-1].start()
    for store in stores:
        store.wait()


def cut_kernel(first, along_x, place, *refs):
    ins, (keep_1, send_1, keep_3, send_3), (both_t, got, total, in_sems) = refs[:4], refs[4:8], refs[8:]
    width, count = total.shape
    rows = both_t.shape[1] // 2
    halves = [pl.ds(0, 576), pl.ds(576, 576)]
    wait = fetch(
        [
            (ins[0], both_t.at[:, pl.ds(0, rows)]), (ins[1].at[:, pl.ds(first, count)], got),
            (ins[2], both_t.at[:, pl.ds(rows, rows)]),
        ]
        + [(ins[3].at[part, :], total.at[part, :]) for part in halves],
        in_sems,
    )
    for at in range(3):
        wait(at)
    for at, part in enumerate(halves):
        value = dot(both_t[part, :], got[...])
        wait(3 + at)
        total[part, :] = total[part, :] + value

    def half(target, which):
        if along_x:
            return total[pl.ds(pl.multiple_of(288 * target + 144 * which, 8), 144), :]
        starts = [288 * (2 * which + block) + 72 * target for block in (0, 1)]
        return jnp.concatenate([total[pl.ds(pl.multiple_of(at, 8), 72), :] for at in starts], axis=0)

    me = place[0]
    top, low = pl.ds(0, 144), pl.ds(144, 144)
    keep_1[top, :] = half(me, 0)
    keep_1[low, :] = half(me ^ 3, 0)
    send_1[top, :] = half(me ^ 1, 0).astype(BF16)
    send_1[low, :] = half(me ^ 2, 0).astype(BF16)
    keep_3[top, :] = half(me, 1)
    keep_3[low, :] = half(me ^ 1, 1)
    send_3[top, :] = half(me ^ 3, 1).astype(BF16)
    send_3[low, :] = half(me ^ 2, 1).astype(BF16)


def second_kernel(keep_1, got_1, keep_3, got_3, own, send_3, send_1):
    top, low = pl.ds(0, 144), pl.ds(144, 144)
    first = keep_1[...] + got_1[...].astype(F32)
    own[top, :] = first[:144]
    send_3[...] = first[144:]
    other = keep_3[...] + got_3[...].astype(F32)
    own[low, :] = other[:144]
    send_1[...] = other[144:]


def third_kernel(place, own, got_3, got_1, *rest):
    outs, total = rest[:4], rest[4]
    total[pl.ds(0, 144), :] = own[pl.ds(0, 144), :] + got_3[...]
    total[pl.ds(144, 144), :] = own[pl.ds(144, 144), :] + got_1[...]
    for j in range(4):
        outs[j][...] = total[pl.ds(pl.multiple_of(72 * (place[0] ^ j), 8), 72), :]


def z_pieces_kernel(place, *rest):
    left, right, outs, total, packed = rest[:4], rest[4:8], rest[8:12], rest[12], rest[13]
    total[:, :SPLIT] = left[0][...] + left[1][...] + left[2][...] + left[3][...]
    total[:, SPLIT:] = right[0][...] + right[1][...] + right[2][...] + right[3][...]
    for at in range(4):
        for tile in range(9):
            packed[at, 18 * tile : 18 * tile + 18, :] = total[18 * at : 18 * at + 18, 128 * tile : 128 * tile + 128]
    for j in range(4):
        outs[j][...] = packed[place[0] ^ j, 0:162, :]


def sum_kernel(a, b, c, d, total):
    total[...] = a[...] + b[...] + c[...] + d[...]


def last_kernel(place, a, b, mine, squares, total):
    total[...] = a[...] + b[...]

    def take(first):
        for tile in range(9):
            mine[9 * tile : 9 * tile + 9, :] = total[18 * tile + first : 18 * tile + first + 9, :]

    @pl.when(place[0] == 0)
    def _():
        take(0)

    @pl.when(place[0] != 0)
    def _():
        take(9)

    value = total[...]
    squares[...] = jnp.broadcast_to(jnp.sum(value * value, axis=0, keepdims=True), squares.shape)


def lanes_kernel(got, squares):
    lanes = jnp.sum(got[...], axis=0, keepdims=True) * 0.125
    squares[...] = jnp.broadcast_to(lanes, squares.shape)


def scale_kernel(rows, got, out):
    total = jnp.sum(jnp.sum(got[...], axis=0, keepdims=True), axis=1, keepdims=True) * 0.125
    entries = 2 * out.shape[1] * out.shape[1]
    spread = jnp.sqrt(total / entries + 1e-06)
    for tile in range(9):
        out[:, 128 * tile : 128 * tile + 128] = rows[9 * tile : 9 * tile + 9, :] / spread


def swap_all(value, bits):
    masks = [sum(1 << bit for at, bit in enumerate(bits) if k >> at & 1) for k in range(2 ** len(bits))]
    groups = [[d | mask for mask in masks] for d in range(lax.axis_size("dp")) if not d & masks[-1]]
    return lax.all_to_all(value, "dp", 0, 0, axis_index_groups=groups, tiled=True)


def per_device(img_feats, txt_feats, img_head, txt_head, log_temp, logit_bias, caption_row):
    me = lax.axis_index("dp")
    core, y, x, z = me & 1, (me >> 1) & 3, (me >> 3) & 3, me >> 5
    first = core == 0
    rows, width = img_feats.shape

    far_img = permute(img_feats, lambda d: d ^ (192 if d & 1 else 64))
    far_txt = permute(txt_feats, lambda d: d ^ (64 if d & 1 else 192))
    p = jnp.where(first, img_feats, txt_feats)
    q = jnp.where(first, txt_feats, img_feats)
    p_head = jnp.where(first, img_head, txt_head)
    q_head = jnp.where(first, txt_head, img_head)
    sib_q = sibling(q)

    temper = jnp.exp(log_temp)
    index = jnp.arange(rows, dtype=jnp.int32)
    match = jnp.where(first, caption_row, index)[:, None] == jnp.where(first, index, caption_row)[None, :]
    label_sign = jnp.where(match, 1.0, -1.0).astype(F32)

    p_unit, p_scale = embed(p, p_head)
    q_unit, q_scale = embed(q, q_head)
    p_low = p_unit.astype(BF16)
    q_low = q_unit.astype(BF16)
    slope = tile_slope(p_low, q_low, label_sign, temper, logit_bias)
    p_grad = dot(slope, q_low)
    q_grad = dot(slope.T, p_low)
    scalars = jnp.stack([temper, logit_bias])
    p_pair, q_pair = call(
        pairs_kernel,
        (p_grad, p_unit, p_scale, q_grad, q_unit, q_scale),
        (shape(2 * rows, width, BF16), shape(2 * rows, width, BF16)),
        1,
        limit=20,
    )
    sib_pair = sibling(q_pair)
    left, right, sib_q_t = call(
        early_kernel,
        (p, sib_q, p_pair),
        (shape(width, SPLIT, F32), shape(width, width - SPLIT, F32), shape(width, rows, BF16)),
        200 * rows * width * width,
        [pltpu.VMEM((width, 2 * rows), BF16)],
        limit=20,
    )
    left, right = call(
        other_early_kernel,
        (sib_q_t, sib_pair, left, right),
        (shape(width, SPLIT, F32), shape(width, width - SPLIT, F32)),
        1,
        (),
        {2: 0, 3: 1},
        limit=24,
    )
    far_img, far_txt, left, right, sib_q_t = lax.optimization_barrier(
        (far_img, far_txt, left, right, sib_q_t)
    )

    wide, low, thin = (pltpu.VMEM(dims, kind) for dims, kind in (
        ((rows, width), F32), ((rows, width), BF16), ((rows, 1), F32),
    ))
    head, tile = pltpu.VMEM((width, width), BF16), pltpu.VMEM((rows, rows), BF16)
    turned = pltpu.VMEM((width, rows), BF16)
    send, qf_t, pf_dz, pf_t = call(
        far_kernel,
        (scalars, jnp.stack([core, 0]), far_img, far_txt, p_head, q_head, q_low, q_unit, q_scale),
        (shape(2 * rows, width, BF16), shape(width, rows, BF16), shape(rows, width, BF16), shape(width, rows, BF16)),
        4 * rows * width * width + 12 * rows * rows * width,
        [
            pltpu.VMEM((2 * rows, width), BF16), turned, low, turned,
            low, low, head, head, low, wide, thin, wide, wide, thin, thin,
            low, low, tile, tile, pltpu.SemaphoreType.DMA((7,)), pltpu.SemaphoreType.DMA((8,)),
        ],
        limit=LIMIT,
        far_ins=range(9),
        far_outs=range(4),
    )
    got, sib_qf_t = sibling(send), sibling(qf_t)
    accumulators = [pltpu.VMEM((width, SPLIT), F32), pltpu.VMEM((width, width - SPLIT), F32)]
    left, right = call(
        near_kernel,
        (pf_t, pf_dz, left, right),
        (shape(width, SPLIT, F32), shape(width, width - SPLIT, F32)),
        2 * rows * width * width,
        [turned, low, *accumulators, pltpu.SemaphoreType.DMA((6,)), pltpu.SemaphoreType.DMA((4,))],
        limit=LIMIT,
        far_ins=range(4),
        far_outs=range(2),
    )

    def cut(first, along_x, place, head_grad):
        count = head_grad.shape[1]
        return call(
            functools.partial(cut_kernel, first, along_x),
            (jnp.stack([place, 0]), sib_q_t, got, sib_qf_t, head_grad),
            (shape(288, count, F32), shape(288, count, BF16)) * 2,
            4 * rows * width * count,
            [
                pltpu.VMEM((width, 2 * rows), BF16), pltpu.VMEM((2 * rows, count), BF16),
                pltpu.VMEM((width, count), F32), pltpu.SemaphoreType.DMA((5,)),
            ],
            limit=24,
            far_ins=range(1, 5),
        )

    def first_step(parts, bit):
        keep_1, send_1, keep_3, send_3 = parts
        return keep_1, permute(send_1, lambda d: d ^ (1 << bit)), keep_3, permute(send_3, lambda d: d ^ (3 << bit))

    def second_step(parts):
        count = parts[0].shape[1]
        return call(
            second_kernel,
            parts,
            (shape(288, count, F32), shape(144, count, F32), shape(144, count, F32)),
            288 * count,
            limit=8,
        )

    def last_step(parts, bit, other, other_bit):
        own, send_3, send_1 = parts
        count = own.shape[1]
        got_3 = permute(send_3, lambda d: d ^ (3 << bit))
        got_1 = permute(send_1, lambda d: d ^ (1 << bit))
        outs = call(
            third_kernel,
            (jnp.stack([other, 0]), own, got_3, got_1),
            [shape(72, count, F32)] * 4,
            288 * count,
            [pltpu.VMEM((288, count), F32)],
            limit=8,
        )
        return outs[0], [permute(outs[j], lambda d, j=j: d ^ (j << other_bit)) for j in (1, 2, 3)]

    own, *left = second_step(first_step(cut(0, True, x, left), 3))
    keep, *right = first_step(cut(SPLIT, False, y, right), 1)
    own, keep = lax.optimization_barrier((own, keep))
    left, right = (own, *left), second_step((keep, *right))
    own, left = last_step(left, 3, y, 1)
    own, keep = lax.optimization_barrier((own, right[0]))
    left = [own, *left]
    own, right = last_step((keep, *right[1:]), 1, x, 3)
    right = [own, *right]
    parts = call(
        z_pieces_kernel,
        (jnp.stack([z >> 1, 0]), *left, *right),
        [shape(162, 128, F32)] * 4,
        6 * 72 * width,
        [pltpu.VMEM((72, width), F32), pltpu.VMEM((4, 168, 128), F32)],
        limit=8,
    )
    parts = [parts[0]] + [permute(parts[j], lambda d, j=j: d ^ (j << 6)) for j in (1, 2, 3)]
    [part] = call(sum_kernel, parts, [shape(162, 128, F32)], 3 * 18 * width, limit=8)

    other = permute(part, lambda d: d ^ 32)
    total, squares = call(
        last_kernel,
        (jnp.stack([z & 1, 0]), part, other),
        (shape(81, 128, F32), shape(64, 128, F32)),
        10 * 18 * width,
        [pltpu.VMEM((162, 128), F32)],
        limit=8,
    )

    def owner(d):
        z, x, y, s = d >> 5, d >> 3 & 3, d >> 1 & 3, d & 1
        return (4 * s + x) << 5 | y << 3 | (z >> 1) << 1 | z & 1

    mine = permute(total, owner)
    [squares] = call(lanes_kernel, (swap_all(squares, (0, 6, 7)),), [shape(128, 128, F32)], 10000, limit=8)
    squares, mine = lax.optimization_barrier((squares, mine))
    got = swap_all(squares, (1, 2, 3, 4))
    [out] = call(scale_kernel, (mine, got), [shape(9, width, F32)], 10 * 9 * width, limit=8)
    return out


def solution(mesh):
    return jax.shard_map(
        per_device,
        mesh=mesh,
        in_specs=(P("dp", None), P("dp", None), P(), P(), P(), P(), P("dp")),
        out_specs=P("dp", None),
        check_vma=False,
    )
```

```python
import functools

import jax
import jax.numpy as jnp
from jax import lax
from jax.experimental import pallas as pl
from jax.experimental.pallas import tpu as pltpu
from jax.sharding import PartitionSpec as P

SPLIT = 640
LIMIT = 62
F32, BF16 = jnp.float32, jnp.bfloat16
VMEM = pl.BlockSpec(memory_space=pltpu.VMEM)
SMEM = pl.BlockSpec(memory_space=pltpu.SMEM)
HBM = pl.BlockSpec(memory_space=pltpu.HBM)


def permute(value, target):
    pairs = [(source, target(source)) for source in range(lax.axis_size("dp"))]
    return lax.ppermute(value, "dp", pairs)


def sibling(value):
    return permute(value, lambda d: d ^ 1)


def dot(a, b):
    return jnp.dot(a, b, preferred_element_type=F32)


def call(kernel, ins, outs, flops, scratch=(), aliases=None, limit=48, far_ins=(), far_outs=()):
    moved = sum(v.size * v.dtype.itemsize for v in [*ins, *outs])
    return pl.pallas_call(
        kernel,
        out_shape=outs,
        in_specs=[SMEM if v.size <= 8 else HBM if at in far_ins else VMEM for at, v in enumerate(ins)],
        out_specs=[HBM if at in far_outs else VMEM for at in range(len(outs))],
        scratch_shapes=scratch,
        input_output_aliases=aliases or {},
        cost_estimate=pl.CostEstimate(
            flops=flops, bytes_accessed=moved if flops > 1 else 1, transcendentals=0
        ),
        compiler_params=pltpu.CompilerParams(vmem_limit_bytes=limit * 2**20),
    )(*ins)


def shape(rows, columns, kind):
    return jax.ShapeDtypeStruct((rows, columns), kind)


def embed(features, head):
    projected = dot(features, head)
    scale = jnp.sqrt(jnp.sum(projected * projected, axis=-1, keepdims=True) + 1e-06)
    return (projected / scale, scale)


def tile_slope(left, right, label_sign, temper, offset):
    scores = temper * dot(left, right.T) + offset
    margin = label_sign * scores
    return (-label_sign * jax.nn.sigmoid(-margin) * temper).astype(BF16)


def project(grad, unit, inverse):
    inner = jnp.sum(unit * grad, axis=-1, keepdims=True)
    return (grad - unit * inner) * inverse


def pairs_kernel(p_grad, p_unit, p_scale, q_grad, q_unit, q_scale, p_pair, q_pair):
    rows = p_grad.shape[0]
    for grad, unit, scale, out in ((q_grad, q_unit, q_scale, q_pair), (p_grad, p_unit, p_scale, p_pair)):
        for at in range(0, rows, 128):
            part = pl.ds(at, 128)
            value = project(grad[part, :], unit[part, :], 1.0 / scale[part, :])
            high = value.astype(BF16)
            out[part, :] = high
            out[pl.ds(rows + at, 128), :] = (value - high.astype(F32)).astype(BF16)


def early_kernel(p, sib_q, p_pair, left, right, sib_q_t, p_twice):
    rows, width = p.shape
    turned = p[...].T
    p_twice[:, :rows] = turned
    p_twice[:, rows:] = turned
    sib_q_t[...] = sib_q[...].T
    for at in range(0, width, 576):
        part = pl.ds(at, 576)
        left[part, :] = dot(p_twice[part, :], p_pair[:, :SPLIT])
        right[part, :] = dot(p_twice[part, :], p_pair[:, SPLIT:])


def other_early_kernel(sib_q_t, sib_pair, left, right, left_out, right_out):
    width, rows = sib_q_t.shape
    for at in range(0, width, 576):
        part = pl.ds(at, 576)
        for before, out, columns in (
            (left, left_out, pl.ds(0, SPLIT)),
            (right, right_out, pl.ds(SPLIT, width - SPLIT)),
        ):
            out[part, :] = (
                before[part, :]
                + dot(sib_q_t[part, :], sib_pair[pl.ds(0, rows), columns])
                + dot(sib_q_t[part, :], sib_pair[pl.ds(rows, rows), columns])
            )


def far_kernel(
    scalars, place, far_img, far_txt, p_head_in, q_head_in, q_low_in, q_unit_in, q_scale_in,
    send_out, qf_t_out, pf_dz_out, pf_t_out,
    send, qf_t, pf_dz, pf_t, pf, qf, p_head, q_head, q_low, q_unit, q_scale, pf_unit, qf_unit, pf_inverse, qf_inverse,
    pf_low, qf_low, slope_a, slope_b, sems, out_sems,
):
    rows = pf.shape[0]
    step = 256
    first = place[0] == 0

    def copy(source, target, at):
        return pltpu.make_async_copy(source, target, sems.at[at])

    @pl.when(first)
    def _():
        copy(far_img, pf, 0).start()

    @pl.when(jnp.logical_not(first))
    def _():
        copy(far_txt, pf, 0).start()

    copies = [copy(p_head_in, p_head, 1)]
    copies[0].start()

    @pl.when(first)
    def _():
        copy(far_txt, qf, 2).start()

    @pl.when(jnp.logical_not(first))
    def _():
        copy(far_img, qf, 2).start()

    for at, (source, target) in enumerate(
        ((q_low_in, q_low), (q_head_in, q_head), (q_unit_in, q_unit), (q_scale_in, q_scale)), 3
    ):
        copies.append(copy(source, target, at))
        copies[-1].start()

    temper, offset = scalars[0], scalars[1]
    stores = []

    def store(source, target, *part):
        if part:
            source, target = source.at[part], target.at[part]
        stores.append(pltpu.make_async_copy(source, target, out_sems.at[len(stores)]))
        stores[-1].start()

    def embed_far(feats, head, unit, inverse, low):
        for at in range(0, rows, step):
            part = pl.ds(at, step)
            projected = dot(feats[part, :], head[...])
            length = jnp.sqrt(jnp.sum(projected * projected, axis=-1, keepdims=True) + 1e-06)
            inverse[part, :] = 1.0 / length
            there = projected * (1.0 / length)
            unit[part, :] = there
            low[part, :] = there.astype(BF16)

    def slopes(low, slope):
        for at in range(0, rows, step):
            part = pl.ds(at, step)
            raw = lax.dot_general(
                pf_low[part, :], low[...], (((1,), (1,)), ((), ())), preferred_element_type=F32
            )
            slope[part, :] = (jax.nn.sigmoid(temper * raw + offset) * temper).astype(BF16)

    copy(far_img, pf, 0).wait()
    copies[0].wait()
    embed_far(pf, p_head, pf_unit, pf_inverse, pf_low)
    pf_t[...] = pf[...].T
    store(pf_t, pf_t_out)
    for at in (1, 2, 3, 4):
        copies[at].wait()
    copy(far_txt, qf, 2).wait()
    qf_t[...] = qf[...].T
    store(qf_t, qf_t_out)
    slopes(q_low, slope_a)
    embed_far(qf, q_head, qf_unit, qf_inverse, qf_low)
    slopes(qf_low, slope_b)
    for at in range(0, rows, step):
        part = pl.ds(at, step)
        grad = dot(slope_a[:, part].T, pf_low[...])
        send[part, :] = project(grad, q_unit[part, :], 1.0 / q_scale[part, :]).astype(BF16)
        store(send, send_out, part)
        again = pl.ds(rows + at, step)
        grad = dot(slope_b[:, part].T, pf_low[...])
        send[again, :] = project(grad, qf_unit[part, :], qf_inverse[part, :]).astype(BF16)
        store(send, send_out, again)
        grad = dot(slope_a[part, :], q_low[...]) + dot(slope_b[part, :], qf_low[...])
        pf_dz[part, :] = project(grad, pf_unit[part, :], pf_inverse[part, :]).astype(BF16)
        store(pf_dz, pf_dz_out, part)
    for copy_out in stores:
        copy_out.wait()


def fetch(pairs, sems):
    copies = [pltpu.make_async_copy(*pair, sems.at[at]) for at, pair in enumerate(pairs)]
    for copy in copies:
        copy.start()
    return lambda at: copies[at].wait()


def near_kernel(*refs):
    ins, outs, held, (in_sems, out_sems) = refs[:4], refs[4:6], refs[6:10], refs[10:]
    pf_t, pf_dz, left, right = held
    width = pf_t.shape[0]
    halves = [pl.ds(0, 576), pl.ds(576, 576)]
    wait = fetch(
        [(ins[1], pf_dz), (ins[0], pf_t)]
        + [(ins[2 + which].at[part, :], held[2 + which].at[part, :]) for part in halves for which in (0, 1)],
        in_sems,
    )
    wait(0)
    wait(1)
    stores = []
    for part in halves:
        for total, out, columns in (
            (left, outs[0], pl.ds(0, SPLIT)),
            (right, outs[1], pl.ds(SPLIT, width - SPLIT)),
        ):
            value = dot(pf_t[part, :], pf_dz[:, columns])
            at = len(stores)
            wait(2 + at)
            total[part, :] = total[part, :] + value
            stores.append(pltpu.make_async_copy(total.at[part, :], out.at[part, :], out_sems.at[at]))
            stores[-1].start()
    for store in stores:
        store.wait()


def cut_kernel(first, along_x, place, *refs):
    ins, (keep_1, send_1, keep_3, send_3), (both_t, got, total, in_sems) = refs[:4], refs[4:8], refs[8:]
    width, count = total.shape
    rows = both_t.shape[1] // 2
    halves = [pl.ds(0, 576), pl.ds(576, 576)]
    wait = fetch(
        [
            (ins[0], both_t.at[:, pl.ds(0, rows)]), (ins[1].at[:, pl.ds(first, count)], got),
            (ins[2], both_t.at[:, pl.ds(rows, rows)]),
        ]
        + [(ins[3].at[part, :], total.at[part, :]) for part in halves],
        in_sems,
    )
    for at in range(3):
        wait(at)
    for at, part in enumerate(halves):
        value = dot(both_t[part, :], got[...])
        wait(3 + at)
        total[part, :] = total[part, :] + value

    def half(target, which):
        if along_x:
            return total[pl.ds(pl.multiple_of(288 * target + 144 * which, 8), 144), :]
        starts = [288 * (2 * which + block) + 72 * target for block in (0, 1)]
        return jnp.concatenate([total[pl.ds(pl.multiple_of(at, 8), 72), :] for at in starts], axis=0)

    me = place[0]
    top, low = pl.ds(0, 144), pl.ds(144, 144)
    keep_1[top, :] = half(me, 0)
    keep_1[low, :] = half(me ^ 3, 0)
    send_1[top, :] = half(me ^ 1, 0).astype(BF16)
    send_1[low, :] = half(me ^ 2, 0).astype(BF16)
    keep_3[top, :] = half(me, 1)
    keep_3[low, :] = half(me ^ 1, 1)
    send_3[top, :] = half(me ^ 3, 1).astype(BF16)
    send_3[low, :] = half(me ^ 2, 1).astype(BF16)


def second_kernel(keep_1, got_1, keep_3, got_3, own, send_3, send_1):
    top, low = pl.ds(0, 144), pl.ds(144, 144)
    first = keep_1[...] + got_1[...].astype(F32)
    own[top, :] = first[:144]
    send_3[...] = first[144:]
    other = keep_3[...] + got_3[...].astype(F32)
    own[low, :] = other[:144]
    send_1[...] = other[144:]


def third_kernel(place, own, got_3, got_1, *rest):
    outs, total = rest[:4], rest[4]
    total[pl.ds(0, 144), :] = own[pl.ds(0, 144), :] + got_3[...]
    total[pl.ds(144, 144), :] = own[pl.ds(144, 144), :] + got_1[...]
    for j in range(4):
        outs[j][...] = total[pl.ds(pl.multiple_of(72 * (place[0] ^ j), 8), 72), :]


def z_pieces_kernel(place, *rest):
    left, right, outs, total, packed = rest[:4], rest[4:8], rest[8:12], rest[12], rest[13]
    total[:, :SPLIT] = left[0][...] + left[1][...] + left[2][...] + left[3][...]
    total[:, SPLIT:] = right[0][...] + right[1][...] + right[2][...] + right[3][...]
    for at in range(4):
        for tile in range(9):
            packed[at, 18 * tile : 18 * tile + 18, :] = total[18 * at : 18 * at + 18, 128 * tile : 128 * tile + 128]
    for j in range(4):
        outs[j][...] = packed[place[0] ^ j, 0:162, :]


def sum_kernel(a, b, c, d, total):
    total[...] = a[...] + b[...] + c[...] + d[...]


def last_kernel(place, a, b, mine, squares, total):
    total[...] = a[...] + b[...]

    def take(first):
        for tile in range(9):
            mine[9 * tile : 9 * tile + 9, :] = total[18 * tile + first : 18 * tile + first + 9, :]

    @pl.when(place[0] == 0)
    def _():
        take(0)

    @pl.when(place[0] != 0)
    def _():
        take(9)

    value = total[...]
    squares[...] = jnp.broadcast_to(jnp.sum(value * value, axis=0, keepdims=True), squares.shape)


def lanes_kernel(got, squares):
    lanes = jnp.sum(got[...], axis=0, keepdims=True) * 0.125
    squares[...] = jnp.broadcast_to(lanes, squares.shape)


def scale_kernel(rows, got, out):
    total = jnp.sum(jnp.sum(got[...], axis=0, keepdims=True), axis=1, keepdims=True) * 0.125
    entries = 2 * out.shape[1] * out.shape[1]
    spread = jnp.sqrt(total / entries + 1e-06)
    for tile in range(9):
        out[:, 128 * tile : 128 * tile + 128] = rows[9 * tile : 9 * tile + 9, :] / spread


def swap_all(value, bits):
    masks = [sum(1 << bit for at, bit in enumerate(bits) if k >> at & 1) for k in range(2 ** len(bits))]
    groups = [[d | mask for mask in masks] for d in range(lax.axis_size("dp")) if not d & masks[-1]]
    return lax.all_to_all(value, "dp", 0, 0, axis_index_groups=groups, tiled=True)


def per_device(img_feats, txt_feats, img_head, txt_head, log_temp, logit_bias, caption_row):
    me = lax.axis_index("dp")
    core, y, x, z = me & 1, (me >> 1) & 3, (me >> 3) & 3, me >> 5
    first = core == 0
    rows, width = img_feats.shape

    far_img = permute(img_feats, lambda d: d ^ (192 if d & 1 else 64))
    far_txt = permute(txt_feats, lambda d: d ^ (64 if d & 1 else 192))
    p = jnp.where(first, img_feats, txt_feats)
    q = jnp.where(first, txt_feats, img_feats)
    p_head = jnp.where(first, img_head, txt_head)
    q_head = jnp.where(first, txt_head, img_head)
    sib_q = sibling(q)

    temper = jnp.exp(log_temp)
    index = jnp.arange(rows, dtype=jnp.int32)
    match = jnp.where(first, caption_row, index)[:, None] == jnp.where(first, index, caption_row)[None, :]
    label_sign = jnp.where(match, 1.0, -1.0).astype(F32)

    p_unit, p_scale = embed(p, p_head)
    q_unit, q_scale = embed(q, q_head)
    p_low = p_unit.astype(BF16)
    q_low = q_unit.astype(BF16)
    slope = tile_slope(p_low, q_low, label_sign, temper, logit_bias)
    p_grad = dot(slope, q_low)
    q_grad = dot(slope.T, p_low)
    scalars = jnp.stack([temper, logit_bias])
    p_pair, q_pair = call(
        pairs_kernel,
        (p_grad, p_unit, p_scale, q_grad, q_unit, q_scale),
        (shape(2 * rows, width, BF16), shape(2 * rows, width, BF16)),
        1,
        limit=20,
    )
    sib_pair = sibling(q_pair)
    left, right, sib_q_t = call(
        early_kernel,
        (p, sib_q, p_pair),
        (shape(width, SPLIT, F32), shape(width, width - SPLIT, F32), shape(width, rows, BF16)),
        200 * rows * width * width,
        [pltpu.VMEM((width, 2 * rows), BF16)],
        limit=20,
    )
    left, right = call(
        other_early_kernel,
        (sib_q_t, sib_pair, left, right),
        (shape(width, SPLIT, F32), shape(width, width - SPLIT, F32)),
        1,
        (),
        {2: 0, 3: 1},
        limit=24,
    )
    far_img, far_txt, left, right, sib_q_t = lax.optimization_barrier(
        (far_img, far_txt, left, right, sib_q_t)
    )

    wide, low, thin = (pltpu.VMEM(dims, kind) for dims, kind in (
        ((rows, width), F32), ((rows, width), BF16), ((rows, 1), F32),
    ))
    head, tile = pltpu.VMEM((width, width), BF16), pltpu.VMEM((rows, rows), BF16)
    turned = pltpu.VMEM((width, rows), BF16)
    send, qf_t, pf_dz, pf_t = call(
        far_kernel,
        (scalars, jnp.stack([core, 0]), far_img, far_txt, p_head, q_head, q_low, q_unit, q_scale),
        (shape(2 * rows, width, BF16), shape(width, rows, BF16), shape(rows, width, BF16), shape(width, rows, BF16)),
        4 * rows * width * width + 12 * rows * rows * width,
        [
            pltpu.VMEM((2 * rows, width), BF16), turned, low, turned,
            low, low, head, head, low, wide, thin, wide, wide, thin, thin,
            low, low, tile, tile, pltpu.SemaphoreType.DMA((7,)), pltpu.SemaphoreType.DMA((8,)),
        ],
        limit=LIMIT,
        far_ins=range(9),
        far_outs=range(4),
    )
    got, sib_qf_t = sibling(send), sibling(qf_t)
    accumulators = [pltpu.VMEM((width, SPLIT), F32), pltpu.VMEM((width, width - SPLIT), F32)]
    left, right = call(
        near_kernel,
        (pf_t, pf_dz, left, right),
        (shape(width, SPLIT, F32), shape(width, width - SPLIT, F32)),
        2 * rows * width * width,
        [turned, low, *accumulators, pltpu.SemaphoreType.DMA((6,)), pltpu.SemaphoreType.DMA((4,))],
        limit=LIMIT,
        far_ins=range(4),
        far_outs=range(2),
    )

    def cut(first, along_x, place, head_grad):
        count = head_grad.shape[1]
        return call(
            functools.partial(cut_kernel, first, along_x),
            (jnp.stack([place, 0]), sib_q_t, got, sib_qf_t, head_grad),
            (shape(288, count, F32), shape(288, count, BF16)) * 2,
            4 * rows * width * count,
            [
                pltpu.VMEM((width, 2 * rows), BF16), pltpu.VMEM((2 * rows, count), BF16),
                pltpu.VMEM((width, count), F32), pltpu.SemaphoreType.DMA((5,)),
            ],
            limit=24,
            far_ins=range(1, 5),
        )

    def first_step(parts, bit):
        keep_1, send_1, keep_3, send_3 = parts
        return keep_1, permute(send_1, lambda d: d ^ (1 << bit)), keep_3, permute(send_3, lambda d: d ^ (3 << bit))

    def second_step(parts):
        count = parts[0].shape[1]
        return call(
            second_kernel,
            parts,
            (shape(288, count, F32), shape(144, count, F32), shape(144, count, F32)),
            288 * count,
            limit=8,
        )

    def last_step(parts, bit, other, other_bit):
        own, send_3, send_1 = parts
        count = own.shape[1]
        got_3 = permute(send_3, lambda d: d ^ (3 << bit))
        got_1 = permute(send_1, lambda d: d ^ (1 << bit))
        outs = call(
            third_kernel,
            (jnp.stack([other, 0]), own, got_3, got_1),
            [shape(72, count, F32)] * 4,
            288 * count,
            [pltpu.VMEM((288, count), F32)],
            limit=8,
        )
        return outs[0], [permute(outs[j], lambda d, j=j: d ^ (j << other_bit)) for j in (1, 2, 3)]

    own, *left = second_step(first_step(cut(0, True, x, left), 3))
    keep, *right = first_step(cut(SPLIT, False, y, right), 1)
    own, keep = lax.optimization_barrier((own, keep))
    left, right = (own, *left), second_step((keep, *right))
    own, left = last_step(left, 3, y, 1)
    own, keep = lax.optimization_barrier((own, right[0]))
    left = [own, *left]
    own, right = last_step((keep, *right[1:]), 1, x, 3)
    right = [own, *right]
    parts = call(
        z_pieces_kernel,
        (jnp.stack([z >> 1, 0]), *left, *right),
        [shape(162, 128, F32)] * 4,
        6 * 72 * width,
        [pltpu.VMEM((72, width), F32), pltpu.VMEM((4, 168, 128), F32)],
        limit=8,
    )
    parts = [parts[0]] + [permute(parts[j], lambda d, j=j: d ^ (j << 6)) for j in (1, 2, 3)]
    [part] = call(sum_kernel, parts, [shape(162, 128, F32)], 3 * 18 * width, limit=8)

    other = permute(part, lambda d: d ^ 32)
    total, squares = call(
        last_kernel,
        (jnp.stack([z & 1, 0]), part, other),
        (shape(81, 128, F32), shape(128, 128, F32)),
        10 * 18 * width,
        [pltpu.VMEM((162, 128), F32)],
        limit=8,
    )

    def owner(d):
        z, x, y, s = d >> 5, d >> 3 & 3, d >> 1 & 3, d & 1
        return (4 * s + x) << 5 | y << 3 | (z >> 1) << 1 | z & 1

    mine = permute(total, owner)
    [squares] = call(lanes_kernel, (swap_all(squares, (1, 2, 3, 4)),), [shape(64, 128, F32)], 10000, limit=8)
    squares, mine = lax.optimization_barrier((squares, mine))
    got = swap_all(squares, (0, 6, 7))
    [out] = call(scale_kernel, (mine, got), [shape(9, width, F32)], 10 * 9 * width, limit=8)
    return out


def solution(mesh):
    return jax.shard_map(
        per_device,
        mesh=mesh,
        in_specs=(P("dp", None), P("dp", None), P(), P(), P(), P(), P("dp")),
        out_specs=P("dp", None),
        check_vma=False,
    )
```
